256 devices in a mesh: grp: 2 (over core), brick: 128 (over z, y, x).
Axes of the slice: x: 4, y: 4, z: 8, core: 2. Of those that a mesh axis runs over, the one named last changes fastest.
Arguments:
- density: float32 [512, 64, 256], P('brick', None, 'grp'), may hold values from 0.5 to 2
- energy_field: float32 [512, 64, 256], P('brick', None, 'grp'), may hold values from -6 to 6
- lepton_field: float32 [512, 64, 256], P('brick', None, 'grp'), may hold values from 0.1 to 0.6
- velocity: float32 [3, 512, 64, 256], P(None, 'brick', None, 'grp'), may hold values from -4 to 4
- abundance: float32 [2, 128, 1024, 128], P('grp', 'brick'), may hold values from -1.2 to 1.2
- tracer_mass: float32 [2, 128, 1024], P('grp', 'brick'), may hold values from 0.2 to 1
- tracer_cell: int32 [2, 128, 1024], P('grp', 'brick'), may hold values from 0 to 32767
- tracer_count: int32 [2, 128], P('grp', 'brick'), may hold values from 1 to 1024, as said below
- weak_rates: float32 [128, 128], replicated, may hold values from -0.5 to 0.5
- capture_rates: float32 [128, 128], replicated, may hold values from -0.5 to 0.5
- binding: float32 [128], replicated, may hold values from -6 to 6
- charge_ratio: float32 [128], replicated, may hold values from 0 to 1
Outputs:
- density_out: float32 [512, 64, 256], P('brick', None, 'grp')
- energy_out: float32 [512, 64, 256], P('brick', None, 'grp')
- lepton_out: float32 [512, 64, 256], P('brick', None, 'grp')
- abundance_out: float32 [2, 128, 1024, 128], P('grp', 'brick')
The draws below stay inside these ranges and needn't reach their ends.
Inputs may be any that keep to these rules, and one draw needn't show every extreme that they name: `tracer_count`: for each index of grp the counts sum to 65536; exactly one brick of each half holds 1024, the most; every other brick holds at most 512, and some brick of each half holds exactly 512.
All inputs are finite; a program needn't handle non-finite values.
Results may differ from the reference program's by a relative error of at most 0.00029.
Values sent between devices are 32-bit elements; how exact they have to be, the bound alone decides.
No kernel may reach another device: no remote copies, remote signals or barrier semaphores. Data moves between devices by JAX's collectives and lax.ppermute only.
A program may use at most 64 MiB of HBM per device.

```python
import math
import jax
import jax.numpy as jnp
from jax import lax

S = 128
CX = 4
CY = 64
CZ = 128
TR_DEV = 512
NEWTON = 2
SWEEPS = 8
TCAP = 1024
NX = 512
NZ = 256
N_GRP = 2
N_BRICK = 128


def draw_tracer_count(key, part):
    first_key, second_key, third_key = jax.random.split(key, 3)
    busiest = jax.random.randint(first_key, (N_GRP,), 0, N_BRICK)
    offset = jax.random.randint(third_key, (N_GRP,), 1, N_BRICK)
    filled = (busiest + offset) % N_BRICK
    weights = jax.random.randint(second_key, (N_GRP, N_BRICK), 1, 4)
    brick_ids = jnp.arange(N_BRICK, dtype=jnp.int32)[None, :]
    is_busiest = brick_ids == busiest[:, None]
    is_filled = brick_ids == filled[:, None]
    others = jnp.logical_not(jnp.logical_or(is_busiest, is_filled)).astype(jnp.int32)
    weights = weights * others
    shares = weights * TR_DEV // jnp.sum(weights, axis=1, keepdims=True)
    leftover = TR_DEV - jnp.sum(shares, axis=1, keepdims=True)
    rank_order = jnp.cumsum(others, axis=1) - 1
    shares = shares + others * (rank_order < leftover).astype(jnp.int32)
    return jnp.where(is_busiest, TCAP, TR_DEV - shares).astype(jnp.int32)


def with_ends(array, stream_key, smallest, top_value):
    shape = array.shape
    place = [jax.random.randint(jax.random.fold_in(stream_key, axis), (), 0, shape[axis]) for axis in range(len(shape))]
    array = array.at[tuple(place)].set(smallest)
    longest = shape.index(max(shape))
    place[longest] = (place[longest] + 1) % shape[longest]
    return array.at[tuple(place)].set(top_value)


def block_scale(own_key, shape, pieces, smallest, high):
    loudness = 1.0
    for axis_at, shards_of in pieces:
        heights = jax.random.uniform(jax.random.fold_in(jax.random.fold_in(own_key, 6), axis_at), (shards_of,), jnp.float32, smallest / len(pieces), high / len(pieces))
        loudness = loudness * jnp.repeat(jnp.exp(heights), shape[axis_at] // shards_of).reshape((-1,) + (1,) * (len(shape) - 1 - axis_at))
    return loudness


def centred(stream_key, extent, deviation, bound, cuts=(), kind=jnp.bfloat16):
    values = deviation * jax.random.normal(stream_key, extent, jnp.float32)
    if cuts:
        values = values * block_scale(stream_key, extent, cuts, -0.22, 0.18)
    return jnp.clip(values, -bound, bound).astype(kind)


def setup_inputs(seed: int = 0) -> dict:
    keys = jax.random.split(jax.random.key(seed), 13)
    return {
        "density": jnp.clip(jnp.exp(math.log(2.0) - 1.3862944 * jax.random.uniform(keys[0], (NX, CY, NZ), jnp.float32) ** block_scale(keys[0], (NX, CY, NZ), ((0, 128), (2, 2)), -0.2, 0.2)), 0.5, 2.0),
        "energy_field": centred(keys[1], (NX, CY, NZ), 1.0, 6.0, ((0, 128), (2, 2)), jnp.float32),
        "lepton_field": jnp.clip(0.1 + 0.5 * jax.random.uniform(keys[2], (NX, CY, NZ), jnp.float32) ** block_scale(keys[2], (NX, CY, NZ), ((0, 128), (2, 2)), -0.2, 0.2), 0.1, 0.6),
        "velocity": centred(keys[3], (3, NX, CY, NZ), 1.0, 4.0, ((1, 128), (3, 2)), jnp.float32),
        "abundance": centred(keys[4], (N_GRP, N_BRICK, TCAP, S), 0.3, 1.2, ((0, 2), (1, 128)), jnp.float32),
        "tracer_mass": jnp.clip(jnp.exp(math.log(1.0) - 1.609438 * jax.random.uniform(keys[5], (N_GRP, N_BRICK, TCAP), jnp.float32) ** block_scale(keys[5], (N_GRP, N_BRICK, TCAP), ((0, 2), (1, 128)), -0.2, 0.2)), 0.2, 1.0),
        "tracer_cell": with_ends(jax.random.randint(keys[6], (N_GRP, N_BRICK, TCAP), 0, CX * CY * CZ), jax.random.fold_in(keys[6], 1), 0, (CX * CY * CZ) - 1).astype(jnp.int32),
        "tracer_count": draw_tracer_count(jax.random.fold_in(keys[12], 71), 0),
        "weak_rates": centred(keys[8], (S, S), S ** -0.5, 0.5, (), jnp.float32),
        "capture_rates": centred(keys[9], (S, S), S ** -0.5, 0.5, (), jnp.float32),
        "binding": centred(keys[10], (S,), 1.0, 6.0, (), jnp.float32),
        "charge_ratio": jnp.clip(jax.random.uniform(keys[11], (S,), jnp.float32, 0.0, 1.0), 0.0, 1.0),
    }


courant = 0.8
highest = lax.Precision.HIGHEST


def rolled_difference(values, axis_number):
    return (8.0 * (jnp.roll(values, -1, axis_number) - jnp.roll(values, 1, axis_number)) - (jnp.roll(values, -2, axis_number) - jnp.roll(values, 2, axis_number))) / 12.0


def full_tendency(fields, speeds):
    along_x = rolled_difference(speeds[0][None] * fields, 1)
    along_y = rolled_difference(speeds[1][None] * fields, 2)
    along_z = rolled_difference(speeds[2][None] * fields, 3)
    return -((along_x + along_y) + along_z)


def thermo_rates(density, energy_field, lepton_field, cells):
    thermo = jnp.stack([density, energy_field, lepton_field]).reshape(3, -1)
    picked = jnp.take(thermo, cells, axis=1)
    weak_scale = 0.62 + 0.04 * picked[0] + 0.05 * (picked[2] / picked[0])
    capture_scale = 0.3 * jax.nn.sigmoid(picked[1] / picked[0])
    return weak_scale, capture_scale


def network_step(initial, rate_weak, rate_capture, matrices):
    species = initial.shape[1]
    iterate = initial
    for newton_turn in range(NEWTON):
        products = jnp.dot(iterate, matrices, precision=highest, preferred_element_type=jnp.float32)
        alpha_part = iterate[:, 0:1]
        capture = products[:, species:]
        target = -(iterate - initial - (rate_weak * products[:, :species] + rate_capture * alpha_part * capture))
        update = target
        for sweep_turn in range(SWEEPS):
            product = jnp.dot(update, matrices, precision=highest, preferred_element_type=jnp.float32)
            update = target + (rate_weak * product[:, :species] + rate_capture * alpha_part * product[:, species:] + rate_capture * update[:, 0:1] * capture)
        iterate = iterate + update
    return iterate


def reference(density, energy_field, lepton_field, velocity, abundance, tracer_mass, tracer_cell, tracer_count, weak_rates, capture_rates, binding, charge_ratio):
    state = jnp.stack([density, energy_field, lepton_field])
    midpoint = state + (0.5 * courant) * full_tendency(state, velocity)
    advanced = state + courant * full_tendency(midpoint, velocity)
    groups_z, groups_x, capacity = tracer_cell.shape
    plane = CY * CZ
    cell_x = tracer_cell // plane
    cell_y = (tracer_cell // CZ) % CY
    cell_z = tracer_cell % CZ
    grp_ids = jnp.arange(groups_z, dtype=jnp.int32)[:, None, None]
    brick_ids = jnp.arange(groups_x, dtype=jnp.int32)[None, :, None]
    global_cell = ((brick_ids * CX + cell_x) * CY + cell_y) * NZ + grp_ids * CZ + cell_z
    flat_ids = global_cell.reshape(-1).astype(jnp.int32)
    weak_scale, capture_scale = thermo_rates(density, energy_field, lepton_field, flat_ids)
    occupied = (jnp.arange(capacity, dtype=jnp.int32)[None, None, :] < tracer_count[:, :, None]).reshape(-1, capacity)
    rows = abundance.reshape(-1, capacity, S)
    rates = jnp.stack([weak_scale, capture_scale], axis=1).reshape(-1, capacity, 2)
    matrices = jnp.concatenate([weak_rates, capture_rates], axis=1)

    def solve_block(block_item):
        return network_step(block_item[0], block_item[1][:, 0:1], block_item[1][:, 1:2], matrices)

    solved = lax.map(solve_block, (rows, rates))
    finished = jnp.where(occupied[..., None], solved, 0.0)
    initial = jnp.where(occupied[..., None], rows, 0.0)
    change = (finished - initial).reshape(-1, S)
    table = jnp.stack([binding, charge_ratio], axis=1)
    gains = jnp.dot(change, table, precision=highest, preferred_element_type=jnp.float32) * tracer_mass.reshape(-1)[:, None]
    deposit = jnp.zeros((NX * CY * NZ, 2), jnp.float32).at[flat_ids].add(gains)
    energy_out = advanced[1] + deposit[:, 0].reshape(NX, CY, NZ)
    lepton_out = advanced[2] + deposit[:, 1].reshape(NX, CY, NZ)
    return advanced[0], energy_out, lepton_out, finished.reshape(abundance.shape)
```

```python
import functools

import jax
import jax.numpy as jnp
from jax import lax
from jax.experimental import pallas as pl
from jax.experimental.pallas import tpu as pltpu
from jax.sharding import PartitionSpec as P

SWEEPS = 8
CHUNK = 512
BLOCK = 128
COURANT = 0.8
F32 = jnp.float32
BF16 = jnp.bfloat16


def split(values):
    high = values.astype(BF16)
    return high, (values - high.astype(F32)).astype(BF16)


def matmul(a, b):
    return lax.dot_general(a, b, (((1,), (0,)), ((), ())), preferred_element_type=F32)


def lanes(rows=64):
    return lax.broadcasted_iota(jnp.int32, (rows, 128), 1)


def pack_z(packed, tile, number, lane):
    moved = pltpu.roll(tile, 4 * number + 2, 1)
    inside = jnp.logical_and(lane >= 4 * number, lane < 4 * number + 4)
    return jnp.where(inside, moved, packed)


def along_z(tile, packed, number, lane):
    other = pltpu.roll(packed, (126 - 4 * number) % 128, 1)
    next1 = pltpu.roll(jnp.where(lane == 0, other, tile), 127, 1)
    next2 = pltpu.roll(jnp.where(lane < 2, other, tile), 126, 1)
    last1 = pltpu.roll(jnp.where(lane == 127, other, tile), 1, 1)
    last2 = pltpu.roll(jnp.where(lane >= 126, other, tile), 2, 1)
    return 8.0 * (next1 - last1) - (next2 - last2)


def along_y(tile):
    size = tile.shape[0]
    return 8.0 * (pltpu.roll(tile, size - 1, 0) - pltpu.roll(tile, 1, 0)) - (
        pltpu.roll(tile, size - 2, 0) - pltpu.roll(tile, 2, 0)
    )


def edges_kernel(density, energy, lepton, velocity, low, high, packed):
    lane = lanes()
    pack = jnp.zeros((64, 128), F32)
    for f, field in enumerate((density, energy, lepton)):
        for i in range(2):
            low[f, i] = velocity[0, i] * field[i]
            high[f, i] = velocity[0, i + 2] * field[i + 2]
        for i in range(4):
            pack = pack_z(pack, velocity[2, i] * field[i], 4 * f + i, lane)
    packed[...] = pack


def sum_of_differences(get, velocity, from_low, from_high, from_other, f, lane):
    planes = [get(i) for i in range(4)]
    speed_x = [from_low[f, 0], from_low[f, 1]]
    speed_x += [velocity[0, i] * planes[i] for i in range(4)]
    speed_x += [from_high[f, 0], from_high[f, 1]]
    packed = from_other[...]
    for i in range(4):
        along_x = 8.0 * (speed_x[i + 3] - speed_x[i + 1]) - (speed_x[i + 4] - speed_x[i])
        total = along_x + along_y(velocity[1, i] * planes[i])
        total = total + along_z(velocity[2, i] * planes[i], packed, 4 * f + i, lane)
        yield i, total


def midpoint_kernel(
    density, energy, lepton, velocity, from_low, from_high, from_other, mid, low, high, packed
):
    lane = lanes()
    pack = jnp.zeros((64, 128), F32)
    for f, field in enumerate((density, energy, lepton)):
        for i, total in sum_of_differences(
            lambda i: field[i], velocity, from_low, from_high, from_other, f, lane
        ):
            value = field[i] - (0.5 * COURANT / 12.0) * total
            mid[f, i] = value
            if i < 2:
                low[f, i] = velocity[0, i] * value
            else:
                high[f, i - 2] = velocity[0, i] * value
            pack = pack_z(pack, velocity[2, i] * value, 4 * f + i, lane)
    packed[...] = pack


def final_kernel(
    density, energy, lepton, velocity, mid, from_low, from_high, from_other, deposit,
    density_out, energy_out, lepton_out,
):
    lane = lanes()
    outs = (density_out, energy_out, lepton_out)
    for f, field in enumerate((density, energy, lepton)):
        for i, total in sum_of_differences(
            lambda i: mid[f, i], velocity, from_low, from_high, from_other, f, lane
        ):
            value = field[i] - (COURANT / 12.0) * total
            if f > 0:
                value = value + deposit[f - 1, pl.ds(64 * i, 64), :]
            outs[f][i] = value


def column(row):
    return jnp.transpose(jnp.broadcast_to(row, (128, 128)))


def load_matrices(weak, capture, both, rest):
    matrix = jnp.concatenate([weak[...], capture[...]], axis=1)
    high, low = split(matrix)
    both[...] = jnp.concatenate([high, high], axis=0)
    rest[...] = low


def newton(base, start, get_target, rows_of, both, rest, w_ref, c_ref, x_ref, t_ref, k_ref, a_ref, finish):
    blocks = CHUNK // BLOCK

    def products(b):
        x = x_ref[pl.ds(b * BLOCK, BLOCK), :]
        return matmul(x, both[...]) + matmul(x[:, :128], rest[...])

    def put(b, values):
        high, low = split(values)
        x_ref[pl.ds(b * BLOCK, BLOCK), :] = jnp.concatenate([high, low], axis=1)

    for b in range(blocks):
        put(b, rows_of(b))
    for b in range(blocks):
        at = pl.ds(b * BLOCK, BLOCK)
        here = pl.ds(base + b * BLOCK, BLOCK)
        product = products(b)
        rows = rows_of(b)
        rate_weak, rate_capture = w_ref[here, :], c_ref[here, :]
        alpha = rate_capture * rows[:, 0:1]
        target = rate_weak * product[:, :128] + alpha * product[:, 128:]
        target = get_target(b, rows, target)
        a_ref[at, :] = alpha
        k_ref[at, :] = rate_capture * product[:, 128:]
        t_ref[at, :] = target
        put(b, target)
        start(b, target)
    for sweep in range(SWEEPS):
        for b in range(blocks):
            at = pl.ds(b * BLOCK, BLOCK)
            here = pl.ds(base + b * BLOCK, BLOCK)
            product = products(b)
            before = finish.last[b]
            update = t_ref[at, :] + (
                w_ref[here, :] * product[:, :128]
                + a_ref[at, :] * product[:, 128:]
                + before * k_ref[at, :]
            )
            if sweep < SWEEPS - 1:
                put(b, update)
                start(b, update)
            else:
                finish(b, rows_of(b) + update)


class Finish:
    def __init__(self, write):
        self.last = {}
        self.write = write

    def keep(self, b, values):
        self.last[b] = values[:, 0:1]

    def __call__(self, b, values):
        self.write(b, values)


def first_kernel(
    count, density, energy, lepton, cells, rows, weak, capture,
    iterate, w_out, c_out,
    table, both, rest, x_ref, t_ref, k_ref, a_ref,
):
    load_matrices(weak, capture, both, rest)
    rho = density[...].reshape(256, 128)
    eps = energy[...].reshape(256, 128)
    lam = lepton[...].reshape(256, 128)
    inverse = 1.0 / rho
    weak_high, weak_low = split(0.62 + 0.04 * rho + 0.05 * (lam * inverse))
    capture_high, capture_low = split(0.3 * jax.nn.sigmoid(eps * inverse))
    table[...] = jnp.concatenate([weak_high, weak_low, capture_high, capture_low], axis=1)
    lane = lanes(BLOCK)
    ones = jnp.ones((256, 128), BF16)

    def chunk(k, carry):
        base = k * CHUNK
        for b in range(CHUNK // BLOCK):
            at = pl.ds(pl.multiple_of(base + b * BLOCK, BLOCK), BLOCK)
            cell = column(cells[pl.ds(k * (CHUNK // BLOCK) + b, 1), :])
            row_id = lax.shift_right_logical(cell, 7)
            hot = jnp.concatenate([row_id == lane, row_id == lane + 128], axis=1)
            picked = matmul(jnp.where(hot, 1.0, 0.0).astype(BF16), table[...])
            here = jnp.bitwise_and(cell, 127) == lane
            here = jnp.concatenate([here, here, here, here], axis=1)
            picked = jnp.where(here, picked, 0.0).astype(BF16)
            w_out[at, :] = matmul(picked[:, :256], ones)
            c_out[at, :] = matmul(picked[:, 256:], ones)

        def rows_of(b):
            return rows[pl.ds(pl.multiple_of(base + b * BLOCK, BLOCK), BLOCK), :]

        def write(b, values):
            iterate[pl.ds(pl.multiple_of(base + b * BLOCK, BLOCK), BLOCK), :] = values

        finish = Finish(write)
        newton(
            base, finish.keep, lambda b, rows, target: target, rows_of, both, rest,
            w_out, c_out, x_ref, t_ref, k_ref, a_ref, finish,
        )
        return carry

    lax.fori_loop(0, (count[0, 0] + CHUNK - 1) // CHUNK, chunk, 0)


def second_kernel(
    count, cells, rows, weak, capture, iterate, w_in, c_in, mass, binding, charge,
    rows_out, deposit,
    both, rest, x_ref, t_ref, k_ref, a_ref, gain_both, gain_rest,
):
    load_matrices(weak, capture, both, rest)
    gains = jnp.concatenate([column(binding[...]), column(charge[...])], axis=1)
    high, low = split(gains)
    gain_both[...] = jnp.concatenate([high, high], axis=0)
    gain_rest[...] = low
    rows_out[...] = jnp.zeros(rows_out.shape, F32)
    deposit[...] = jnp.zeros(deposit.shape, F32)
    lane = lanes(BLOCK)
    sublane = lax.broadcasted_iota(jnp.int32, (256, 128), 0)

    def chunk(k, carry):
        base = k * CHUNK

        def place(b):
            return pl.ds(pl.multiple_of(base + b * BLOCK, BLOCK), BLOCK)

        def rows_of(b):
            return iterate[place(b), :]

        def get_target(b, current, target):
            return target - (current - rows[place(b), :])

        def write(b, values):
            slot = base + b * BLOCK + lax.broadcasted_iota(jnp.int32, (BLOCK, 128), 0)
            occupied = slot < count[0, 0]
            rows_out[place(b), :] = jnp.where(occupied, values, 0.0)
            change = jnp.where(occupied, values - rows[place(b), :], 0.0)
            high, low = split(change)
            x_ref[pl.ds(b * BLOCK, BLOCK), :] = jnp.concatenate([high, low], axis=1)

        finish = Finish(write)
        newton(
            base, finish.keep, get_target, rows_of, both, rest,
            w_in, c_in, x_ref, t_ref, k_ref, a_ref, finish,
        )
        hots, values = [], []
        for b in range(CHUNK // BLOCK):
            number = pl.ds(k * (CHUNK // BLOCK) + b, 1)
            cell = cells[number, :]
            hot = lax.shift_right_logical(cell, 7) == sublane
            hots.append(jnp.where(hot, 1.0, 0.0).astype(BF16))
            x = x_ref[pl.ds(b * BLOCK, BLOCK), :]
            gain = matmul(x, gain_both[...]) + matmul(x[:, :128], gain_rest[...])
            weight = jnp.where(
                jnp.bitwise_and(column(cell), 127) == lane, column(mass[number, :]), 0.0
            )
            gain = gain * jnp.concatenate([weight, weight], axis=1)
            high, low = split(gain)
            values.append(jnp.concatenate([high, low], axis=1))
        sums = matmul(jnp.concatenate(hots, axis=1), jnp.concatenate(values, axis=0))
        deposit[0] += sums[:, :128] + sums[:, 256:384]
        deposit[1] += sums[:, 128:256] + sums[:, 384:]
        return carry

    lax.fori_loop(0, (count[0, 0] + CHUNK - 1) // CHUNK, chunk, 0)


VMEM = pl.BlockSpec(memory_space=pltpu.VMEM)
SMEM = pl.BlockSpec(memory_space=pltpu.SMEM)


def call(kernel, name, outs, args, scratch=(), flops=0, smem=0):
    moved = sum(a.size * 4 for a in args) + sum(4 * functools.reduce(lambda p, s: p * s, o) for o in outs)
    return pl.pallas_call(
        kernel,
        name=name,
        out_shape=[jax.ShapeDtypeStruct(o, F32) for o in outs],
        in_specs=[SMEM] * smem + [VMEM] * (len(args) - smem),
        out_specs=[VMEM] * len(outs),
        scratch_shapes=list(scratch),
        compiler_params=pltpu.CompilerParams(vmem_limit_bytes=24 * 2**20),
        cost_estimate=pl.CostEstimate(flops=flops, bytes_accessed=moved, transcendentals=0),
    )(*args)


def exchange(low, high, packed):
    count = lax.axis_size("brick")
    forward = [(i, (i + 1) % count) for i in range(count)]
    backward = [(b, a) for a, b in forward]
    halves = lax.axis_size("grp")
    swap = [(i, (i + 1) % halves) for i in range(halves)]
    from_low = lax.ppermute(high, "brick", forward)
    from_high = lax.ppermute(low, "brick", backward)
    from_other = lax.ppermute(packed, "grp", swap)
    return from_low, from_high, from_other


def on_device(
    density,
    energy_field,
    lepton_field,
    velocity,
    abundance,
    tracer_mass,
    tracer_cell,
    tracer_count,
    weak_rates,
    capture_rates,
    binding,
    charge_ratio,
):
    fields = (density, energy_field, lepton_field)
    edge, tile, all_rows = (3, 2, 64, 128), (64, 128), (1024, 128)
    edges = call(edges_kernel, "edges", [edge, edge, tile], (*fields, velocity))
    arrived = exchange(*edges)

    rows = abundance.reshape(1024, 128)
    cells = tracer_cell.reshape(8, 128)
    mass = tracer_mass.reshape(8, 128)
    matrices = [pltpu.VMEM((256, 256), BF16), pltpu.VMEM((128, 256), BF16)]
    state = [pltpu.VMEM((CHUNK, 256), BF16)] + [pltpu.VMEM((CHUNK, 128), F32)] * 3
    flops = 6 * 2 * 1024 * 128 * 256 * 9
    iterate, rate_weak, rate_capture = call(
        first_kernel, "newton_first", [all_rows] * 3,
        (tracer_count, *fields, cells, rows, weak_rates, capture_rates),
        [pltpu.VMEM((256, 512), BF16), *matrices, *state], flops, 1,
    )
    mid, *edges = call(
        midpoint_kernel, "midpoint", [(3, 4, 64, 128), edge, edge, tile], (*fields, velocity, *arrived)
    )
    arrived = exchange(*edges)
    finished, deposit = call(
        second_kernel, "newton_second", [all_rows, (2, 256, 128)],
        (
            tracer_count, cells, rows, weak_rates, capture_rates, iterate, rate_weak, rate_capture,
            mass, binding.reshape(1, 128), charge_ratio.reshape(1, 128),
        ),
        [*matrices, *state, *matrices], flops, 1,
    )
    outs = call(
        final_kernel, "advance", [(4, 64, 128)] * 3, (*fields, velocity, mid, *arrived, deposit)
    )
    return (*outs, finished[None, None])


def solution(mesh):
    return jax.shard_map(
        on_device,
        mesh=mesh,
        in_specs=(
            P("brick", None, "grp"),
            P("brick", None, "grp"),
            P("brick", None, "grp"),
            P(None, "brick", None, "grp"),
            P("grp", "brick", None, None),
            P("grp", "brick", None),
            P("grp", "brick", None),
            P("grp", "brick"),
            P(),
            P(),
            P(),
            P(),
        ),
        out_specs=(
            P("brick", None, "grp"),
            P("brick", None, "grp"),
            P("brick", None, "grp"),
            P("grp", "brick", None, None),
        ),
        check_vma=False,
    )
```

```python
import math

import jax
import jax.numpy as jnp
from jax import lax
from jax.experimental import pallas as pl
from jax.experimental.pallas import tpu as pltpu
from jax.sharding import PartitionSpec as P

SWEEPS = 8
CHUNK = 512
BLOCK = 128
COURANT = 0.8
HALF = 0.5 * COURANT / 12.0
FULL = COURANT / 12.0
F32 = jnp.float32
BF16 = jnp.bfloat16


def split(values):
    high = values.astype(BF16)
    return high, (values - high.astype(F32)).astype(BF16)


def matmul(a, b):
    return lax.dot_general(a, b, (((1,), (0,)), ((), ())), preferred_element_type=F32)


def lanes(rows=64):
    return lax.broadcasted_iota(jnp.int32, (rows, 128), 1)


def pack_z(packed, tile, first, lane):
    moved = pltpu.roll(tile, first + 2, 1)
    inside = jnp.logical_and(lane >= first, lane < first + 4)
    return jnp.where(inside, moved, packed)


def unpack_z(packed, first, lane):
    moved = pltpu.roll(packed, (126 - first) % 128, 1)
    return jnp.where(jnp.logical_or(lane < 2, lane >= 126), moved, 0.0)


def edge_correction(other, own, lane):
    lack = other - own
    place = jnp.bitwise_and(lane, 3)
    far = jnp.where(place < 2, -pltpu.roll(lack, 126, 1), pltpu.roll(lack, 2, 1))
    near = jnp.where(place == 1, pltpu.roll(lack, 127, 1), 0.0)
    near = near - jnp.where(place == 2, pltpu.roll(lack, 1, 1), 0.0)
    return far + 8.0 * near


def along_z(tile):
    after = 8.0 * tile - pltpu.roll(tile, 127, 1)
    before = 8.0 * tile - pltpu.roll(tile, 1, 1)
    return pltpu.roll(after, 127, 1) - pltpu.roll(before, 1, 1)


def along_y(tile, pad):
    pad[pl.ds(8, 64), :] = tile
    pad[pl.ds(0, 8), :] = tile[56:]
    pad[pl.ds(72, 8), :] = tile[:8]
    return 8.0 * (pad[pl.ds(9, 64), :] - pad[pl.ds(7, 64), :]) - (
        pad[pl.ds(10, 64), :] - pad[pl.ds(6, 64), :]
    )


def inner_differences(get, velocity, pads, f):
    for i in range(4):
        plane = [velocity[0, j] * get(j) for j in range(4) if 0 < abs(j - i) < 3]
        if i == 0:
            total = 8.0 * plane[0] - plane[1]
        elif i == 1:
            total = 8.0 * (plane[1] - plane[0]) - plane[2]
        elif i == 2:
            total = 8.0 * (plane[2] - plane[1]) + plane[0]
        else:
            total = plane[0] - 8.0 * plane[1]
        total = total + along_y(velocity[1, i] * get(i), pads.at[4 * f + i])
        yield i, total + along_z(velocity[2, i] * get(i))


def sides():
    odd = jnp.bitwise_and(lax.axis_index("brick"), 1)
    even = 1 - odd
    return (
        (3 * even, 1 + even, (1 - 2 * odd).astype(F32)),
        (3 * odd, 1 + odd, (2 * odd - 1).astype(F32)),
    )


def edges_kernel(
    density, energy, lepton, speeds, state, velocity, partial, first, second, packed, pads, sems
):
    copies = [
        pltpu.make_async_copy(ref, state.at[f], sems.at[f])
        for f, ref in enumerate((density, energy, lepton))
    ]
    copies.append(pltpu.make_async_copy(speeds, velocity, sems.at[3]))
    for copy in copies:
        copy.start()
    for copy in copies:
        copy.wait()
    lane = lanes()
    pack = jnp.zeros((64, 128), F32)
    for f in range(3):
        for i, total in inner_differences(lambda i: state[f, i], velocity, pads, f):
            partial[f, i] = total
            pack = pack_z(pack, velocity[2, i] * state[f, i], 4 * (4 * f + i), lane)
    packed[...] = pack
    for (near, far, _), out, start in zip(sides(), (first, second), (48, 72)):
        pack = jnp.zeros((64, 128), F32)
        for k, plane in enumerate((near, far)):
            speed = velocity[0, plane]
            out[12 + k] = speed
            for f in range(3):
                value = state[f, plane]
                out[2 * f + k] = speed * value
                out[6 + 2 * f + k] = speed * (value - HALF * partial[f, plane])
                pack = pack_z(pack, velocity[2, plane] * value, start + 4 * (2 * f + k), lane)
        out[14] = pack


def midpoint_kernel(
    state, velocity, partial, first, second, packed, from_other, deposit, mid, exchanged, total
):
    lane = lanes()
    correction = edge_correction(from_other[...], packed[...], lane)
    for f in range(3):
        for i in range(4):
            total[i] = partial[f, i] + unpack_z(correction, 4 * (4 * f + i), lane)
        for (near, far, sign), side in zip(sides(), (first, second)):
            total[near] += sign * (8.0 * side[2 * f] - side[2 * f + 1])
            total[far] += -sign * side[2 * f]
        for i in range(4):
            mid[f, i] = state[f, i] - HALF * total[i]
    pack = jnp.where(lane < 72, first[14], second[14])
    for f in range(3):
        for i in range(4):
            pack = pack_z(pack, velocity[2, i] * mid[f, i], 4 * (4 * f + i), lane)
    exchanged[...] = pack


def advance_kernel(state, velocity, mid, first, second, deposit, advanced, pads):
    for f in range(3):
        for i, total in inner_differences(lambda i: mid[f, i], velocity, pads, f):
            value = state[f, i] - FULL * total
            if f > 0:
                value = value + deposit[f - 1, pl.ds(64 * i, 64), :]
            advanced[f, i] = value
        for (near, far, sign), side in zip(sides(), (first, second)):
            here = velocity[0, near] * state[f, near]
            behind = velocity[0, far] * state[f, far]
            step = sign * HALF
            close = side[6 + 2 * f] + step * (side[12] * (8.0 * here - behind))
            remote = side[7 + 2 * f] - step * (side[13] * here)
            advanced[f, near] += (-FULL * sign) * (8.0 * close - remote)
            advanced[f, far] += (FULL * sign) * close


def finish_kernel(
    advanced, first, second, sent, from_other, density_out, energy_out, lepton_out, total
):
    lane = lanes()
    correction = edge_correction(from_other[...], sent[...], lane)
    outs = (density_out, energy_out, lepton_out)
    for f in range(3):
        for i in range(4):
            total[i] = unpack_z(correction, 4 * (4 * f + i), lane)
        for (near, far, sign), side, start in zip(sides(), (first, second), (48, 72)):
            start = start + 8 * f
            close = (sign * HALF) * (side[12] * unpack_z(correction, start, lane))
            remote = (sign * HALF) * (side[13] * unpack_z(correction, start + 4, lane))
            total[near] += remote - 8.0 * close
            total[far] += close
        for i in range(4):
            outs[f][i] = advanced[f, i] - FULL * total[i]


def column(row):
    return jnp.transpose(jnp.broadcast_to(row, (128, 128)))


def load_matrices(weak, capture, both, rest):
    matrix = jnp.concatenate([weak[...], capture[...]], axis=1)
    high, low = split(matrix)
    both[...] = jnp.concatenate([high, high], axis=0)
    rest[...] = low


def newton(base, start, get_target, rows_of, both, rest, w_ref, c_ref, x_ref, t_ref, k_ref, a_ref, finish):
    blocks = CHUNK // BLOCK

    def products(b):
        x = x_ref[pl.ds(b * BLOCK, BLOCK), :]
        return matmul(x, both[...]) + matmul(x[:, :128], rest[...])

    def put(b, values):
        high, low = split(values)
        x_ref[pl.ds(b * BLOCK, BLOCK), :] = jnp.concatenate([high, low], axis=1)

    for b in range(blocks):
        put(b, rows_of(b))
    for b in range(blocks):
        at = pl.ds(b * BLOCK, BLOCK)
        here = pl.ds(base + b * BLOCK, BLOCK)
        product = products(b)
        rows = rows_of(b)
        rate_weak, rate_capture = w_ref[here, :], c_ref[here, :]
        alpha = rate_capture * rows[:, 0:1]
        target = rate_weak * product[:, :128] + alpha * product[:, 128:]
        target = get_target(b, rows, target)
        a_ref[at, :] = alpha
        k_ref[at, :] = rate_capture * product[:, 128:]
        t_ref[at, :] = target
        put(b, target)
        start(b, target)
    for sweep in range(SWEEPS):
        for b in range(blocks):
            at = pl.ds(b * BLOCK, BLOCK)
            here = pl.ds(base + b * BLOCK, BLOCK)
            product = products(b)
            before = finish.last[b]
            update = t_ref[at, :] + (
                w_ref[here, :] * product[:, :128]
                + a_ref[at, :] * product[:, 128:]
                + before * k_ref[at, :]
            )
            if sweep < SWEEPS - 1:
                put(b, update)
                start(b, update)
            else:
                finish(b, rows_of(b) + update)


class Finish:
    def __init__(self, write):
        self.last = {}
        self.write = write

    def keep(self, b, values):
        self.last[b] = values[:, 0:1]

    def __call__(self, b, values):
        self.write(b, values)


def network_kernel(
    count, state, cells, rows, weak, capture, mass, binding, charge,
    rows_out, deposit,
    table, both, rest, x_ref, t_ref, k_ref, a_ref, w_ref, c_ref, iterate, gain_both, gain_rest,
):
    load_matrices(weak, capture, both, rest)
    rho, eps, lam = (state[f].reshape(256, 128) for f in range(3))
    inverse = 1.0 / rho
    weak_high, weak_low = split(0.62 + 0.04 * rho + 0.05 * (lam * inverse))
    capture_high, capture_low = split(0.3 * jax.nn.sigmoid(eps * inverse))
    table[...] = jnp.concatenate([weak_high, weak_low, capture_high, capture_low], axis=1)
    gains = jnp.concatenate([column(binding[...]), column(charge[...])], axis=1)
    high, low = split(gains)
    gain_both[...] = jnp.concatenate([high, high], axis=0)
    gain_rest[...] = low
    rows_out[...] = jnp.zeros(rows_out.shape, F32)
    deposit[...] = jnp.zeros(deposit.shape, F32)
    lane = lanes(BLOCK)
    sublane = lax.broadcasted_iota(jnp.int32, (256, 128), 0)
    ones = jnp.ones((256, 128), BF16)

    def chunk(k, carry):
        base = k * CHUNK

        def place(b):
            return pl.ds(pl.multiple_of(base + b * BLOCK, BLOCK), BLOCK)

        def inside(b):
            return pl.ds(b * BLOCK, BLOCK)

        for b in range(CHUNK // BLOCK):
            cell = column(cells[pl.ds(k * (CHUNK // BLOCK) + b, 1), :])
            row_id = lax.shift_right_logical(cell, 7)
            hot = jnp.concatenate([row_id == lane, row_id == lane + 128], axis=1)
            picked = matmul(jnp.where(hot, 1.0, 0.0).astype(BF16), table[...])
            here = jnp.bitwise_and(cell, 127) == lane
            here = jnp.concatenate([here, here, here, here], axis=1)
            picked = jnp.where(here, picked, 0.0).astype(BF16)
            w_ref[inside(b), :] = matmul(picked[:, :256], ones)
            c_ref[inside(b), :] = matmul(picked[:, 256:], ones)

        def write_first(b, values):
            iterate[inside(b), :] = values

        def write_last(b, values):
            slot = base + b * BLOCK + lax.broadcasted_iota(jnp.int32, (BLOCK, 128), 0)
            occupied = slot < count[0, 0]
            rows_out[place(b), :] = jnp.where(occupied, values, 0.0)
            change = jnp.where(occupied, values - rows[place(b), :], 0.0)
            high, low = split(change)
            x_ref[inside(b), :] = jnp.concatenate([high, low], axis=1)

        finish = Finish(write_first)
        newton(
            0, finish.keep, lambda b, current, target: target, lambda b: rows[place(b), :],
            both, rest, w_ref, c_ref, x_ref, t_ref, k_ref, a_ref, finish,
        )
        finish = Finish(write_last)
        newton(
            0, finish.keep, lambda b, current, target: target - (current - rows[place(b), :]),
            lambda b: iterate[inside(b), :],
            both, rest, w_ref, c_ref, x_ref, t_ref, k_ref, a_ref, finish,
        )
        hots, values = [], []
        for b in range(CHUNK // BLOCK):
            number = pl.ds(k * (CHUNK // BLOCK) + b, 1)
            cell = cells[number, :]
            hot = lax.shift_right_logical(cell, 7) == sublane
            hots.append(jnp.where(hot, 1.0, 0.0).astype(BF16))
            x = x_ref[inside(b), :]
            gain = matmul(x, gain_both[...]) + matmul(x[:, :128], gain_rest[...])
            weight = jnp.where(
                jnp.bitwise_and(column(cell), 127) == lane, column(mass[number, :]), 0.0
            )
            gain = gain * jnp.concatenate([weight, weight], axis=1)
            high, low = split(gain)
            values.append(jnp.concatenate([high, low], axis=1))
        sums = matmul(jnp.concatenate(hots, axis=1), jnp.concatenate(values, axis=0))
        deposit[0] += sums[:, :128] + sums[:, 256:384]
        deposit[1] += sums[:, 128:256] + sums[:, 384:]
        return carry

    lax.fori_loop(0, (count[0, 0] + CHUNK - 1) // CHUNK, chunk, 0)


VMEM = pl.BlockSpec(memory_space=pltpu.VMEM)
SMEM = pl.BlockSpec(memory_space=pltpu.SMEM)
HBM = pl.BlockSpec(memory_space=pltpu.HBM)


def call(kernel, name, outs, args, scratch=(), flops=0, first=()):
    args = [
        pltpu.with_memory_space_constraint(a, pltpu.HBM) if s is HBM else a
        for a, s in zip(args, list(first) + [None] * len(args))
    ]
    moved = sum(a.size * 4 for a in args) + sum(4 * math.prod(o) for o in outs)
    return pl.pallas_call(
        kernel,
        name=name,
        out_shape=[jax.ShapeDtypeStruct(o, F32) for o in outs],
        in_specs=list(first) + [VMEM] * (len(args) - len(first)),
        out_specs=[VMEM] * len(outs),
        scratch_shapes=list(scratch),
        compiler_params=pltpu.CompilerParams(vmem_limit_bytes=24 * 2**20),
        cost_estimate=pl.CostEstimate(flops=flops, bytes_accessed=moved, transcendentals=0),
    )(*args)


def swap_halves(packed):
    halves = lax.axis_size("grp")
    return lax.ppermute(packed, "grp", [(i, (i + 1) % halves) for i in range(halves)])


def swap_pairs(first, second):
    count = lax.axis_size("brick")
    even = [(i, i ^ 1) for i in range(count)]
    odd = [(i, (i + 1) % count if i % 2 else (i - 1) % count) for i in range(count)]
    return lax.ppermute(first, "brick", even), lax.ppermute(second, "brick", odd)


def on_device(
    density,
    energy_field,
    lepton_field,
    velocity,
    abundance,
    tracer_mass,
    tracer_cell,
    tracer_count,
    weak_rates,
    capture_rates,
    binding,
    charge_ratio,
):
    fields = (density, energy_field, lepton_field)
    whole, side, tile = (3, 4, 64, 128), (15, 64, 128), (64, 128)
    pads = pltpu.VMEM((12, 80, 128), F32)
    planes = pltpu.VMEM((4, 64, 128), F32)
    state, speeds, partial, first, second, packed = call(
        edges_kernel, "edges", [whole, whole, whole, side, side, tile], (*fields, velocity),
        [pads, pltpu.SemaphoreType.DMA((4,))], 0, [HBM] * 4,
    )
    first, second = swap_pairs(first, second)
    from_other = swap_halves(packed)

    rows = pltpu.VMEM((CHUNK, 128), F32)
    matrices = [pltpu.VMEM((256, 256), BF16), pltpu.VMEM((128, 256), BF16)]
    finished, deposit = call(
        network_kernel, "network", [(1024, 128), (2, 256, 128)],
        (
            tracer_count, state, tracer_cell.reshape(8, 128), abundance.reshape(1024, 128),
            weak_rates, capture_rates, tracer_mass.reshape(8, 128),
            binding.reshape(1, 128), charge_ratio.reshape(1, 128),
        ),
        [pltpu.VMEM((256, 512), BF16), *matrices, pltpu.VMEM((CHUNK, 256), BF16)]
        + [rows] * 6 + matrices,
        6 * 2 * 1024 * 128 * 256 * 18, [SMEM],
    )
    mid, sent = call(
        midpoint_kernel, "midpoint", [whole, tile],
        (state, speeds, partial, first, second, packed, from_other, deposit), [planes],
    )
    from_other = swap_halves(sent)
    (advanced,) = call(
        advance_kernel, "advance", [whole], (state, speeds, mid, first, second, deposit), [pads]
    )
    outs = call(
        finish_kernel, "finish", [(4, 64, 128)] * 3, (advanced, first, second, sent, from_other), [planes]
    )
    return (*outs, finished[None, None])


def solution(mesh):
    return jax.shard_map(
        on_device,
        mesh=mesh,
        in_specs=(
            P("brick", None, "grp"),
            P("brick", None, "grp"),
            P("brick", None, "grp"),
            P(None, "brick", None, "grp"),
            P("grp", "brick", None, None),
            P("grp", "brick", None),
            P("grp", "brick", None),
            P("grp", "brick"),
            P(),
            P(),
            P(),
            P(),
        ),
        out_specs=(
            P("brick", None, "grp"),
            P("brick", None, "grp"),
            P("brick", None, "grp"),
            P("grp", "brick", None, None),
        ),
        check_vma=False,
    )
```

```python
import math

import jax
import jax.numpy as jnp
from jax import lax
from jax.experimental import pallas as pl
from jax.experimental.pallas import tpu as pltpu
from jax.sharding import PartitionSpec as P

SWEEPS = 8
CHUNK = 512
BLOCK = 128
COURANT = 0.8
HALF = 0.5 * COURANT / 12.0
FULL = COURANT / 12.0
F32 = jnp.float32
BF16 = jnp.bfloat16


def split(values):
    high = values.astype(BF16)
    return high, (values - high.astype(F32)).astype(BF16)


def matmul(a, b):
    return lax.dot_general(a, b, (((1,), (0,)), ((), ())), preferred_element_type=F32)


def lanes(rows=64):
    return lax.broadcasted_iota(jnp.int32, (rows, 128), 1)


def groups():
    return lax.shift_right_logical(lanes(), 2)


def spreading():
    row = lax.broadcasted_iota(jnp.int32, (128, 128), 0)
    source = jnp.bitwise_and(126 + jnp.bitwise_and(lanes(128), 3), 127)
    return jnp.where(row == source, 1.0, 0.0)


def circulant():
    row = lax.broadcasted_iota(jnp.int32, (128, 128), 0)
    offset = jnp.bitwise_and(row - lanes(128), 127)
    near = jnp.where(offset == 1, 8.0, jnp.where(offset == 127, -8.0, 0.0))
    return jnp.where(offset == 2, -1.0, jnp.where(offset == 126, 1.0, near))


def twice(matrix):
    matrix = matrix.astype(BF16)
    return jnp.concatenate([matrix, matrix], axis=0)


def parts(values):
    high, low = split(values)
    return jnp.concatenate([high, low], axis=1)


def unpack_z(packed, first, lane):
    moved = pltpu.roll(packed, (126 - first) % 128, 1)
    return jnp.where(jnp.logical_or(lane < 2, lane >= 126), moved, 0.0)


def edge_correction(other, own, lane):
    lack = other - own
    place = jnp.bitwise_and(lane, 3)
    far = jnp.where(place < 2, -pltpu.roll(lack, 126, 1), pltpu.roll(lack, 2, 1))
    near = jnp.where(place == 1, pltpu.roll(lack, 127, 1), 0.0)
    near = near - jnp.where(place == 2, pltpu.roll(lack, 1, 1), 0.0)
    return far + 8.0 * near


def along_y(tile, pad):
    pad[pl.ds(8, 64), :] = tile
    pad[pl.ds(0, 8), :] = tile[56:]
    pad[pl.ds(72, 8), :] = tile[:8]
    return 8.0 * (pad[pl.ds(9, 64), :] - pad[pl.ds(7, 64), :]) - (
        pad[pl.ds(10, 64), :] - pad[pl.ds(6, 64), :]
    )


def inner_differences(get, velocity, pads, f, weights):
    speed_z = [parts(velocity[2, i] * get(i)) for i in range(4)]
    along_z = matmul(jnp.concatenate(speed_z, axis=0), weights)
    for i in range(4):
        plane = [velocity[0, j] * get(j) for j in range(4) if 0 < abs(j - i) < 3]
        if i == 0:
            total = 8.0 * plane[0] - plane[1]
        elif i == 1:
            total = 8.0 * (plane[1] - plane[0]) - plane[2]
        elif i == 2:
            total = 8.0 * (plane[2] - plane[1]) + plane[0]
        else:
            total = plane[0] - 8.0 * plane[1]
        total = total + along_y(velocity[1, i] * get(i), pads.at[4 * f + i])
        here = along_z[64 * i : 64 * i + 64]
        yield i, total + here[:, :128], here[:, 128:]


def sides():
    odd = jnp.bitwise_and(lax.axis_index("brick"), 1)
    even = 1 - odd
    return (
        (3 * even, 1 + even, (1 - 2 * odd).astype(F32)),
        (3 * odd, 1 + odd, (2 * odd - 1).astype(F32)),
    )


def rows_of_tile(number):
    return pl.ds(64 * number, 64)


def edges_kernel(
    density, energy, lepton, speeds,
    state, velocity, partial, first, second, packed,
    pads, spread, sems,
):
    wait_speeds = pltpu.make_async_copy(speeds, velocity, sems.at[3])
    wait_speeds.start()
    copies = [
        pltpu.make_async_copy(ref, state.at[f], sems.at[f])
        for f, ref in enumerate((density, energy, lepton))
    ]
    for copy in copies:
        copy.start()
    weights = twice(jnp.concatenate([circulant(), spreading()], axis=1))
    group = groups()
    pack = jnp.zeros((64, 128), F32)
    wait_speeds.wait()
    for f in range(3):
        copies[f].wait()
        for i, total, edge in inner_differences(
            lambda i: state[f, i], velocity, pads, f, weights
        ):
            partial[f, i] = total
            spread[f, i] = edge
            pack = jnp.where(group == 4 * f + i, edge, pack)
    packed[...] = pack
    group = group[:32]
    for (near, far, _), out in zip(sides(), (first, second)):
        pack = jnp.zeros((32, 128), F32)
        for k, plane in enumerate((near, far)):
            speed = velocity[0, plane]
            out[rows_of_tile(12 + k), :] = speed
            for f in range(3):
                value = state[f, plane]
                out[rows_of_tile(2 * f + k), :] = speed * value
                out[rows_of_tile(6 + 2 * f + k), :] = speed * (value - HALF * partial[f, plane])
                place = 4 * f + 3 - plane
                pack = jnp.where(group == place, spread[f, plane, pl.ds(0, 32), :], pack)
                pack = jnp.where(group == place + 16, spread[f, plane, pl.ds(32, 32), :], pack)
        out[pl.ds(64 * 14, 32), :] = pack


def midpoint_kernel(
    state, velocity, partial, first, second, packed, from_other, deposit, mid, exchanged, total
):
    lane = lanes()
    correction = edge_correction(from_other[...], packed[...], lane)
    group = groups()
    weights = twice(spreading())
    pack = jnp.zeros((64, 128), F32)
    for f in range(3):
        for i in range(4):
            total[i] = partial[f, i] + unpack_z(correction, 4 * (4 * f + i), lane)
        for (near, far, sign), side in zip(sides(), (first, second)):
            close = side[rows_of_tile(2 * f), :]
            total[near] += sign * (8.0 * close - side[rows_of_tile(2 * f + 1), :])
            total[far] += -sign * close
        speed_z = []
        for i in range(4):
            value = state[f, i] - HALF * total[i]
            mid[f, i] = value
            speed_z.append(parts(velocity[2, i] * value))
        edge = matmul(jnp.concatenate(speed_z, axis=0), weights)
        for i in range(4):
            pack = jnp.where(group == 4 * f + i, edge[64 * i : 64 * i + 64], pack)
    exchanged[pl.ds(0, 64), :] = pack
    odd = jnp.bitwise_and(lax.axis_index("brick"), 1)
    upper = jnp.bitwise_and(lax.shift_right_logical(group[:32], 1), 1)
    folded = jnp.where(
        upper != odd, first[pl.ds(64 * 14, 32), :], second[pl.ds(64 * 14, 32), :]
    )
    exchanged[pl.ds(64, 32), :] = folded
    exchanged[pl.ds(96, 32), :] = pltpu.roll(
        jnp.where(upper != odd, first[pl.ds(64 * 14, 32), :], second[pl.ds(64 * 14, 32), :]), 64, 1
    )


def advance_kernel(
    state, velocity, mid, first, second, deposit, advanced, edge_speed, pads
):
    weights = twice(circulant())
    for f in range(3):
        for i, total, _ in inner_differences(lambda i: mid[f, i], velocity, pads, f, weights):
            value = state[f, i] - FULL * total
            if f > 0:
                value = value + deposit[f - 1, pl.ds(64 * i, 64), :]
            advanced[f, i] = value
        for (near, far, sign), side in zip(sides(), (first, second)):
            here = velocity[0, near] * state[f, near]
            behind = velocity[0, far] * state[f, far]
            step = sign * HALF
            speed, speed_far = side[rows_of_tile(12), :], side[rows_of_tile(13), :]
            close = side[rows_of_tile(6 + 2 * f), :] + step * (speed * (8.0 * here - behind))
            remote = side[rows_of_tile(7 + 2 * f), :] - step * (speed_far * here)
            advanced[f, near] += (-FULL * sign) * (8.0 * close - remote)
            advanced[f, far] += (FULL * sign) * close
    weights = twice(spreading())
    plane = jnp.bitwise_and(groups(), 3)
    pack = jnp.zeros((64, 128), F32)
    for (near, far, _), side in zip(sides(), (first, second)):
        for k, number in enumerate((near, far)):
            edge = matmul(parts(side[rows_of_tile(12 + k), :]), weights)
            pack = jnp.where(plane == number, edge, pack)
    edge_speed[...] = pack


def finish_kernel(
    advanced, edge_speed, sent, from_other, density_out, energy_out, lepton_out, result, sems
):
    lane = lanes()
    own, side = pl.ds(0, 64), pl.ds(64, 64)
    correction = edge_correction(from_other[own, :], sent[own, :], lane)
    moved = edge_correction(from_other[side, :], sent[side, :], lane)
    moved = HALF * (edge_speed[...] * moved)
    before, after = pltpu.roll(moved, 4, 1), pltpu.roll(moved, 124, 1)
    plane = jnp.bitwise_and(groups(), 3)
    low = jnp.where(plane == 0, 8.0 * moved - after, -before)
    high = jnp.where(plane == 2, after, before - 8.0 * moved)
    correction = FULL * (correction + jnp.where(plane < 2, low, high))
    copies = []
    for f, out in enumerate((density_out, energy_out, lepton_out)):
        for i in range(4):
            result[f, i] = advanced[f, i] - unpack_z(correction, 4 * (4 * f + i), lane)
        copies.append(pltpu.make_async_copy(result.at[f], out, sems.at[f]))
        copies[f].start()
    for copy in copies:
        copy.wait()


def column(row):
    return jnp.transpose(jnp.broadcast_to(row, (128, 128)))


def load_matrices(weak, capture, both, rest):
    matrix = jnp.concatenate([weak[...], capture[...]], axis=1)
    high, low = split(matrix)
    both[...] = jnp.concatenate([high, high], axis=0)
    rest[...] = low


def newton(base, start, get_target, rows_of, both, rest, w_ref, c_ref, x_ref, t_ref, k_ref, a_ref, finish):
    blocks = CHUNK // BLOCK

    def products(b):
        x = x_ref[pl.ds(b * BLOCK, BLOCK), :]
        return matmul(x, both[...]) + matmul(x[:, :128], rest[...])

    def put(b, values):
        high, low = split(values)
        x_ref[pl.ds(b * BLOCK, BLOCK), :] = jnp.concatenate([high, low], axis=1)

    for b in range(blocks):
        put(b, rows_of(b))
    for b in range(blocks):
        at = pl.ds(b * BLOCK, BLOCK)
        here = pl.ds(base + b * BLOCK, BLOCK)
        product = products(b)
        rows = rows_of(b)
        rate_weak, rate_capture = w_ref[here, :], c_ref[here, :]
        alpha = rate_capture * rows[:, 0:1]
        target = rate_weak * product[:, :128] + alpha * product[:, 128:]
        target = get_target(b, rows, target)
        a_ref[at, :] = alpha
        k_ref[at, :] = rate_capture * product[:, 128:]
        t_ref[at, :] = target
        put(b, target)
        start(b, target)
    for sweep in range(SWEEPS):
        for b in range(blocks):
            at = pl.ds(b * BLOCK, BLOCK)
            here = pl.ds(base + b * BLOCK, BLOCK)
            product = products(b)
            before = finish.last[b]
            update = t_ref[at, :] + (
                w_ref[here, :] * product[:, :128]
                + a_ref[at, :] * product[:, 128:]
                + before * k_ref[at, :]
            )
            if sweep < SWEEPS - 1:
                put(b, update)
                start(b, update)
            else:
                finish(b, rows_of(b) + update)


class Finish:
    def __init__(self, write):
        self.last = {}
        self.write = write

    def keep(self, b, values):
        self.last[b] = values[:, 0:1]

    def __call__(self, b, values):
        self.write(b, values)


def network_kernel(
    count, state, cells, rows, weak, capture, mass, binding, charge,
    rows_out, deposit,
    table, both, rest, x_ref, t_ref, k_ref, a_ref, w_ref, c_ref, iterate, gain_both, gain_rest,
):
    load_matrices(weak, capture, both, rest)
    rho, eps, lam = (state[f].reshape(256, 128) for f in range(3))
    inverse = 1.0 / rho
    weak_high, weak_low = split(0.62 + 0.04 * rho + 0.05 * (lam * inverse))
    capture_high, capture_low = split(0.3 * jax.nn.sigmoid(eps * inverse))
    table[...] = jnp.concatenate([weak_high, weak_low, capture_high, capture_low], axis=1)
    gains = jnp.concatenate([column(binding[...]), column(charge[...])], axis=1)
    high, low = split(gains)
    gain_both[...] = jnp.concatenate([high, high], axis=0)
    gain_rest[...] = low
    rows_out[...] = jnp.zeros(rows_out.shape, F32)
    deposit[...] = jnp.zeros(deposit.shape, F32)
    lane = lanes(BLOCK)
    sublane = lax.broadcasted_iota(jnp.int32, (256, 128), 0)
    ones = jnp.ones((256, 128), BF16)

    def chunk(k, carry):
        base = k * CHUNK

        def place(b):
            return pl.ds(pl.multiple_of(base + b * BLOCK, BLOCK), BLOCK)

        def inside(b):
            return pl.ds(b * BLOCK, BLOCK)

        for b in range(CHUNK // BLOCK):
            cell = column(cells[pl.ds(k * (CHUNK // BLOCK) + b, 1), :])
            row_id = lax.shift_right_logical(cell, 7)
            hot = jnp.concatenate([row_id == lane, row_id == lane + 128], axis=1)
            picked = matmul(jnp.where(hot, 1.0, 0.0).astype(BF16), table[...])
            here = jnp.bitwise_and(cell, 127) == lane
            here = jnp.concatenate([here, here, here, here], axis=1)
            picked = jnp.where(here, picked, 0.0).astype(BF16)
            w_ref[inside(b), :] = matmul(picked[:, :256], ones)
            c_ref[inside(b), :] = matmul(picked[:, 256:], ones)

        def write_first(b, values):
            iterate[inside(b), :] = values

        def write_last(b, values):
            slot = base + b * BLOCK + lax.broadcasted_iota(jnp.int32, (BLOCK, 128), 0)
            occupied = slot < count[0, 0]
            rows_out[place(b), :] = jnp.where(occupied, values, 0.0)
            change = jnp.where(occupied, values - rows[place(b), :], 0.0)
            high, low = split(change)
            x_ref[inside(b), :] = jnp.concatenate([high, low], axis=1)

        finish = Finish(write_first)
        newton(
            0, finish.keep, lambda b, current, target: target, lambda b: rows[place(b), :],
            both, rest, w_ref, c_ref, x_ref, t_ref, k_ref, a_ref, finish,
        )
        finish = Finish(write_last)
        newton(
            0, finish.keep, lambda b, current, target: target - (current - rows[place(b), :]),
            lambda b: iterate[inside(b), :],
            both, rest, w_ref, c_ref, x_ref, t_ref, k_ref, a_ref, finish,
        )
        hots, values = [], []
        for b in range(CHUNK // BLOCK):
            number = pl.ds(k * (CHUNK // BLOCK) + b, 1)
            cell = cells[number, :]
            hot = lax.shift_right_logical(cell, 7) == sublane
            hots.append(jnp.where(hot, 1.0, 0.0).astype(BF16))
            x = x_ref[inside(b), :]
            gain = matmul(x, gain_both[...]) + matmul(x[:, :128], gain_rest[...])
            weight = jnp.where(
                jnp.bitwise_and(column(cell), 127) == lane, column(mass[number, :]), 0.0
            )
            gain = gain * jnp.concatenate([weight, weight], axis=1)
            high, low = split(gain)
            values.append(jnp.concatenate([high, low], axis=1))
        sums = matmul(jnp.concatenate(hots, axis=1), jnp.concatenate(values, axis=0))
        deposit[0] += sums[:, :128] + sums[:, 256:384]
        deposit[1] += sums[:, 128:256] + sums[:, 384:]
        return carry

    lax.fori_loop(0, (count[0, 0] + CHUNK - 1) // CHUNK, chunk, 0)


VMEM = pl.BlockSpec(memory_space=pltpu.VMEM)
SMEM = pl.BlockSpec(memory_space=pltpu.SMEM)
HBM = pl.BlockSpec(memory_space=pltpu.HBM)


def call(kernel, name, outs, args, scratch=(), flops=0, first=(), out=VMEM):
    args = [
        pltpu.with_memory_space_constraint(a, pltpu.HBM) if s is HBM else a
        for a, s in zip(args, list(first) + [None] * len(args))
    ]
    moved = sum(a.size * 4 for a in args) + sum(4 * math.prod(o) for o in outs)
    return pl.pallas_call(
        kernel,
        name=name,
        out_shape=[jax.ShapeDtypeStruct(o, F32) for o in outs],
        in_specs=list(first) + [VMEM] * (len(args) - len(first)),
        out_specs=[out] * len(outs),
        scratch_shapes=list(scratch),
        compiler_params=pltpu.CompilerParams(vmem_limit_bytes=24 * 2**20),
        cost_estimate=pl.CostEstimate(flops=flops, bytes_accessed=moved, transcendentals=0),
    )(*args)


def swap_halves(packed):
    halves = lax.axis_size("grp")
    return lax.ppermute(packed, "grp", [(i, (i + 1) % halves) for i in range(halves)])


def swap_pairs(first, second):
    count = lax.axis_size("brick")
    even = [(i, i ^ 1) for i in range(count)]
    odd = [(i, (i + 1) % count if i % 2 else (i - 1) % count) for i in range(count)]
    return lax.ppermute(first, "brick", even), lax.ppermute(second, "brick", odd)


def on_device(
    density,
    energy_field,
    lepton_field,
    velocity,
    abundance,
    tracer_mass,
    tracer_cell,
    tracer_count,
    weak_rates,
    capture_rates,
    binding,
    charge_ratio,
):
    fields = (density, energy_field, lepton_field)
    whole, side, tile = (3, 4, 64, 128), (928, 128), (64, 128)
    pads = pltpu.VMEM((12, 80, 128), F32)
    planes = pltpu.VMEM((4, 64, 128), F32)
    state, speeds, partial, first, second, packed = call(
        edges_kernel, "edges", [whole, whole, whole, side, side, tile], (*fields, velocity),
        [pads, pltpu.VMEM(whole, F32), pltpu.SemaphoreType.DMA((4,))], 0, [HBM] * 4,
    )
    first, second = swap_pairs(first, second)

    rows = pltpu.VMEM((CHUNK, 128), F32)
    matrices = [pltpu.VMEM((256, 256), BF16), pltpu.VMEM((128, 256), BF16)]
    finished, deposit = call(
        network_kernel, "network", [(1024, 128), (2, 256, 128)],
        (
            tracer_count, state, tracer_cell.reshape(8, 128), abundance.reshape(1024, 128),
            weak_rates, capture_rates, tracer_mass.reshape(8, 128),
            binding.reshape(1, 128), charge_ratio.reshape(1, 128),
        ),
        [pltpu.VMEM((256, 512), BF16), *matrices, pltpu.VMEM((CHUNK, 256), BF16)]
        + [rows] * 6 + matrices,
        6 * 2 * 1024 * 128 * 256 * 18, [SMEM],
    )
    packed, deposit = lax.optimization_barrier((packed, deposit))
    from_other = swap_halves(packed)
    mid, sent = call(
        midpoint_kernel, "midpoint", [whole, (128, 128)],
        (state, speeds, partial, first, second, packed, from_other, deposit), [planes],
    )
    from_other = swap_halves(sent)
    advanced, edge_speed = call(
        advance_kernel, "advance", [whole, tile], (state, speeds, mid, first, second, deposit), [pads]
    )
    outs = call(
        finish_kernel, "finish", [(4, 64, 128)] * 3, (advanced, edge_speed, sent, from_other),
        [pltpu.VMEM(whole, F32), pltpu.SemaphoreType.DMA((3,))], 0, (), pl.BlockSpec(memory_space=pl.ANY),
    )
    return (*outs, finished[None, None])


def solution(mesh):
    return jax.shard_map(
        on_device,
        mesh=mesh,
        in_specs=(
            P("brick", None, "grp"),
            P("brick", None, "grp"),
            P("brick", None, "grp"),
            P(None, "brick", None, "grp"),
            P("grp", "brick", None, None),
            P("grp", "brick", None),
            P("grp", "brick", None),
            P("grp", "brick"),
            P(),
            P(),
            P(),
            P(),
        ),
        out_specs=(
            P("brick", None, "grp"),
            P("brick", None, "grp"),
            P("brick", None, "grp"),
            P("grp", "brick", None, None),
        ),
        check_vma=False,
    )
```

```python
import math

import jax
import jax.numpy as jnp
from jax import lax
from jax.experimental import pallas as pl
from jax.experimental.pallas import tpu as pltpu
from jax.sharding import PartitionSpec as P

SWEEPS = 8
CHUNK = 512
BLOCK = 128
COURANT = 0.8
HALF = 0.5 * COURANT / 12.0
FULL = COURANT / 12.0
F32 = jnp.float32
BF16 = jnp.bfloat16


def split(values):
    high = values.astype(BF16)
    return high, (values - high.astype(F32)).astype(BF16)


def matmul(a, b):
    return lax.dot_general(a, b, (((1,), (0,)), ((), ())), preferred_element_type=F32)


def lanes(rows=64):
    return lax.broadcasted_iota(jnp.int32, (rows, 128), 1)


def groups():
    return lax.shift_right_logical(lanes(), 2)


def spreading():
    row = lax.broadcasted_iota(jnp.int32, (128, 128), 0)
    source = jnp.bitwise_and(126 + jnp.bitwise_and(lanes(128), 3), 127)
    return jnp.where(row == source, 1.0, 0.0)


def circulant():
    row = lax.broadcasted_iota(jnp.int32, (128, 128), 0)
    offset = jnp.bitwise_and(row - lanes(128), 127)
    near = jnp.where(offset == 1, 8.0, jnp.where(offset == 127, -8.0, 0.0))
    return jnp.where(offset == 2, -1.0, jnp.where(offset == 126, 1.0, near))


def twice(matrix):
    matrix = matrix.astype(BF16)
    return jnp.concatenate([matrix, matrix], axis=0)


def parts(values):
    high, low = split(values)
    return jnp.concatenate([high, low], axis=1)


def unpack_z(packed, first, lane):
    moved = pltpu.roll(packed, (126 - first) % 128, 1)
    return jnp.where(jnp.logical_or(lane < 2, lane >= 126), moved, 0.0)


def edge_correction(other, own, lane):
    lack = other - own
    place = jnp.bitwise_and(lane, 3)
    far = jnp.where(place < 2, -pltpu.roll(lack, 126, 1), pltpu.roll(lack, 2, 1))
    near = jnp.where(place == 1, pltpu.roll(lack, 127, 1), 0.0)
    near = near - jnp.where(place == 2, pltpu.roll(lack, 1, 1), 0.0)
    return far + 8.0 * near


def along_y(tile, pad):
    pad[pl.ds(8, 64), :] = tile
    pad[pl.ds(0, 8), :] = tile[56:]
    pad[pl.ds(72, 8), :] = tile[:8]
    return 8.0 * (pad[pl.ds(9, 64), :] - pad[pl.ds(7, 64), :]) - (
        pad[pl.ds(10, 64), :] - pad[pl.ds(6, 64), :]
    )


def inner_differences(get, velocity, pads, f, weights):
    speed_z = [parts(velocity[2, i] * get(i)) for i in range(4)]
    along_z = matmul(jnp.concatenate(speed_z, axis=0), weights)
    for i in range(4):
        plane = [velocity[0, j] * get(j) for j in range(4) if 0 < abs(j - i) < 3]
        if i == 0:
            total = 8.0 * plane[0] - plane[1]
        elif i == 1:
            total = 8.0 * (plane[1] - plane[0]) - plane[2]
        elif i == 2:
            total = 8.0 * (plane[2] - plane[1]) + plane[0]
        else:
            total = plane[0] - 8.0 * plane[1]
        total = total + along_y(velocity[1, i] * get(i), pads.at[4 * f + i])
        here = along_z[64 * i : 64 * i + 64]
        yield i, total + here[:, :128], here[:, 128:]


def sides(low, high):
    return ((0, 1, -1.0, low), (3, 2, 1.0, high))


def rows_of_tile(number):
    return pl.ds(64 * number, 64)


def edges_kernel(
    density, energy, lepton, speeds,
    state, velocity, partial, first, second, packed,
    pads, spread, sems,
):
    wait_speeds = pltpu.make_async_copy(speeds, velocity, sems.at[3])
    wait_speeds.start()
    copies = [
        pltpu.make_async_copy(ref, state.at[f], sems.at[f])
        for f, ref in enumerate((density, energy, lepton))
    ]
    for copy in copies:
        copy.start()
    weights = twice(jnp.concatenate([circulant(), spreading()], axis=1))
    group = groups()
    pack = jnp.zeros((64, 128), F32)
    wait_speeds.wait()
    for f in range(3):
        copies[f].wait()
        for i, total, edge in inner_differences(
            lambda i: state[f, i], velocity, pads, f, weights
        ):
            partial[f, i] = total
            spread[f, i] = edge
            pack = jnp.where(group == 4 * f + i, edge, pack)
    packed[...] = pack
    group = group[:32]
    for near, far, out in ((3, 2, first), (0, 1, second)):
        pack = jnp.zeros((32, 128), F32)
        for k, plane in enumerate((near, far)):
            speed = velocity[0, plane]
            out[rows_of_tile(12 + k), :] = speed
            for f in range(3):
                value = state[f, plane]
                out[rows_of_tile(2 * f + k), :] = speed * value
                out[rows_of_tile(6 + 2 * f + k), :] = speed * (value - HALF * partial[f, plane])
                place = 4 * f + 3 - plane
                pack = jnp.where(group == place, spread[f, plane, pl.ds(0, 32), :], pack)
                pack = jnp.where(group == place + 16, spread[f, plane, pl.ds(32, 32), :], pack)
        out[pl.ds(64 * 14, 32), :] = pack


def midpoint_kernel(
    state, velocity, partial, first, second, packed, from_other, deposit, mid, exchanged, total
):
    lane = lanes()
    correction = edge_correction(from_other[...], packed[...], lane)
    group = groups()
    weights = twice(spreading())
    pack = jnp.zeros((64, 128), F32)
    for f in range(3):
        for i in range(4):
            total[i] = partial[f, i] + unpack_z(correction, 4 * (4 * f + i), lane)
        for near, far, sign, side in sides(first, second):
            close = side[rows_of_tile(2 * f), :]
            total[near] += sign * (8.0 * close - side[rows_of_tile(2 * f + 1), :])
            total[far] += -sign * close
        speed_z = []
        for i in range(4):
            value = state[f, i] - HALF * total[i]
            mid[f, i] = value
            speed_z.append(parts(velocity[2, i] * value))
        edge = matmul(jnp.concatenate(speed_z, axis=0), weights)
        for i in range(4):
            pack = jnp.where(group == 4 * f + i, edge[64 * i : 64 * i + 64], pack)
    exchanged[pl.ds(0, 64), :] = pack
    edge = pl.ds(64 * 14, 32)
    upper = jnp.bitwise_and(group[:32], 3) >= 2
    folded = jnp.where(upper, second[edge, :], first[edge, :])
    exchanged[pl.ds(64, 32), :] = folded
    exchanged[pl.ds(96, 32), :] = pltpu.roll(folded, 64, 1)


def advance_kernel(
    state, velocity, mid, first, second, deposit, advanced, edge_speed, pads
):
    weights = twice(circulant())
    for f in range(3):
        for i, total, _ in inner_differences(lambda i: mid[f, i], velocity, pads, f, weights):
            value = state[f, i] - FULL * total
            if f > 0:
                value = value + deposit[f - 1, pl.ds(64 * i, 64), :]
            advanced[f, i] = value
        for near, far, sign, side in sides(first, second):
            here = velocity[0, near] * state[f, near]
            behind = velocity[0, far] * state[f, far]
            step = sign * HALF
            speed, speed_far = side[rows_of_tile(12), :], side[rows_of_tile(13), :]
            close = side[rows_of_tile(6 + 2 * f), :] + step * (speed * (8.0 * here - behind))
            remote = side[rows_of_tile(7 + 2 * f), :] - step * (speed_far * here)
            advanced[f, near] += (-FULL * sign) * (8.0 * close - remote)
            advanced[f, far] += (FULL * sign) * close
    weights = twice(spreading())
    plane = jnp.bitwise_and(groups(), 3)
    pack = jnp.zeros((64, 128), F32)
    for near, far, _, side in sides(first, second):
        for k, number in enumerate((near, far)):
            edge = matmul(parts(side[rows_of_tile(12 + k), :]), weights)
            pack = jnp.where(plane == number, edge, pack)
    edge_speed[...] = pack


def finish_kernel(
    advanced, edge_speed, sent, from_other, density_out, energy_out, lepton_out, result, sems
):
    lane = lanes()
    own, side = pl.ds(0, 64), pl.ds(64, 64)
    correction = edge_correction(from_other[own, :], sent[own, :], lane)
    moved = edge_correction(from_other[side, :], sent[side, :], lane)
    moved = HALF * (edge_speed[...] * moved)
    before, after = pltpu.roll(moved, 4, 1), pltpu.roll(moved, 124, 1)
    plane = jnp.bitwise_and(groups(), 3)
    low = jnp.where(plane == 0, 8.0 * moved - after, -before)
    high = jnp.where(plane == 2, after, before - 8.0 * moved)
    correction = FULL * (correction + jnp.where(plane < 2, low, high))
    copies = []
    for f, out in enumerate((density_out, energy_out, lepton_out)):
        for i in range(4):
            result[f, i] = advanced[f, i] - unpack_z(correction, 4 * (4 * f + i), lane)
        copies.append(pltpu.make_async_copy(result.at[f], out, sems.at[f]))
        copies[f].start()
    for copy in copies:
        copy.wait()


def column(row):
    return jnp.transpose(jnp.broadcast_to(row, (128, 128)))


def load_matrices(weak, capture, both, rest):
    matrix = jnp.concatenate([weak[...], capture[...]], axis=1)
    high, low = split(matrix)
    both[...] = jnp.concatenate([high, high], axis=0)
    rest[...] = low


def newton(base, start, get_target, rows_of, both, rest, w_ref, c_ref, x_ref, t_ref, k_ref, a_ref, finish):
    blocks = CHUNK // BLOCK

    def products(b):
        x = x_ref[pl.ds(b * BLOCK, BLOCK), :]
        return matmul(x, both[...]) + matmul(x[:, :128], rest[...])

    def put(b, values):
        high, low = split(values)
        x_ref[pl.ds(b * BLOCK, BLOCK), :] = jnp.concatenate([high, low], axis=1)

    for b in range(blocks):
        put(b, rows_of(b))
    for b in range(blocks):
        at = pl.ds(b * BLOCK, BLOCK)
        here = pl.ds(base + b * BLOCK, BLOCK)
        product = products(b)
        rows = rows_of(b)
        rate_weak, rate_capture = w_ref[here, :], c_ref[here, :]
        alpha = rate_capture * rows[:, 0:1]
        target = rate_weak * product[:, :128] + alpha * product[:, 128:]
        target = get_target(b, rows, target)
        a_ref[at, :] = alpha
        k_ref[at, :] = rate_capture * product[:, 128:]
        t_ref[at, :] = target
        put(b, target)
        start(b, target)
    for sweep in range(SWEEPS):
        for b in range(blocks):
            at = pl.ds(b * BLOCK, BLOCK)
            here = pl.ds(base + b * BLOCK, BLOCK)
            product = products(b)
            before = finish.last[b]
            update = t_ref[at, :] + (
                w_ref[here, :] * product[:, :128]
                + a_ref[at, :] * product[:, 128:]
                + before * k_ref[at, :]
            )
            if sweep < SWEEPS - 1:
                put(b, update)
                start(b, update)
            else:
                finish(b, rows_of(b) + update)


class Finish:
    def __init__(self, write):
        self.last = {}
        self.write = write

    def keep(self, b, values):
        self.last[b] = values[:, 0:1]

    def __call__(self, b, values):
        self.write(b, values)


def fill_table(state, table):
    rho, eps, lam = (state[f].reshape(256, 128) for f in range(3))
    inverse = 1.0 / rho
    weak_high, weak_low = split(0.62 + 0.04 * rho + 0.05 * (lam * inverse))
    capture_high, capture_low = split(0.3 * jax.nn.sigmoid(eps * inverse))
    table[...] = jnp.concatenate([weak_high, weak_low, capture_high, capture_low], axis=1)


def chunks(count):
    return (count[0, 0] + CHUNK - 1) // CHUNK


def first_kernel(
    count, state, cells, rows, weak, capture,
    iterate, w_out, c_out,
    table, both, rest, x_ref, t_ref, k_ref, a_ref,
):
    load_matrices(weak, capture, both, rest)
    fill_table(state, table)
    lane = lanes(BLOCK)
    ones = jnp.ones((256, 128), BF16)

    def chunk(k, carry):
        base = pl.multiple_of(k * CHUNK, CHUNK)

        def place(b):
            return pl.ds(pl.multiple_of(base + b * BLOCK, BLOCK), BLOCK)

        for b in range(CHUNK // BLOCK):
            cell = column(cells[pl.ds(k * (CHUNK // BLOCK) + b, 1), :])
            row_id = lax.shift_right_logical(cell, 7)
            hot = jnp.concatenate([row_id == lane, row_id == lane + 128], axis=1)
            picked = matmul(jnp.where(hot, 1.0, 0.0).astype(BF16), table[...])
            here = jnp.bitwise_and(cell, 127) == lane
            here = jnp.concatenate([here, here, here, here], axis=1)
            picked = jnp.where(here, picked, 0.0).astype(BF16)
            w_out[place(b), :] = matmul(picked[:, :256], ones)
            c_out[place(b), :] = matmul(picked[:, 256:], ones)

        def write(b, values):
            iterate[place(b), :] = values

        finish = Finish(write)
        newton(
            base, finish.keep, lambda b, current, target: target, lambda b: rows[place(b), :],
            both, rest, w_out, c_out, x_ref, t_ref, k_ref, a_ref, finish,
        )
        return carry

    lax.fori_loop(0, chunks(count), chunk, 0)


def second_kernel(
    count, cells, rows, weak, capture, mass, binding, charge, iterate, w_ref, c_ref,
    rows_out, deposit,
    both, rest, x_ref, t_ref, k_ref, a_ref, gain_both, gain_rest,
):
    load_matrices(weak, capture, both, rest)
    gains = jnp.concatenate([column(binding[...]), column(charge[...])], axis=1)
    high, low = split(gains)
    gain_both[...] = jnp.concatenate([high, high], axis=0)
    gain_rest[...] = low
    rows_out[...] = jnp.zeros(rows_out.shape, F32)
    deposit[...] = jnp.zeros(deposit.shape, F32)
    lane = lanes(BLOCK)
    sublane = lax.broadcasted_iota(jnp.int32, (256, 128), 0)

    def chunk(k, carry):
        base = pl.multiple_of(k * CHUNK, CHUNK)

        def place(b):
            return pl.ds(pl.multiple_of(base + b * BLOCK, BLOCK), BLOCK)

        def inside(b):
            return pl.ds(b * BLOCK, BLOCK)

        def write(b, values):
            slot = base + b * BLOCK + lax.broadcasted_iota(jnp.int32, (BLOCK, 128), 0)
            occupied = slot < count[0, 0]
            rows_out[place(b), :] = jnp.where(occupied, values, 0.0)
            change = jnp.where(occupied, values - rows[place(b), :], 0.0)
            x_ref[inside(b), :] = parts(change)

        finish = Finish(write)
        newton(
            base, finish.keep, lambda b, current, target: target - (current - rows[place(b), :]),
            lambda b: iterate[place(b), :],
            both, rest, w_ref, c_ref, x_ref, t_ref, k_ref, a_ref, finish,
        )
        hots, values = [], []
        for b in range(CHUNK // BLOCK):
            number = pl.ds(k * (CHUNK // BLOCK) + b, 1)
            cell = cells[number, :]
            hot = lax.shift_right_logical(cell, 7) == sublane
            hots.append(jnp.where(hot, 1.0, 0.0).astype(BF16))
            x = x_ref[inside(b), :]
            gain = matmul(x, gain_both[...]) + matmul(x[:, :128], gain_rest[...])
            weight = jnp.where(
                jnp.bitwise_and(column(cell), 127) == lane, column(mass[number, :]), 0.0
            )
            gain = gain * jnp.concatenate([weight, weight], axis=1)
            values.append(parts(gain))
        sums = matmul(jnp.concatenate(hots, axis=1), jnp.concatenate(values, axis=0))
        deposit[0] += sums[:, :128] + sums[:, 256:384]
        deposit[1] += sums[:, 128:256] + sums[:, 384:]
        return carry

    lax.fori_loop(0, chunks(count), chunk, 0)


VMEM = pl.BlockSpec(memory_space=pltpu.VMEM)
SMEM = pl.BlockSpec(memory_space=pltpu.SMEM)
HBM = pl.BlockSpec(memory_space=pltpu.HBM)


def call(kernel, name, outs, args, scratch=(), flops=0, first=(), out=VMEM):
    args = [
        pltpu.with_memory_space_constraint(a, pltpu.HBM) if s is HBM else a
        for a, s in zip(args, list(first) + [None] * len(args))
    ]
    moved = sum(a.size * 4 for a in args) + sum(4 * math.prod(o) for o in outs)
    return pl.pallas_call(
        kernel,
        name=name,
        out_shape=[jax.ShapeDtypeStruct(o, F32) for o in outs],
        in_specs=list(first) + [VMEM] * (len(args) - len(first)),
        out_specs=[out] * len(outs),
        scratch_shapes=list(scratch),
        compiler_params=pltpu.CompilerParams(vmem_limit_bytes=24 * 2**20),
        cost_estimate=pl.CostEstimate(flops=flops, bytes_accessed=moved, transcendentals=0),
    )(*args)


def swap_halves(packed):
    halves = lax.axis_size("grp")
    return lax.ppermute(packed, "grp", [(i, (i + 1) % halves) for i in range(halves)])


def send(message, step):
    count = lax.axis_size("brick")
    return lax.ppermute(message, "brick", [(i, (i + step) % count) for i in range(count)])


def on_device(
    density,
    energy_field,
    lepton_field,
    velocity,
    abundance,
    tracer_mass,
    tracer_cell,
    tracer_count,
    weak_rates,
    capture_rates,
    binding,
    charge_ratio,
):
    fields = (density, energy_field, lepton_field)
    whole, side, tile = (3, 4, 64, 128), (928, 128), (64, 128)
    pads = pltpu.VMEM((12, 80, 128), F32)
    planes = pltpu.VMEM((4, 64, 128), F32)
    state, speeds, partial, first, second, packed = call(
        edges_kernel, "edges", [whole, whole, whole, side, side, tile], (*fields, velocity),
        [pads, pltpu.VMEM(whole, F32), pltpu.SemaphoreType.DMA((4,))], 0, [HBM] * 4,
    )
    first = send(first, 1)

    rows = abundance.reshape(1024, 128)
    cells = tracer_cell.reshape(8, 128)
    scratch = [pltpu.VMEM((256, 256), BF16), pltpu.VMEM((128, 256), BF16)]
    scratch += [pltpu.VMEM((CHUNK, 256), BF16)] + [pltpu.VMEM((CHUNK, 128), F32)] * 3
    flops = 6 * 2 * 1024 * 128 * 256 * 9
    solved = call(
        first_kernel, "newton_first", [(1024, 128)] * 3,
        (tracer_count, state, cells, rows, weak_rates, capture_rates),
        [pltpu.VMEM((256, 512), BF16), *scratch], flops, [SMEM],
    )
    second, *solved = lax.optimization_barrier((second, *solved))
    second = send(second, -1)
    finished, deposit = call(
        second_kernel, "newton_second", [(1024, 128), (2, 256, 128)],
        (
            tracer_count, cells, rows, weak_rates, capture_rates, tracer_mass.reshape(8, 128),
            binding.reshape(1, 128), charge_ratio.reshape(1, 128), *solved,
        ),
        [*scratch, *scratch[:2]], flops, [SMEM],
    )
    packed, deposit = lax.optimization_barrier((packed, deposit))
    from_other = swap_halves(packed)
    mid, sent = call(
        midpoint_kernel, "midpoint", [whole, (128, 128)],
        (state, speeds, partial, first, second, packed, from_other, deposit), [planes],
    )
    from_other = swap_halves(sent)
    advanced, edge_speed = call(
        advance_kernel, "advance", [whole, tile], (state, speeds, mid, first, second, deposit), [pads]
    )
    outs = call(
        finish_kernel, "finish", [(4, 64, 128)] * 3, (advanced, edge_speed, sent, from_other),
        [pltpu.VMEM(whole, F32), pltpu.SemaphoreType.DMA((3,))], 0, (), pl.BlockSpec(memory_space=pl.ANY),
    )
    return (*outs, finished[None, None])


def solution(mesh):
    return jax.shard_map(
        on_device,
        mesh=mesh,
        in_specs=(
            P("brick", None, "grp"),
            P("brick", None, "grp"),
            P("brick", None, "grp"),
            P(None, "brick", None, "grp"),
            P("grp", "brick", None, None),
            P("grp", "brick", None),
            P("grp", "brick", None),
            P("grp", "brick"),
            P(),
            P(),
            P(),
            P(),
        ),
        out_specs=(
            P("brick", None, "grp"),
            P("brick", None, "grp"),
            P("brick", None, "grp"),
            P("grp", "brick", None, None),
        ),
        check_vma=False,
    )
```

```python
import math

import jax
import jax.numpy as jnp
from jax import lax
from jax.experimental import pallas as pl
from jax.experimental.pallas import tpu as pltpu
from jax.sharding import PartitionSpec as P

SWEEPS = 8
CHUNK = 512
BLOCK = 128
COURANT = 0.8
HALF = 0.5 * COURANT / 12.0
FULL = COURANT / 12.0
F32 = jnp.float32
BF16 = jnp.bfloat16


def split(values):
    high = values.astype(BF16)
    return high, (values - high.astype(F32)).astype(BF16)


def matmul(a, b):
    return lax.dot_general(a, b, (((1,), (0,)), ((), ())), preferred_element_type=F32)


def lanes(rows=64):
    return lax.broadcasted_iota(jnp.int32, (rows, 128), 1)


def groups():
    return lax.shift_right_logical(lanes(), 2)


def spreading():
    row = lax.broadcasted_iota(jnp.int32, (128, 128), 0)
    source = jnp.bitwise_and(126 + jnp.bitwise_and(lanes(128), 3), 127)
    return jnp.where(row == source, 1.0, 0.0)


def circulant():
    row = lax.broadcasted_iota(jnp.int32, (128, 128), 0)
    offset = jnp.bitwise_and(row - lanes(128), 127)
    near = jnp.where(offset == 1, 8.0, jnp.where(offset == 127, -8.0, 0.0))
    return jnp.where(offset == 2, -1.0, jnp.where(offset == 126, 1.0, near))


def twice(matrix):
    matrix = matrix.astype(BF16)
    return jnp.concatenate([matrix, matrix], axis=0)


def parts(values):
    high, low = split(values)
    return jnp.concatenate([high, low], axis=1)


def unpack_z(packed, first, lane):
    moved = pltpu.roll(packed, (126 - first) % 128, 1)
    return jnp.where(jnp.logical_or(lane < 2, lane >= 126), moved, 0.0)


def edge_correction(other, own, lane):
    lack = other - own
    place = jnp.bitwise_and(lane, 3)
    far = jnp.where(place < 2, -pltpu.roll(lack, 126, 1), pltpu.roll(lack, 2, 1))
    near = jnp.where(place == 1, pltpu.roll(lack, 127, 1), 0.0)
    near = near - jnp.where(place == 2, pltpu.roll(lack, 1, 1), 0.0)
    return far + 8.0 * near


def along_y(tile, pad):
    pad[pl.ds(8, 64), :] = tile
    pad[pl.ds(0, 8), :] = tile[56:]
    pad[pl.ds(72, 8), :] = tile[:8]
    return 8.0 * (pad[pl.ds(9, 64), :] - pad[pl.ds(7, 64), :]) - (
        pad[pl.ds(10, 64), :] - pad[pl.ds(6, 64), :]
    )


def inner_differences(get, velocity, pads, f, weights):
    speed_z = [parts(velocity[2, i] * get(i)) for i in range(4)]
    along_z = matmul(jnp.concatenate(speed_z, axis=0), weights)
    for i in range(4):
        plane = [velocity[0, j] * get(j) for j in range(4) if 0 < abs(j - i) < 3]
        if i == 0:
            total = 8.0 * plane[0] - plane[1]
        elif i == 1:
            total = 8.0 * (plane[1] - plane[0]) - plane[2]
        elif i == 2:
            total = 8.0 * (plane[2] - plane[1]) + plane[0]
        else:
            total = plane[0] - 8.0 * plane[1]
        total = total + along_y(velocity[1, i] * get(i), pads.at[4 * f + i])
        here = along_z[64 * i : 64 * i + 64]
        yield i, total + here[:, :128], here[:, 128:]


SIDES = ((0, 1, -1.0), (3, 2, 1.0))


def rows_of_tile(number):
    return pl.ds(64 * number, 64)


def edges_kernel(
    density, energy, lepton, speeds,
    state, velocity, partial, low_first, low_second, high, packed,
    pads, spread, sems,
):
    wait_speeds = pltpu.make_async_copy(speeds, velocity, sems.at[3])
    wait_speeds.start()
    copies = [
        pltpu.make_async_copy(ref, state.at[f], sems.at[f])
        for f, ref in enumerate((density, energy, lepton))
    ]
    for copy in copies:
        copy.start()
    weights = twice(jnp.concatenate([circulant(), spreading()], axis=1))
    group = groups()
    pack = jnp.zeros((64, 128), F32)
    wait_speeds.wait()
    for f in range(3):
        copies[f].wait()
        for i, total, edge in inner_differences(
            lambda i: state[f, i], velocity, pads, f, weights
        ):
            partial[f, i] = total
            spread[f, i] = edge
            pack = jnp.where(group == 4 * f + i, edge, pack)
    packed[...] = pack
    group = group[:32]
    for near, far, early, late, start in (
        (3, 2, low_first, low_second, 0),
        (0, 1, high, high, 416),
    ):
        pack = jnp.zeros((32, 128), F32)
        for k, plane in enumerate((near, far)):
            speed = velocity[0, plane]
            late[pl.ds(start + 64 * (6 + k), 64), :] = speed
            for f in range(3):
                value = state[f, plane]
                early[rows_of_tile(2 * f + k), :] = speed * value
                late[pl.ds(start + 64 * (2 * f + k), 64), :] = speed * (
                    value - HALF * partial[f, plane]
                )
                place = 4 * f + 3 - plane
                pack = jnp.where(group == place, spread[f, plane, pl.ds(0, 32), :], pack)
                pack = jnp.where(group == place + 16, spread[f, plane, pl.ds(32, 32), :], pack)
        early[pl.ds(384, 32), :] = pack


def midpoint_kernel(
    state, velocity, partial, low, high, packed, from_other, deposit, mid, exchanged, total
):
    lane = lanes()
    correction = edge_correction(from_other[...], packed[...], lane)
    group = groups()
    weights = twice(spreading())
    pack = jnp.zeros((64, 128), F32)
    for f in range(3):
        for i in range(4):
            total[i] = partial[f, i] + unpack_z(correction, 4 * (4 * f + i), lane)
        for (near, far, sign), side in zip(SIDES, (low, high)):
            close = side[rows_of_tile(2 * f), :]
            total[near] += sign * (8.0 * close - side[rows_of_tile(2 * f + 1), :])
            total[far] += -sign * close
        speed_z = []
        for i in range(4):
            value = state[f, i] - HALF * total[i]
            mid[f, i] = value
            speed_z.append(parts(velocity[2, i] * value))
        edge = matmul(jnp.concatenate(speed_z, axis=0), weights)
        for i in range(4):
            pack = jnp.where(group == 4 * f + i, edge[64 * i : 64 * i + 64], pack)
    exchanged[pl.ds(0, 64), :] = pack
    edge = pl.ds(384, 32)
    upper = jnp.bitwise_and(group[:32], 3) >= 2
    folded = jnp.where(upper, high[edge, :], low[edge, :])
    exchanged[pl.ds(64, 32), :] = folded
    exchanged[pl.ds(96, 32), :] = pltpu.roll(folded, 64, 1)


def advance_kernel(
    state, velocity, mid, low, high, deposit, advanced, edge_speed, pads
):
    weights = twice(circulant())
    for f in range(3):
        for i, total, _ in inner_differences(lambda i: mid[f, i], velocity, pads, f, weights):
            value = state[f, i] - FULL * total
            if f > 0:
                value = value + deposit[f - 1, pl.ds(64 * i, 64), :]
            advanced[f, i] = value
        for (near, far, sign), side, start in zip(SIDES, (low, high), (0, 416)):
            here = velocity[0, near] * state[f, near]
            behind = velocity[0, far] * state[f, far]
            step = sign * HALF
            speed, speed_far = (side[pl.ds(start + 64 * (6 + k), 64), :] for k in range(2))
            close, remote = (side[pl.ds(start + 64 * (2 * f + k), 64), :] for k in range(2))
            close = close + step * (speed * (8.0 * here - behind))
            remote = remote - step * (speed_far * here)
            advanced[f, near] += (-FULL * sign) * (8.0 * close - remote)
            advanced[f, far] += (FULL * sign) * close
    weights = twice(spreading())
    plane = jnp.bitwise_and(groups(), 3)
    pack = jnp.zeros((64, 128), F32)
    for (near, far, _), side, start in zip(SIDES, (low, high), (0, 416)):
        for k, number in enumerate((near, far)):
            edge = matmul(parts(side[pl.ds(start + 64 * (6 + k), 64), :]), weights)
            pack = jnp.where(plane == number, edge, pack)
    edge_speed[...] = pack


def finish_kernel(
    advanced, edge_speed, sent, from_other, density_out, energy_out, lepton_out, result, sems
):
    lane = lanes()
    own, side = pl.ds(0, 64), pl.ds(64, 64)
    correction = edge_correction(from_other[own, :], sent[own, :], lane)
    moved = edge_correction(from_other[side, :], sent[side, :], lane)
    moved = HALF * (edge_speed[...] * moved)
    before, after = pltpu.roll(moved, 4, 1), pltpu.roll(moved, 124, 1)
    plane = jnp.bitwise_and(groups(), 3)
    low = jnp.where(plane == 0, 8.0 * moved - after, -before)
    high = jnp.where(plane == 2, after, before - 8.0 * moved)
    correction = FULL * (correction + jnp.where(plane < 2, low, high))
    copies = []
    for f, out in enumerate((density_out, energy_out, lepton_out)):
        for i in range(4):
            result[f, i] = advanced[f, i] - unpack_z(correction, 4 * (4 * f + i), lane)
        copies.append(pltpu.make_async_copy(result.at[f], out, sems.at[f]))
        copies[f].start()
    for copy in copies:
        copy.wait()


def column(row):
    return jnp.transpose(jnp.broadcast_to(row, (128, 128)))


def load_matrices(weak, capture, both, rest):
    matrix = jnp.concatenate([weak[...], capture[...]], axis=1)
    high, low = split(matrix)
    both[...] = jnp.concatenate([high, high], axis=0)
    rest[...] = low


def newton(base, start, get_target, rows_of, both, rest, w_ref, c_ref, x_ref, t_ref, k_ref, a_ref, finish):
    blocks = CHUNK // BLOCK

    def products(b):
        x = x_ref[pl.ds(b * BLOCK, BLOCK), :]
        return matmul(x, both[...]) + matmul(x[:, :128], rest[...])

    def put(b, values):
        high, low = split(values)
        x_ref[pl.ds(b * BLOCK, BLOCK), :] = jnp.concatenate([high, low], axis=1)

    for b in range(blocks):
        put(b, rows_of(b))
    for b in range(blocks):
        at = pl.ds(b * BLOCK, BLOCK)
        here = pl.ds(base + b * BLOCK, BLOCK)
        product = products(b)
        rows = rows_of(b)
        rate_weak, rate_capture = w_ref[here, :], c_ref[here, :]
        alpha = rate_capture * rows[:, 0:1]
        target = rate_weak * product[:, :128] + alpha * product[:, 128:]
        target = get_target(b, rows, target)
        a_ref[at, :] = alpha
        k_ref[at, :] = rate_capture * product[:, 128:]
        t_ref[at, :] = target
        put(b, target)
        start(b, target)
    for sweep in range(SWEEPS):
        for b in range(blocks):
            at = pl.ds(b * BLOCK, BLOCK)
            here = pl.ds(base + b * BLOCK, BLOCK)
            product = products(b)
            before = finish.last[b]
            update = t_ref[at, :] + (
                w_ref[here, :] * product[:, :128]
                + a_ref[at, :] * product[:, 128:]
                + before * k_ref[at, :]
            )
            if sweep < SWEEPS - 1:
                put(b, update)
                start(b, update)
            else:
                finish(b, rows_of(b) + update)


class Finish:
    def __init__(self, write):
        self.last = {}
        self.write = write

    def keep(self, b, values):
        self.last[b] = values[:, 0:1]

    def __call__(self, b, values):
        self.write(b, values)


def network_kernel(
    count, state, cells, rows, weak, capture, mass, binding, charge,
    rows_out, deposit,
    table, both, rest, x_ref, t_ref, k_ref, a_ref, w_ref, c_ref, iterate, gain_both, gain_rest,
):
    load_matrices(weak, capture, both, rest)
    rho, eps, lam = (state[f].reshape(256, 128) for f in range(3))
    inverse = 1.0 / rho
    weak_high, weak_low = split(0.62 + 0.04 * rho + 0.05 * (lam * inverse))
    capture_high, capture_low = split(0.3 * jax.nn.sigmoid(eps * inverse))
    table[...] = jnp.concatenate([weak_high, weak_low, capture_high, capture_low], axis=1)
    gains = jnp.concatenate([column(binding[...]), column(charge[...])], axis=1)
    high, low = split(gains)
    gain_both[...] = jnp.concatenate([high, high], axis=0)
    gain_rest[...] = low
    rows_out[...] = jnp.zeros(rows_out.shape, F32)
    deposit[...] = jnp.zeros(deposit.shape, F32)
    lane = lanes(BLOCK)
    sublane = lax.broadcasted_iota(jnp.int32, (256, 128), 0)
    ones = jnp.ones((256, 128), BF16)

    def chunk(k, carry):
        base = k * CHUNK

        def place(b):
            return pl.ds(pl.multiple_of(base + b * BLOCK, BLOCK), BLOCK)

        def inside(b):
            return pl.ds(b * BLOCK, BLOCK)

        for b in range(CHUNK // BLOCK):
            cell = column(cells[pl.ds(k * (CHUNK // BLOCK) + b, 1), :])
            row_id = lax.shift_right_logical(cell, 7)
            hot = jnp.concatenate([row_id == lane, row_id == lane + 128], axis=1)
            picked = matmul(jnp.where(hot, 1.0, 0.0).astype(BF16), table[...])
            here = jnp.bitwise_and(cell, 127) == lane
            here = jnp.concatenate([here, here, here, here], axis=1)
            picked = jnp.where(here, picked, 0.0).astype(BF16)
            w_ref[inside(b), :] = matmul(picked[:, :256], ones)
            c_ref[inside(b), :] = matmul(picked[:, 256:], ones)

        def write_first(b, values):
            iterate[inside(b), :] = values

        def write_last(b, values):
            slot = base + b * BLOCK + lax.broadcasted_iota(jnp.int32, (BLOCK, 128), 0)
            occupied = slot < count[0, 0]
            rows_out[place(b), :] = jnp.where(occupied, values, 0.0)
            change = jnp.where(occupied, values - rows[place(b), :], 0.0)
            high, low = split(change)
            x_ref[inside(b), :] = jnp.concatenate([high, low], axis=1)

        finish = Finish(write_first)
        newton(
            0, finish.keep, lambda b, current, target: target, lambda b: rows[place(b), :],
            both, rest, w_ref, c_ref, x_ref, t_ref, k_ref, a_ref, finish,
        )
        finish = Finish(write_last)
        newton(
            0, finish.keep, lambda b, current, target: target - (current - rows[place(b), :]),
            lambda b: iterate[inside(b), :],
            both, rest, w_ref, c_ref, x_ref, t_ref, k_ref, a_ref, finish,
        )
        hots, values = [], []
        for b in range(CHUNK // BLOCK):
            number = pl.ds(k * (CHUNK // BLOCK) + b, 1)
            cell = cells[number, :]
            hot = lax.shift_right_logical(cell, 7) == sublane
            hots.append(jnp.where(hot, 1.0, 0.0).astype(BF16))
            x = x_ref[inside(b), :]
            gain = matmul(x, gain_both[...]) + matmul(x[:, :128], gain_rest[...])
            weight = jnp.where(
                jnp.bitwise_and(column(cell), 127) == lane, column(mass[number, :]), 0.0
            )
            gain = gain * jnp.concatenate([weight, weight], axis=1)
            high, low = split(gain)
            values.append(jnp.concatenate([high, low], axis=1))
        sums = matmul(jnp.concatenate(hots, axis=1), jnp.concatenate(values, axis=0))
        deposit[0] += sums[:, :128] + sums[:, 256:384]
        deposit[1] += sums[:, 128:256] + sums[:, 384:]
        return carry

    lax.fori_loop(0, (count[0, 0] + CHUNK - 1) // CHUNK, chunk, 0)


VMEM = pl.BlockSpec(memory_space=pltpu.VMEM)
SMEM = pl.BlockSpec(memory_space=pltpu.SMEM)
HBM = pl.BlockSpec(memory_space=pltpu.HBM)


def call(kernel, name, outs, args, scratch=(), flops=0, first=(), out=VMEM):
    args = [
        pltpu.with_memory_space_constraint(a, pltpu.HBM) if s is HBM else a
        for a, s in zip(args, list(first) + [None] * len(args))
    ]
    moved = sum(a.size * 4 for a in args) + sum(4 * math.prod(o) for o in outs)
    return pl.pallas_call(
        kernel,
        name=name,
        out_shape=[jax.ShapeDtypeStruct(o, F32) for o in outs],
        in_specs=list(first) + [VMEM] * (len(args) - len(first)),
        out_specs=[out] * len(outs),
        scratch_shapes=list(scratch),
        compiler_params=pltpu.CompilerParams(vmem_limit_bytes=24 * 2**20),
        cost_estimate=pl.CostEstimate(flops=flops, bytes_accessed=moved, transcendentals=0),
    )(*args)


def swap_halves(packed):
    halves = lax.axis_size("grp")
    return lax.ppermute(packed, "grp", [(i, (i + 1) % halves) for i in range(halves)])


def send(message, step):
    count = lax.axis_size("brick")
    return lax.ppermute(message, "brick", [(i, (i + step) % count) for i in range(count)])


def on_device(
    density,
    energy_field,
    lepton_field,
    velocity,
    abundance,
    tracer_mass,
    tracer_cell,
    tracer_count,
    weak_rates,
    capture_rates,
    binding,
    charge_ratio,
):
    fields = (density, energy_field, lepton_field)
    whole, tile = (3, 4, 64, 128), (64, 128)
    pads = pltpu.VMEM((12, 80, 128), F32)
    planes = pltpu.VMEM((4, 64, 128), F32)
    state, speeds, partial, low_first, low_second, high, packed = call(
        edges_kernel, "edges",
        [whole, whole, whole, (416, 128), (512, 128), (928, 128), tile], (*fields, velocity),
        [pads, pltpu.VMEM(whole, F32), pltpu.SemaphoreType.DMA((4,))], 0, [HBM] * 4,
    )
    low_first = send(low_first, 1)
    low_second = send(low_second, 1)
    high = send(high, -1)

    rows = pltpu.VMEM((CHUNK, 128), F32)
    matrices = [pltpu.VMEM((256, 256), BF16), pltpu.VMEM((128, 256), BF16)]
    finished, deposit = call(
        network_kernel, "network", [(1024, 128), (2, 256, 128)],
        (
            tracer_count, state, tracer_cell.reshape(8, 128), abundance.reshape(1024, 128),
            weak_rates, capture_rates, tracer_mass.reshape(8, 128),
            binding.reshape(1, 128), charge_ratio.reshape(1, 128),
        ),
        [pltpu.VMEM((256, 512), BF16), *matrices, pltpu.VMEM((CHUNK, 256), BF16)]
        + [rows] * 6 + matrices,
        6 * 2 * 1024 * 128 * 256 * 18, [SMEM],
    )
    packed, deposit = lax.optimization_barrier((packed, deposit))
    from_other = swap_halves(packed)
    mid, sent = call(
        midpoint_kernel, "midpoint", [whole, (128, 128)],
        (state, speeds, partial, low_first, high, packed, from_other, deposit), [planes],
    )
    from_other = swap_halves(sent)
    advanced, edge_speed = call(
        advance_kernel, "advance", [whole, tile],
        (state, speeds, mid, low_second, high, deposit), [pads],
    )
    outs = call(
        finish_kernel, "finish", [(4, 64, 128)] * 3, (advanced, edge_speed, sent, from_other),
        [pltpu.VMEM(whole, F32), pltpu.SemaphoreType.DMA((3,))], 0, (), pl.BlockSpec(memory_space=pl.ANY),
    )
    return (*outs, finished[None, None])


def solution(mesh):
    return jax.shard_map(
        on_device,
        mesh=mesh,
        in_specs=(
            P("brick", None, "grp"),
            P("brick", None, "grp"),
            P("brick", None, "grp"),
            P(None, "brick", None, "grp"),
            P("grp", "brick", None, None),
            P("grp", "brick", None),
            P("grp", "brick", None),
            P("grp", "brick"),
            P(),
            P(),
            P(),
            P(),
        ),
        out_specs=(
            P("brick", None, "grp"),
            P("brick", None, "grp"),
            P("brick", None, "grp"),
            P("grp", "brick", None, None),
        ),
        check_vma=False,
    )
```

```python
import math

import jax
import jax.numpy as jnp
from jax import lax
from jax.experimental import pallas as pl
from jax.experimental.pallas import tpu as pltpu
from jax.sharding import PartitionSpec as P

SWEEPS = 8
CHUNK = 512
BLOCK = 128
COURANT = 0.8
HALF = 0.5 * COURANT / 12.0
FULL = COURANT / 12.0
F32 = jnp.float32
BF16 = jnp.bfloat16


def split(values):
    high = values.astype(BF16)
    return high, (values - high.astype(F32)).astype(BF16)


def matmul(a, b):
    return lax.dot_general(a, b, (((1,), (0,)), ((), ())), preferred_element_type=F32)


def lanes(rows=64):
    return lax.broadcasted_iota(jnp.int32, (rows, 128), 1)


def groups():
    return lax.shift_right_logical(lanes(), 2)


def spreading():
    row = lax.broadcasted_iota(jnp.int32, (128, 128), 0)
    source = jnp.bitwise_and(126 + jnp.bitwise_and(lanes(128), 3), 127)
    return jnp.where(row == source, 1.0, 0.0)


def circulant():
    row = lax.broadcasted_iota(jnp.int32, (128, 128), 0)
    offset = jnp.bitwise_and(row - lanes(128), 127)
    near = jnp.where(offset == 1, 8.0, jnp.where(offset == 127, -8.0, 0.0))
    return jnp.where(offset == 2, -1.0, jnp.where(offset == 126, 1.0, near))


def twice(matrix):
    matrix = matrix.astype(BF16)
    return jnp.concatenate([matrix, matrix], axis=0)


def parts(values):
    high, low = split(values)
    return jnp.concatenate([high, low], axis=1)


def unpack_z(packed, first, lane):
    moved = pltpu.roll(packed, (126 - first) % 128, 1)
    return jnp.where(jnp.logical_or(lane < 2, lane >= 126), moved, 0.0)


def edge_correction(other, own, lane):
    lack = other - own
    place = jnp.bitwise_and(lane, 3)
    far = jnp.where(place < 2, -pltpu.roll(lack, 126, 1), pltpu.roll(lack, 2, 1))
    near = jnp.where(place == 1, pltpu.roll(lack, 127, 1), 0.0)
    near = near - jnp.where(place == 2, pltpu.roll(lack, 1, 1), 0.0)
    return far + 8.0 * near


def along_y(tile, pad):
    pad[pl.ds(8, 64), :] = tile
    pad[pl.ds(0, 8), :] = tile[56:]
    pad[pl.ds(72, 8), :] = tile[:8]
    return 8.0 * (pad[pl.ds(9, 64), :] - pad[pl.ds(7, 64), :]) - (
        pad[pl.ds(10, 64), :] - pad[pl.ds(6, 64), :]
    )


def inner_differences(get, velocity, pads, f, weights):
    speed_z = [parts(velocity[2, i] * get(i)) for i in range(4)]
    along_z = matmul(jnp.concatenate(speed_z, axis=0), weights)
    for i in range(4):
        plane = [velocity[0, j] * get(j) for j in range(4) if 0 < abs(j - i) < 3]
        if i == 0:
            total = 8.0 * plane[0] - plane[1]
        elif i == 1:
            total = 8.0 * (plane[1] - plane[0]) - plane[2]
        elif i == 2:
            total = 8.0 * (plane[2] - plane[1]) + plane[0]
        else:
            total = plane[0] - 8.0 * plane[1]
        total = total + along_y(velocity[1, i] * get(i), pads.at[4 * f + i])
        here = along_z[64 * i : 64 * i + 64]
        yield i, total + here[:, :128], here[:, 128:]


SIDES = ((0, 1, -1.0), (3, 2, 1.0))


def rows_of_tile(number):
    return pl.ds(64 * number, 64)


def fold(folded, edge, place, group):
    folded = jnp.where(group == place, edge[:32], folded)
    return jnp.where(group == place + 16, edge[32:], folded)


def write_message(state, velocity, partial, planes, early, late):
    for k, plane in enumerate(planes):
        speed = velocity[0, plane]
        late[rows_of_tile(6 + k), :] = speed
        for f in range(3):
            value = state[f, plane]
            early[rows_of_tile(2 * f + k), :] = speed * value
            late[rows_of_tile(2 * f + k), :] = speed * (value - HALF * partial[f, plane])


def edges_kernel(
    density, energy, lepton, speeds,
    state, velocity, partial, low_first, low_second, folded, packed,
    pads, sems,
):
    wait_speeds = pltpu.make_async_copy(speeds, velocity, sems.at[3])
    wait_speeds.start()
    copies = [
        pltpu.make_async_copy(ref, state.at[f], sems.at[f])
        for f, ref in enumerate((density, energy, lepton))
    ]
    for copy in copies:
        copy.start()
    weights = twice(jnp.concatenate([circulant(), spreading()], axis=1))
    group = groups()
    pack = jnp.zeros((64, 128), F32)
    up = down = jnp.zeros((32, 128), F32)
    wait_speeds.wait()
    for f in range(3):
        copies[f].wait()
        for i, total, edge in inner_differences(
            lambda i: state[f, i], velocity, pads, f, weights
        ):
            partial[f, i] = total
            pack = jnp.where(group == 4 * f + i, edge, pack)
            if i < 2:
                down = fold(down, edge, 4 * f + 3 - i, group[:32])
            else:
                up = fold(up, edge, 4 * f + 3 - i, group[:32])
    packed[...] = pack
    folded[...] = down
    low_first[pl.ds(384, 32), :] = up
    write_message(state, velocity, partial, (3, 2), low_first, low_second)


def backward_kernel(state, velocity, partial, folded, packed, high_first, high_second, copied):
    copied[...] = packed[...]
    high_first[pl.ds(384, 32), :] = folded[...]
    write_message(state, velocity, partial, (0, 1), high_first, high_second)


def midpoint_kernel(
    state, velocity, partial, low, high, packed, from_other, deposit, mid, exchanged, total
):
    lane = lanes()
    correction = edge_correction(from_other[...], packed[...], lane)
    group = groups()
    weights = twice(spreading())
    pack = jnp.zeros((64, 128), F32)
    for f in range(3):
        for i in range(4):
            total[i] = partial[f, i] + unpack_z(correction, 4 * (4 * f + i), lane)
        for (near, far, sign), side in zip(SIDES, (low, high)):
            close = side[rows_of_tile(2 * f), :]
            total[near] += sign * (8.0 * close - side[rows_of_tile(2 * f + 1), :])
            total[far] += -sign * close
        speed_z = []
        for i in range(4):
            value = state[f, i] - HALF * total[i]
            mid[f, i] = value
            speed_z.append(parts(velocity[2, i] * value))
        edge = matmul(jnp.concatenate(speed_z, axis=0), weights)
        for i in range(4):
            pack = jnp.where(group == 4 * f + i, edge[64 * i : 64 * i + 64], pack)
    exchanged[pl.ds(0, 64), :] = pack
    edge = pl.ds(384, 32)
    upper = jnp.bitwise_and(group[:32], 3) >= 2
    folded = jnp.where(upper, high[edge, :], low[edge, :])
    exchanged[pl.ds(64, 32), :] = folded
    exchanged[pl.ds(96, 32), :] = pltpu.roll(folded, 64, 1)


def advance_kernel(
    state, velocity, mid, low, high, deposit, advanced, edge_speed, pads
):
    weights = twice(circulant())
    for f in range(3):
        for i, total, _ in inner_differences(lambda i: mid[f, i], velocity, pads, f, weights):
            value = state[f, i] - FULL * total
            if f > 0:
                value = value + deposit[f - 1, pl.ds(64 * i, 64), :]
            advanced[f, i] = value
        for (near, far, sign), side in zip(SIDES, (low, high)):
            here = velocity[0, near] * state[f, near]
            behind = velocity[0, far] * state[f, far]
            step = sign * HALF
            speed, speed_far = (side[rows_of_tile(6 + k), :] for k in range(2))
            close, remote = (side[rows_of_tile(2 * f + k), :] for k in range(2))
            close = close + step * (speed * (8.0 * here - behind))
            remote = remote - step * (speed_far * here)
            advanced[f, near] += (-FULL * sign) * (8.0 * close - remote)
            advanced[f, far] += (FULL * sign) * close
    weights = twice(spreading())
    plane = jnp.bitwise_and(groups(), 3)
    pack = jnp.zeros((64, 128), F32)
    for (near, far, _), side in zip(SIDES, (low, high)):
        for k, number in enumerate((near, far)):
            edge = matmul(parts(side[rows_of_tile(6 + k), :]), weights)
            pack = jnp.where(plane == number, edge, pack)
    edge_speed[...] = pack


def finish_kernel(
    advanced, edge_speed, sent, from_other, density_out, energy_out, lepton_out, result, sems
):
    lane = lanes()
    own, side = pl.ds(0, 64), pl.ds(64, 64)
    correction = edge_correction(from_other[own, :], sent[own, :], lane)
    moved = edge_correction(from_other[side, :], sent[side, :], lane)
    moved = HALF * (edge_speed[...] * moved)
    before, after = pltpu.roll(moved, 4, 1), pltpu.roll(moved, 124, 1)
    plane = jnp.bitwise_and(groups(), 3)
    low = jnp.where(plane == 0, 8.0 * moved - after, -before)
    high = jnp.where(plane == 2, after, before - 8.0 * moved)
    correction = FULL * (correction + jnp.where(plane < 2, low, high))
    copies = []
    for f, out in enumerate((density_out, energy_out, lepton_out)):
        for i in range(4):
            result[f, i] = advanced[f, i] - unpack_z(correction, 4 * (4 * f + i), lane)
        copies.append(pltpu.make_async_copy(result.at[f], out, sems.at[f]))
        copies[f].start()
    for copy in copies:
        copy.wait()


def column(row):
    return jnp.transpose(jnp.broadcast_to(row, (128, 128)))


def load_matrices(weak, capture, both, rest):
    matrix = jnp.concatenate([weak[...], capture[...]], axis=1)
    high, low = split(matrix)
    both[...] = jnp.concatenate([high, high], axis=0)
    rest[...] = low


def newton(base, start, get_target, rows_of, both, rest, w_ref, c_ref, x_ref, t_ref, k_ref, a_ref, finish):
    blocks = CHUNK // BLOCK

    def products(b):
        x = x_ref[pl.ds(b * BLOCK, BLOCK), :]
        return matmul(x, both[...]) + matmul(x[:, :128], rest[...])

    def put(b, values):
        high, low = split(values)
        x_ref[pl.ds(b * BLOCK, BLOCK), :] = jnp.concatenate([high, low], axis=1)

    for b in range(blocks):
        put(b, rows_of(b))
    for b in range(blocks):
        at = pl.ds(b * BLOCK, BLOCK)
        here = pl.ds(base + b * BLOCK, BLOCK)
        product = products(b)
        rows = rows_of(b)
        rate_weak, rate_capture = w_ref[here, :], c_ref[here, :]
        alpha = rate_capture * rows[:, 0:1]
        target = rate_weak * product[:, :128] + alpha * product[:, 128:]
        target = get_target(b, rows, target)
        a_ref[at, :] = alpha
        k_ref[at, :] = rate_capture * product[:, 128:]
        t_ref[at, :] = target
        put(b, target)
        start(b, target)
    for sweep in range(SWEEPS):
        for b in range(blocks):
            at = pl.ds(b * BLOCK, BLOCK)
            here = pl.ds(base + b * BLOCK, BLOCK)
            product = products(b)
            before = finish.last[b]
            update = t_ref[at, :] + (
                w_ref[here, :] * product[:, :128]
                + a_ref[at, :] * product[:, 128:]
                + before * k_ref[at, :]
            )
            if sweep < SWEEPS - 1:
                put(b, update)
                start(b, update)
            else:
                finish(b, rows_of(b) + update)


class Finish:
    def __init__(self, write):
        self.last = {}
        self.write = write

    def keep(self, b, values):
        self.last[b] = values[:, 0:1]

    def __call__(self, b, values):
        self.write(b, values)


def network_kernel(
    count, state, cells, rows, weak, capture, mass, binding, charge,
    rows_out, deposit,
    table, both, rest, x_ref, t_ref, k_ref, a_ref, w_ref, c_ref, iterate, gain_both, gain_rest,
):
    load_matrices(weak, capture, both, rest)
    rho, eps, lam = (state[f].reshape(256, 128) for f in range(3))
    inverse = 1.0 / rho
    weak_high, weak_low = split(0.62 + 0.04 * rho + 0.05 * (lam * inverse))
    capture_high, capture_low = split(0.3 * jax.nn.sigmoid(eps * inverse))
    table[...] = jnp.concatenate([weak_high, weak_low, capture_high, capture_low], axis=1)
    gains = jnp.concatenate([column(binding[...]), column(charge[...])], axis=1)
    high, low = split(gains)
    gain_both[...] = jnp.concatenate([high, high], axis=0)
    gain_rest[...] = low
    rows_out[...] = jnp.zeros(rows_out.shape, F32)
    deposit[...] = jnp.zeros(deposit.shape, F32)
    lane = lanes(BLOCK)
    sublane = lax.broadcasted_iota(jnp.int32, (256, 128), 0)
    ones = jnp.ones((256, 128), BF16)

    def chunk(k, carry):
        base = k * CHUNK

        def place(b):
            return pl.ds(pl.multiple_of(base + b * BLOCK, BLOCK), BLOCK)

        def inside(b):
            return pl.ds(b * BLOCK, BLOCK)

        for b in range(CHUNK // BLOCK):
            cell = column(cells[pl.ds(k * (CHUNK // BLOCK) + b, 1), :])
            row_id = lax.shift_right_logical(cell, 7)
            hot = jnp.concatenate([row_id == lane, row_id == lane + 128], axis=1)
            picked = matmul(jnp.where(hot, 1.0, 0.0).astype(BF16), table[...])
            here = jnp.bitwise_and(cell, 127) == lane
            here = jnp.concatenate([here, here, here, here], axis=1)
            picked = jnp.where(here, picked, 0.0).astype(BF16)
            w_ref[inside(b), :] = matmul(picked[:, :256], ones)
            c_ref[inside(b), :] = matmul(picked[:, 256:], ones)

        def write_first(b, values):
            iterate[inside(b), :] = values

        def write_last(b, values):
            slot = base + b * BLOCK + lax.broadcasted_iota(jnp.int32, (BLOCK, 128), 0)
            occupied = slot < count[0, 0]
            rows_out[place(b), :] = jnp.where(occupied, values, 0.0)
            change = jnp.where(occupied, values - rows[place(b), :], 0.0)
            high, low = split(change)
            x_ref[inside(b), :] = jnp.concatenate([high, low], axis=1)

        finish = Finish(write_first)
        newton(
            0, finish.keep, lambda b, current, target: target, lambda b: rows[place(b), :],
            both, rest, w_ref, c_ref, x_ref, t_ref, k_ref, a_ref, finish,
        )
        finish = Finish(write_last)
        newton(
            0, finish.keep, lambda b, current, target: target - (current - rows[place(b), :]),
            lambda b: iterate[inside(b), :],
            both, rest, w_ref, c_ref, x_ref, t_ref, k_ref, a_ref, finish,
        )
        hots, values = [], []
        for b in range(CHUNK // BLOCK):
            number = pl.ds(k * (CHUNK // BLOCK) + b, 1)
            cell = cells[number, :]
            hot = lax.shift_right_logical(cell, 7) == sublane
            hots.append(jnp.where(hot, 1.0, 0.0).astype(BF16))
            x = x_ref[inside(b), :]
            gain = matmul(x, gain_both[...]) + matmul(x[:, :128], gain_rest[...])
            weight = jnp.where(
                jnp.bitwise_and(column(cell), 127) == lane, column(mass[number, :]), 0.0
            )
            gain = gain * jnp.concatenate([weight, weight], axis=1)
            high, low = split(gain)
            values.append(jnp.concatenate([high, low], axis=1))
        sums = matmul(jnp.concatenate(hots, axis=1), jnp.concatenate(values, axis=0))
        deposit[0] += sums[:, :128] + sums[:, 256:384]
        deposit[1] += sums[:, 128:256] + sums[:, 384:]
        return carry

    lax.fori_loop(0, (count[0, 0] + CHUNK - 1) // CHUNK, chunk, 0)


VMEM = pl.BlockSpec(memory_space=pltpu.VMEM)
SMEM = pl.BlockSpec(memory_space=pltpu.SMEM)
HBM = pl.BlockSpec(memory_space=pltpu.HBM)


def call(kernel, name, outs, args, scratch=(), flops=0, first=(), out=VMEM):
    args = [
        pltpu.with_memory_space_constraint(a, pltpu.HBM) if s is HBM else a
        for a, s in zip(args, list(first) + [None] * len(args))
    ]
    moved = sum(a.size * 4 for a in args) + sum(4 * math.prod(o) for o in outs)
    return pl.pallas_call(
        kernel,
        name=name,
        out_shape=[jax.ShapeDtypeStruct(o, F32) for o in outs],
        in_specs=list(first) + [VMEM] * (len(args) - len(first)),
        out_specs=[out] * len(outs),
        scratch_shapes=list(scratch),
        compiler_params=pltpu.CompilerParams(vmem_limit_bytes=24 * 2**20),
        cost_estimate=pl.CostEstimate(flops=flops, bytes_accessed=moved, transcendentals=0),
    )(*args)


def swap_halves(packed):
    halves = lax.axis_size("grp")
    return lax.ppermute(packed, "grp", [(i, (i + 1) % halves) for i in range(halves)])


def send(message, step):
    count = lax.axis_size("brick")
    return lax.ppermute(message, "brick", [(i, (i + step) % count) for i in range(count)])


def on_device(
    density,
    energy_field,
    lepton_field,
    velocity,
    abundance,
    tracer_mass,
    tracer_cell,
    tracer_count,
    weak_rates,
    capture_rates,
    binding,
    charge_ratio,
):
    fields = (density, energy_field, lepton_field)
    whole, tile = (3, 4, 64, 128), (64, 128)
    pads = pltpu.VMEM((12, 80, 128), F32)
    planes = pltpu.VMEM((4, 64, 128), F32)
    messages = [(416, 128), (512, 128)]
    state, speeds, partial, low_first, low_second, folded, packed = call(
        edges_kernel, "edges", [whole] * 3 + messages + [(32, 128), tile], (*fields, velocity),
        [pads, pltpu.SemaphoreType.DMA((4,))], 0, [HBM] * 4,
    )
    low_first = send(low_first, 1)
    low_second = send(low_second, 1)
    high_first, high_second, packed = call(
        backward_kernel, "backward", messages + [tile], (state, speeds, partial, folded, packed)
    )
    high_first = send(high_first, -1)
    high_second = send(high_second, -1)
    from_other = swap_halves(packed)

    rows = pltpu.VMEM((CHUNK, 128), F32)
    matrices = [pltpu.VMEM((256, 256), BF16), pltpu.VMEM((128, 256), BF16)]
    finished, deposit = call(
        network_kernel, "network", [(1024, 128), (2, 256, 128)],
        (
            tracer_count, state, tracer_cell.reshape(8, 128), abundance.reshape(1024, 128),
            weak_rates, capture_rates, tracer_mass.reshape(8, 128),
            binding.reshape(1, 128), charge_ratio.reshape(1, 128),
        ),
        [pltpu.VMEM((256, 512), BF16), *matrices, pltpu.VMEM((CHUNK, 256), BF16)]
        + [rows] * 6 + matrices,
        6 * 2 * 1024 * 128 * 256 * 18, [SMEM],
    )
    mid, sent = call(
        midpoint_kernel, "midpoint", [whole, (128, 128)],
        (state, speeds, partial, low_first, high_first, packed, from_other, deposit), [planes],
    )
    from_other = swap_halves(sent)
    advanced, edge_speed = call(
        advance_kernel, "advance", [whole, tile],
        (state, speeds, mid, low_second, high_second, deposit), [pads],
    )
    outs = call(
        finish_kernel, "finish", [(4, 64, 128)] * 3, (advanced, edge_speed, sent, from_other),
        [pltpu.VMEM(whole, F32), pltpu.SemaphoreType.DMA((3,))], 0, (), pl.BlockSpec(memory_space=pl.ANY),
    )
    return (*outs, finished[None, None])


def solution(mesh):
    return jax.shard_map(
        on_device,
        mesh=mesh,
        in_specs=(
            P("brick", None, "grp"),
            P("brick", None, "grp"),
            P("brick", None, "grp"),
            P(None, "brick", None, "grp"),
            P("grp", "brick", None, None),
            P("grp", "brick", None),
            P("grp", "brick", None),
            P("grp", "brick"),
            P(),
            P(),
            P(),
            P(),
        ),
        out_specs=(
            P("brick", None, "grp"),
            P("brick", None, "grp"),
            P("brick", None, "grp"),
            P("grp", "brick", None, None),
        ),
        check_vma=False,
    )
```

```python
import math

import jax
import jax.numpy as jnp
from jax import lax
from jax.experimental import pallas as pl
from jax.experimental.pallas import tpu as pltpu
from jax.sharding import PartitionSpec as P

SWEEPS = 8
CHUNK = 512
BLOCK = 128
COURANT = 0.8
HALF = 0.5 * COURANT / 12.0
FULL = COURANT / 12.0
F32 = jnp.float32
BF16 = jnp.bfloat16


def split(values):
    high = values.astype(BF16)
    return high, (values - high.astype(F32)).astype(BF16)


def matmul(a, b):
    return lax.dot_general(a, b, (((1,), (0,)), ((), ())), preferred_element_type=F32)


def lanes(rows=64):
    return lax.broadcasted_iota(jnp.int32, (rows, 128), 1)


def groups():
    return lax.shift_right_logical(lanes(), 2)


def spreading():
    row = lax.broadcasted_iota(jnp.int32, (128, 128), 0)
    source = jnp.bitwise_and(126 + jnp.bitwise_and(lanes(128), 3), 127)
    return jnp.where(row == source, 1.0, 0.0)


def circulant():
    row = lax.broadcasted_iota(jnp.int32, (128, 128), 0)
    offset = jnp.bitwise_and(row - lanes(128), 127)
    near = jnp.where(offset == 1, 8.0, jnp.where(offset == 127, -8.0, 0.0))
    return jnp.where(offset == 2, -1.0, jnp.where(offset == 126, 1.0, near))


def twice(matrix):
    matrix = matrix.astype(BF16)
    return jnp.concatenate([matrix, matrix], axis=0)


def parts(values):
    high, low = split(values)
    return jnp.concatenate([high, low], axis=1)


def unpack_z(packed, first, lane):
    moved = pltpu.roll(packed, (126 - first) % 128, 1)
    return jnp.where(jnp.logical_or(lane < 2, lane >= 126), moved, 0.0)


def edge_correction(other, own, lane):
    lack = other - own
    place = jnp.bitwise_and(lane, 3)
    far = jnp.where(place < 2, -pltpu.roll(lack, 126, 1), pltpu.roll(lack, 2, 1))
    near = jnp.where(place == 1, pltpu.roll(lack, 127, 1), 0.0)
    near = near - jnp.where(place == 2, pltpu.roll(lack, 1, 1), 0.0)
    return far + 8.0 * near


def along_y(tile, pad):
    pad[pl.ds(8, 64), :] = tile
    pad[pl.ds(0, 8), :] = tile[56:]
    pad[pl.ds(72, 8), :] = tile[:8]
    return 8.0 * (pad[pl.ds(9, 64), :] - pad[pl.ds(7, 64), :]) - (
        pad[pl.ds(10, 64), :] - pad[pl.ds(6, 64), :]
    )


def inner_differences(get, velocity, pads, f, weights):
    speed_z = [parts(velocity[2, i] * get(i)) for i in range(4)]
    along_z = matmul(jnp.concatenate(speed_z, axis=0), weights)
    for i in range(4):
        plane = [velocity[0, j] * get(j) for j in range(4) if 0 < abs(j - i) < 3]
        if i == 0:
            total = 8.0 * plane[0] - plane[1]
        elif i == 1:
            total = 8.0 * (plane[1] - plane[0]) - plane[2]
        elif i == 2:
            total = 8.0 * (plane[2] - plane[1]) + plane[0]
        else:
            total = plane[0] - 8.0 * plane[1]
        total = total + along_y(velocity[1, i] * get(i), pads.at[4 * f + i])
        here = along_z[64 * i : 64 * i + 64]
        yield i, total + here[:, :128], here[:, 128:]


SIDES = ((0, 1, -1.0), (3, 2, 1.0))


def rows_of_tile(number):
    return pl.ds(64 * number, 64)


def fold(folded, edge, place, group):
    folded = jnp.where(group == place, edge[:32], folded)
    return jnp.where(group == place + 16, edge[32:], folded)


def write_message(state, velocity, partial, planes, early, late):
    for k, plane in enumerate(planes):
        speed = velocity[0, plane]
        late[rows_of_tile(6 + k), :] = speed
        for f in range(3):
            value = state[f, plane]
            early[rows_of_tile(2 * f + k), :] = speed * value
            late[rows_of_tile(2 * f + k), :] = speed * (value - HALF * partial[f, plane])


def edges_kernel(
    density, energy, lepton, speeds,
    state, velocity, partial, low_first, low_second, folded, packed,
    pads, sems,
):
    wait_speeds = pltpu.make_async_copy(speeds, velocity, sems.at[3])
    wait_speeds.start()
    copies = [
        pltpu.make_async_copy(ref, state.at[f], sems.at[f])
        for f, ref in enumerate((density, energy, lepton))
    ]
    for copy in copies:
        copy.start()
    weights = twice(jnp.concatenate([circulant(), spreading()], axis=1))
    group = groups()
    pack = jnp.zeros((64, 128), F32)
    up = down = jnp.zeros((32, 128), F32)
    wait_speeds.wait()
    for f in range(3):
        copies[f].wait()
        for i, total, edge in inner_differences(
            lambda i: state[f, i], velocity, pads, f, weights
        ):
            partial[f, i] = total
            pack = jnp.where(group == 4 * f + i, edge, pack)
            if i < 2:
                down = fold(down, edge, 4 * f + 3 - i, group[:32])
            else:
                up = fold(up, edge, 4 * f + 3 - i, group[:32])
    packed[...] = pack
    folded[...] = down
    low_first[pl.ds(384, 32), :] = up
    write_message(state, velocity, partial, (3, 2), low_first, low_second)


def backward_kernel(state, velocity, partial, folded, packed, high_first, high_second, copied):
    copied[...] = packed[...]
    high_first[pl.ds(384, 32), :] = folded[...]
    write_message(state, velocity, partial, (0, 1), high_first, high_second)


def midpoint_kernel(
    state, velocity, partial, low, high, packed, from_other, deposit, mid, exchanged, total
):
    lane = lanes()
    correction = edge_correction(from_other[...], packed[...], lane)
    group = groups()
    weights = twice(spreading())
    pack = jnp.zeros((64, 128), F32)
    for f in range(3):
        for i in range(4):
            total[i] = partial[f, i] + unpack_z(correction, 4 * (4 * f + i), lane)
        for (near, far, sign), side in zip(SIDES, (low, high)):
            close = side[rows_of_tile(2 * f), :]
            total[near] += sign * (8.0 * close - side[rows_of_tile(2 * f + 1), :])
            total[far] += -sign * close
        speed_z = []
        for i in range(4):
            value = state[f, i] - HALF * total[i]
            mid[f, i] = value
            speed_z.append(parts(velocity[2, i] * value))
        edge = matmul(jnp.concatenate(speed_z, axis=0), weights)
        for i in range(4):
            pack = jnp.where(group == 4 * f + i, edge[64 * i : 64 * i + 64], pack)
    exchanged[pl.ds(0, 64), :] = pack
    edge = pl.ds(384, 32)
    upper = jnp.bitwise_and(group[:32], 3) >= 2
    folded = jnp.where(upper, high[edge, :], low[edge, :])
    exchanged[pl.ds(64, 32), :] = folded
    exchanged[pl.ds(96, 32), :] = pltpu.roll(folded, 64, 1)


def advance_kernel(state, velocity, mid, deposit, advanced, pads):
    weights = twice(circulant())
    for f in range(3):
        for i, total, _ in inner_differences(lambda i: mid[f, i], velocity, pads, f, weights):
            value = state[f, i] - FULL * total
            if f > 0:
                value = value + deposit[f - 1, pl.ds(64 * i, 64), :]
            advanced[f, i] = value


def finish_kernel(
    state, velocity, advanced, low, high, sent, from_other,
    density_out, energy_out, lepton_out, result, sems,
):
    lane = lanes()
    plane = jnp.bitwise_and(groups(), 3)
    weights = twice(spreading())
    edge_speed = jnp.zeros((64, 128), F32)
    for (near, far, _), side in zip(SIDES, (low, high)):
        for k, number in enumerate((near, far)):
            edge = matmul(parts(side[rows_of_tile(6 + k), :]), weights)
            edge_speed = jnp.where(plane == number, edge, edge_speed)
    own, side = pl.ds(0, 64), pl.ds(64, 64)
    correction = edge_correction(from_other[own, :], sent[own, :], lane)
    moved = edge_correction(from_other[side, :], sent[side, :], lane)
    moved = HALF * (edge_speed * moved)
    before, after = pltpu.roll(moved, 4, 1), pltpu.roll(moved, 124, 1)
    below = jnp.where(plane == 0, 8.0 * moved - after, -before)
    above = jnp.where(plane == 2, after, before - 8.0 * moved)
    correction = FULL * (correction + jnp.where(plane < 2, below, above))
    copies = []
    for f, out in enumerate((density_out, energy_out, lepton_out)):
        for (near, far, sign), side in zip(SIDES, (low, high)):
            here = velocity[0, near] * state[f, near]
            behind = velocity[0, far] * state[f, far]
            step = sign * HALF
            speed, speed_far = (side[rows_of_tile(6 + k), :] for k in range(2))
            close, remote = (side[rows_of_tile(2 * f + k), :] for k in range(2))
            close = close + step * (speed * (8.0 * here - behind))
            remote = remote - step * (speed_far * here)
            for i, part in ((near, remote - 8.0 * close), (far, close)):
                packed = unpack_z(correction, 4 * (4 * f + i), lane)
                result[f, i] = advanced[f, i] + (FULL * sign) * part - packed
        copies.append(pltpu.make_async_copy(result.at[f], out, sems.at[f]))
        copies[f].start()
    for copy in copies:
        copy.wait()


def column(row):
    return jnp.transpose(jnp.broadcast_to(row, (128, 128)))


def load_matrices(weak, capture, both, rest):
    matrix = jnp.concatenate([weak[...], capture[...]], axis=1)
    high, low = split(matrix)
    both[...] = jnp.concatenate([high, high], axis=0)
    rest[...] = low


def newton(base, start, get_target, rows_of, both, rest, w_ref, c_ref, x_ref, t_ref, k_ref, a_ref, finish):
    blocks = CHUNK // BLOCK

    def products(b):
        x = x_ref[pl.ds(b * BLOCK, BLOCK), :]
        return matmul(x, both[...]) + matmul(x[:, :128], rest[...])

    def put(b, values):
        high, low = split(values)
        x_ref[pl.ds(b * BLOCK, BLOCK), :] = jnp.concatenate([high, low], axis=1)

    for b in range(blocks):
        put(b, rows_of(b))
    for b in range(blocks):
        at = pl.ds(b * BLOCK, BLOCK)
        here = pl.ds(base + b * BLOCK, BLOCK)
        product = products(b)
        rows = rows_of(b)
        rate_weak, rate_capture = w_ref[here, :], c_ref[here, :]
        alpha = rate_capture * rows[:, 0:1]
        target = rate_weak * product[:, :128] + alpha * product[:, 128:]
        target = get_target(b, rows, target)
        a_ref[at, :] = alpha
        k_ref[at, :] = rate_capture * product[:, 128:]
        t_ref[at, :] = target
        put(b, target)
        start(b, target)
    for sweep in range(SWEEPS):
        for b in range(blocks):
            at = pl.ds(b * BLOCK, BLOCK)
            here = pl.ds(base + b * BLOCK, BLOCK)
            product = products(b)
            before = finish.last[b]
            update = t_ref[at, :] + (
                w_ref[here, :] * product[:, :128]
                + a_ref[at, :] * product[:, 128:]
                + before * k_ref[at, :]
            )
            if sweep < SWEEPS - 1:
                put(b, update)
                start(b, update)
            else:
                finish(b, rows_of(b) + update)


class Finish:
    def __init__(self, write):
        self.last = {}
        self.write = write

    def keep(self, b, values):
        self.last[b] = values[:, 0:1]

    def __call__(self, b, values):
        self.write(b, values)


def network_kernel(
    count, state, cells, rows, weak, capture, mass, binding, charge,
    rows_out, deposit,
    table, both, rest, x_ref, t_ref, k_ref, a_ref, w_ref, c_ref, iterate, gain_both, gain_rest,
):
    load_matrices(weak, capture, both, rest)
    rho, eps, lam = (state[f].reshape(256, 128) for f in range(3))
    inverse = 1.0 / rho
    weak_high, weak_low = split(0.62 + 0.04 * rho + 0.05 * (lam * inverse))
    capture_high, capture_low = split(0.3 * jax.nn.sigmoid(eps * inverse))
    table[...] = jnp.concatenate([weak_high, weak_low, capture_high, capture_low], axis=1)
    gains = jnp.concatenate([column(binding[...]), column(charge[...])], axis=1)
    high, low = split(gains)
    gain_both[...] = jnp.concatenate([high, high], axis=0)
    gain_rest[...] = low
    rows_out[...] = jnp.zeros(rows_out.shape, F32)
    deposit[...] = jnp.zeros(deposit.shape, F32)
    lane = lanes(BLOCK)
    sublane = lax.broadcasted_iota(jnp.int32, (256, 128), 0)
    ones = jnp.ones((256, 128), BF16)

    def chunk(k, carry):
        base = k * CHUNK

        def place(b):
            return pl.ds(pl.multiple_of(base + b * BLOCK, BLOCK), BLOCK)

        def inside(b):
            return pl.ds(b * BLOCK, BLOCK)

        for b in range(CHUNK // BLOCK):
            cell = column(cells[pl.ds(k * (CHUNK // BLOCK) + b, 1), :])
            row_id = lax.shift_right_logical(cell, 7)
            hot = jnp.concatenate([row_id == lane, row_id == lane + 128], axis=1)
            picked = matmul(jnp.where(hot, 1.0, 0.0).astype(BF16), table[...])
            here = jnp.bitwise_and(cell, 127) == lane
            here = jnp.concatenate([here, here, here, here], axis=1)
            picked = jnp.where(here, picked, 0.0).astype(BF16)
            w_ref[inside(b), :] = matmul(picked[:, :256], ones)
            c_ref[inside(b), :] = matmul(picked[:, 256:], ones)

        def write_first(b, values):
            iterate[inside(b), :] = values

        def write_last(b, values):
            slot = base + b * BLOCK + lax.broadcasted_iota(jnp.int32, (BLOCK, 128), 0)
            occupied = slot < count[0, 0]
            rows_out[place(b), :] = jnp.where(occupied, values, 0.0)
            change = jnp.where(occupied, values - rows[place(b), :], 0.0)
            high, low = split(change)
            x_ref[inside(b), :] = jnp.concatenate([high, low], axis=1)

        finish = Finish(write_first)
        newton(
            0, finish.keep, lambda b, current, target: target, lambda b: rows[place(b), :],
            both, rest, w_ref, c_ref, x_ref, t_ref, k_ref, a_ref, finish,
        )
        finish = Finish(write_last)
        newton(
            0, finish.keep, lambda b, current, target: target - (current - rows[place(b), :]),
            lambda b: iterate[inside(b), :],
            both, rest, w_ref, c_ref, x_ref, t_ref, k_ref, a_ref, finish,
        )
        hots, values = [], []
        for b in range(CHUNK // BLOCK):
            number = pl.ds(k * (CHUNK // BLOCK) + b, 1)
            cell = cells[number, :]
            hot = lax.shift_right_logical(cell, 7) == sublane
            hots.append(jnp.where(hot, 1.0, 0.0).astype(BF16))
            x = x_ref[inside(b), :]
            gain = matmul(x, gain_both[...]) + matmul(x[:, :128], gain_rest[...])
            weight = jnp.where(
                jnp.bitwise_and(column(cell), 127) == lane, column(mass[number, :]), 0.0
            )
            gain = gain * jnp.concatenate([weight, weight], axis=1)
            high, low = split(gain)
            values.append(jnp.concatenate([high, low], axis=1))
        sums = matmul(jnp.concatenate(hots, axis=1), jnp.concatenate(values, axis=0))
        deposit[0] += sums[:, :128] + sums[:, 256:384]
        deposit[1] += sums[:, 128:256] + sums[:, 384:]
        return carry

    lax.fori_loop(0, (count[0, 0] + CHUNK - 1) // CHUNK, chunk, 0)


VMEM = pl.BlockSpec(memory_space=pltpu.VMEM)
SMEM = pl.BlockSpec(memory_space=pltpu.SMEM)
HBM = pl.BlockSpec(memory_space=pltpu.HBM)


def call(kernel, name, outs, args, scratch=(), flops=0, first=(), out=VMEM):
    args = [
        pltpu.with_memory_space_constraint(a, pltpu.HBM) if s is HBM else a
        for a, s in zip(args, list(first) + [None] * len(args))
    ]
    moved = sum(a.size * 4 for a in args) + sum(4 * math.prod(o) for o in outs)
    return pl.pallas_call(
        kernel,
        name=name,
        out_shape=[jax.ShapeDtypeStruct(o, F32) for o in outs],
        in_specs=list(first) + [VMEM] * (len(args) - len(first)),
        out_specs=[out] * len(outs),
        scratch_shapes=list(scratch),
        compiler_params=pltpu.CompilerParams(vmem_limit_bytes=24 * 2**20),
        cost_estimate=pl.CostEstimate(flops=flops, bytes_accessed=moved, transcendentals=0),
    )(*args)


def swap_halves(packed):
    halves = lax.axis_size("grp")
    return lax.ppermute(packed, "grp", [(i, (i + 1) % halves) for i in range(halves)])


def send(message, step):
    count = lax.axis_size("brick")
    return lax.ppermute(message, "brick", [(i, (i + step) % count) for i in range(count)])


def on_device(
    density,
    energy_field,
    lepton_field,
    velocity,
    abundance,
    tracer_mass,
    tracer_cell,
    tracer_count,
    weak_rates,
    capture_rates,
    binding,
    charge_ratio,
):
    fields = (density, energy_field, lepton_field)
    whole, tile = (3, 4, 64, 128), (64, 128)
    pads = pltpu.VMEM((12, 80, 128), F32)
    planes = pltpu.VMEM((4, 64, 128), F32)
    messages = [(416, 128), (512, 128)]
    state, speeds, partial, low_first, low_second, folded, packed = call(
        edges_kernel, "edges", [whole] * 3 + messages + [(32, 128), tile], (*fields, velocity),
        [pads, pltpu.SemaphoreType.DMA((4,))], 0, [HBM] * 4,
    )
    low_first = send(low_first, 1)
    low_second = send(low_second, 1)
    high_first, high_second, packed = call(
        backward_kernel, "backward", messages + [tile], (state, speeds, partial, folded, packed)
    )
    high_first = send(high_first, -1)
    high_second = send(high_second, -1)
    from_other = swap_halves(packed)

    rows = pltpu.VMEM((CHUNK, 128), F32)
    matrices = [pltpu.VMEM((256, 256), BF16), pltpu.VMEM((128, 256), BF16)]
    finished, deposit = call(
        network_kernel, "network", [(1024, 128), (2, 256, 128)],
        (
            tracer_count, state, tracer_cell.reshape(8, 128), abundance.reshape(1024, 128),
            weak_rates, capture_rates, tracer_mass.reshape(8, 128),
            binding.reshape(1, 128), charge_ratio.reshape(1, 128),
        ),
        [pltpu.VMEM((256, 512), BF16), *matrices, pltpu.VMEM((CHUNK, 256), BF16)]
        + [rows] * 6 + matrices,
        6 * 2 * 1024 * 128 * 256 * 18, [SMEM],
    )
    mid, sent = call(
        midpoint_kernel, "midpoint", [whole, (128, 128)],
        (state, speeds, partial, low_first, high_first, packed, from_other, deposit), [planes],
    )
    from_other = swap_halves(sent)
    (advanced,) = call(
        advance_kernel, "advance", [whole], (state, speeds, mid, deposit), [pads]
    )
    outs = call(
        finish_kernel, "finish", [(4, 64, 128)] * 3,
        (state, speeds, advanced, low_second, high_second, sent, from_other),
        [pltpu.VMEM(whole, F32), pltpu.SemaphoreType.DMA((3,))], 0, (), pl.BlockSpec(memory_space=pl.ANY),
    )
    return (*outs, finished[None, None])


def solution(mesh):
    return jax.shard_map(
        on_device,
        mesh=mesh,
        in_specs=(
            P("brick", None, "grp"),
            P("brick", None, "grp"),
            P("brick", None, "grp"),
            P(None, "brick", None, "grp"),
            P("grp", "brick", None, None),
            P("grp", "brick", None),
            P("grp", "brick", None),
            P("grp", "brick"),
            P(),
            P(),
            P(),
            P(),
        ),
        out_specs=(
            P("brick", None, "grp"),
            P("brick", None, "grp"),
            P("brick", None, "grp"),
            P("grp", "brick", None, None),
        ),
        check_vma=False,
    )
```

```python
import math

import jax
import jax.numpy as jnp
from jax import lax
from jax.experimental import pallas as pl
from jax.experimental.pallas import tpu as pltpu
from jax.sharding import PartitionSpec as P

SWEEPS = 8
CHUNK = 512
BLOCK = 128
COURANT = 0.8
HALF = 0.5 * COURANT / 12.0
FULL = COURANT / 12.0
F32 = jnp.float32
BF16 = jnp.bfloat16


def split(values):
    high = values.astype(BF16)
    return high, (values - high.astype(F32)).astype(BF16)


def matmul(a, b):
    return lax.dot_general(a, b, (((1,), (0,)), ((), ())), preferred_element_type=F32)


def lanes(rows=64):
    return lax.broadcasted_iota(jnp.int32, (rows, 128), 1)


def groups():
    return lax.shift_right_logical(lanes(), 2)


def spreading():
    row = lax.broadcasted_iota(jnp.int32, (128, 128), 0)
    source = jnp.bitwise_and(126 + jnp.bitwise_and(lanes(128), 3), 127)
    return jnp.where(row == source, 1.0, 0.0)


def circulant():
    row = lax.broadcasted_iota(jnp.int32, (128, 128), 0)
    offset = jnp.bitwise_and(row - lanes(128), 127)
    near = jnp.where(offset == 1, 8.0, jnp.where(offset == 127, -8.0, 0.0))
    return jnp.where(offset == 2, -1.0, jnp.where(offset == 126, 1.0, near))


def twice(matrix):
    matrix = matrix.astype(BF16)
    return jnp.concatenate([matrix, matrix], axis=0)


def parts(values):
    high, low = split(values)
    return jnp.concatenate([high, low], axis=1)


def unpack_z(packed, first, lane):
    moved = pltpu.roll(packed, (126 - first) % 128, 1)
    return jnp.where(jnp.logical_or(lane < 2, lane >= 126), moved, 0.0)


def edge_correction(other, own, lane):
    lack = other - own
    place = jnp.bitwise_and(lane, 3)
    far = jnp.where(place < 2, -pltpu.roll(lack, 126, 1), pltpu.roll(lack, 2, 1))
    near = jnp.where(place == 1, pltpu.roll(lack, 127, 1), 0.0)
    near = near - jnp.where(place == 2, pltpu.roll(lack, 1, 1), 0.0)
    return far + 8.0 * near


def along_y(tile, pad):
    pad[pl.ds(8, 64), :] = tile
    pad[pl.ds(0, 8), :] = tile[56:]
    pad[pl.ds(72, 8), :] = tile[:8]
    return 8.0 * (pad[pl.ds(9, 64), :] - pad[pl.ds(7, 64), :]) - (
        pad[pl.ds(10, 64), :] - pad[pl.ds(6, 64), :]
    )


def inner_differences(get, velocity, pads, f, weights):
    speed_z = [parts(velocity[2, i] * get(i)) for i in range(4)]
    along_z = matmul(jnp.concatenate(speed_z, axis=0), weights)
    for i in range(4):
        plane = [velocity[0, j] * get(j) for j in range(4) if 0 < abs(j - i) < 3]
        if i == 0:
            total = 8.0 * plane[0] - plane[1]
        elif i == 1:
            total = 8.0 * (plane[1] - plane[0]) - plane[2]
        elif i == 2:
            total = 8.0 * (plane[2] - plane[1]) + plane[0]
        else:
            total = plane[0] - 8.0 * plane[1]
        total = total + along_y(velocity[1, i] * get(i), pads.at[4 * f + i])
        here = along_z[64 * i : 64 * i + 64]
        yield i, total + here[:, :128], here[:, 128:]


SIDES = ((0, 1, -1.0), (3, 2, 1.0))


def rows_of_tile(number):
    return pl.ds(64 * number, 64)


def fold(folded, edge, place, group):
    folded = jnp.where(group == place, edge[:32], folded)
    return jnp.where(group == place + 16, edge[32:], folded)


def write_message(state, velocity, partial, planes, early, late):
    for k, plane in enumerate(planes):
        speed = velocity[0, plane]
        late[rows_of_tile(6 + k), :] = speed
        for f in range(3):
            value = state[f, plane]
            early[rows_of_tile(2 * f + k), :] = speed * value
            late[rows_of_tile(2 * f + k), :] = speed * (value - HALF * partial[f, plane])


def is_odd():
    return jnp.full((64, 128), jnp.bitwise_and(lax.axis_index("brick"), 1)) == 1


def chosen(odd, when_odd, when_even, start_odd=0, start_even=0):
    return lambda number: jnp.where(
        odd,
        when_odd[pl.ds(start_odd + 64 * number, 64), :],
        when_even[pl.ds(start_even + 64 * number, 64), :],
    )


def edges_kernel(
    density, energy, lepton, speeds,
    state, velocity, partial, low_first, low_second, folded, packed,
    pads, sems,
):
    wait_speeds = pltpu.make_async_copy(speeds, velocity, sems.at[3])
    wait_speeds.start()
    copies = [
        pltpu.make_async_copy(ref, state.at[f], sems.at[f])
        for f, ref in enumerate((density, energy, lepton))
    ]
    for copy in copies:
        copy.start()
    weights = twice(jnp.concatenate([circulant(), spreading()], axis=1))
    group = groups()
    pack = jnp.zeros((64, 128), F32)
    up = down = jnp.zeros((32, 128), F32)
    wait_speeds.wait()
    for f in range(3):
        copies[f].wait()
        for i, total, edge in inner_differences(
            lambda i: state[f, i], velocity, pads, f, weights
        ):
            partial[f, i] = total
            pack = jnp.where(group == 4 * f + i, edge, pack)
            if i < 2:
                down = fold(down, edge, 4 * f + 3 - i, group[:32])
            else:
                up = fold(up, edge, 4 * f + 3 - i, group[:32])
    packed[...] = pack
    folded[...] = down
    low_first[pl.ds(384, 32), :] = up
    write_message(state, velocity, partial, (3, 2), low_first, low_second)


def pair_kernel(state, velocity, partial, folded, low_first, pair):
    even = 1 - jnp.bitwise_and(lax.axis_index("brick"), 1)
    edge = pl.ds(384, 32)
    pair[edge, :] = jnp.where(is_odd()[:32], folded[...], low_first[edge, :])
    write_message(
        state, velocity, partial, (3 * even, 1 + even),
        pair.at[pl.ds(0, 416)], pair.at[pl.ds(416, 512)],
    )


def backward_kernel(
    state, velocity, partial, folded, pair, from_other, high_first, high_second
):
    high_first[pl.ds(384, 32), :] = folded[...]
    write_message(state, velocity, partial, (0, 1), high_first, high_second)


def midpoint_kernel(
    state, velocity, partial, forward, backward, pair, packed, from_other, deposit,
    mid, exchanged, total,
):
    lane = lanes()
    correction = edge_correction(from_other[...], packed[...], lane)
    group = groups()
    weights = twice(spreading())
    pack = jnp.zeros((64, 128), F32)
    odd = is_odd()
    low, high = chosen(odd, pair, forward), chosen(odd, backward, pair)
    for f in range(3):
        for i in range(4):
            total[i] = partial[f, i] + unpack_z(correction, 4 * (4 * f + i), lane)
        for (near, far, sign), side in zip(SIDES, (low, high)):
            close = side(2 * f)
            total[near] += sign * (8.0 * close - side(2 * f + 1))
            total[far] += -sign * close
        speed_z = []
        for i in range(4):
            value = state[f, i] - HALF * total[i]
            mid[f, i] = value
            speed_z.append(parts(velocity[2, i] * value))
        edge = matmul(jnp.concatenate(speed_z, axis=0), weights)
        for i in range(4):
            pack = jnp.where(group == 4 * f + i, edge[64 * i : 64 * i + 64], pack)
    exchanged[pl.ds(0, 64), :] = pack
    edge = pl.ds(384, 32)
    upper = jnp.bitwise_and(group[:32], 3) >= 2
    odd = odd[:32]
    high = jnp.where(odd, backward[edge, :], pair[edge, :])
    low = jnp.where(odd, pair[edge, :], forward[edge, :])
    folded = jnp.where(upper, high, low)
    exchanged[pl.ds(64, 32), :] = folded
    exchanged[pl.ds(96, 32), :] = pltpu.roll(folded, 64, 1)


def advance_kernel(state, velocity, mid, deposit, advanced, pads):
    weights = twice(circulant())
    for f in range(3):
        for i, total, _ in inner_differences(lambda i: mid[f, i], velocity, pads, f, weights):
            value = state[f, i] - FULL * total
            if f > 0:
                value = value + deposit[f - 1, pl.ds(64 * i, 64), :]
            advanced[f, i] = value


def finish_kernel(
    state, velocity, advanced, forward, backward, pair, sent, from_other,
    density_out, energy_out, lepton_out, result, sems,
):
    lane = lanes()
    plane = jnp.bitwise_and(groups(), 3)
    weights = twice(spreading())
    edge_speed = jnp.zeros((64, 128), F32)
    odd = is_odd()
    low, high = chosen(odd, pair, forward, 416, 0), chosen(odd, backward, pair, 0, 416)
    for (near, far, _), side in zip(SIDES, (low, high)):
        for k, number in enumerate((near, far)):
            edge = matmul(parts(side(6 + k)), weights)
            edge_speed = jnp.where(plane == number, edge, edge_speed)
    own, side = pl.ds(0, 64), pl.ds(64, 64)
    correction = edge_correction(from_other[own, :], sent[own, :], lane)
    moved = edge_correction(from_other[side, :], sent[side, :], lane)
    moved = HALF * (edge_speed * moved)
    before, after = pltpu.roll(moved, 4, 1), pltpu.roll(moved, 124, 1)
    below = jnp.where(plane == 0, 8.0 * moved - after, -before)
    above = jnp.where(plane == 2, after, before - 8.0 * moved)
    correction = FULL * (correction + jnp.where(plane < 2, below, above))
    copies = []
    for f, out in enumerate((density_out, energy_out, lepton_out)):
        for (near, far, sign), side in zip(SIDES, (low, high)):
            here = velocity[0, near] * state[f, near]
            behind = velocity[0, far] * state[f, far]
            step = sign * HALF
            speed, speed_far = side(6), side(7)
            close, remote = side(2 * f), side(2 * f + 1)
            close = close + step * (speed * (8.0 * here - behind))
            remote = remote - step * (speed_far * here)
            for i, part in ((near, remote - 8.0 * close), (far, close)):
                packed = unpack_z(correction, 4 * (4 * f + i), lane)
                result[f, i] = advanced[f, i] + (FULL * sign) * part - packed
        copies.append(pltpu.make_async_copy(result.at[f], out, sems.at[f]))
        copies[f].start()
    for copy in copies:
        copy.wait()


def column(row):
    return jnp.transpose(jnp.broadcast_to(row, (128, 128)))


def load_matrices(weak, capture, both, rest):
    matrix = jnp.concatenate([weak[...], capture[...]], axis=1)
    high, low = split(matrix)
    both[...] = jnp.concatenate([high, high], axis=0)
    rest[...] = low


def newton(base, start, get_target, rows_of, both, rest, w_ref, c_ref, x_ref, t_ref, k_ref, a_ref, finish):
    blocks = CHUNK // BLOCK

    def products(b):
        x = x_ref[pl.ds(b * BLOCK, BLOCK), :]
        return matmul(x, both[...]) + matmul(x[:, :128], rest[...])

    def put(b, values):
        high, low = split(values)
        x_ref[pl.ds(b * BLOCK, BLOCK), :] = jnp.concatenate([high, low], axis=1)

    for b in range(blocks):
        put(b, rows_of(b))
    for b in range(blocks):
        at = pl.ds(b * BLOCK, BLOCK)
        here = pl.ds(base + b * BLOCK, BLOCK)
        product = products(b)
        rows = rows_of(b)
        rate_weak, rate_capture = w_ref[here, :], c_ref[here, :]
        alpha = rate_capture * rows[:, 0:1]
        target = rate_weak * product[:, :128] + alpha * product[:, 128:]
        target = get_target(b, rows, target)
        a_ref[at, :] = alpha
        k_ref[at, :] = rate_capture * product[:, 128:]
        t_ref[at, :] = target
        put(b, target)
        start(b, target)
    for sweep in range(SWEEPS):
        for b in range(blocks):
            at = pl.ds(b * BLOCK, BLOCK)
            here = pl.ds(base + b * BLOCK, BLOCK)
            product = products(b)
            before = finish.last[b]
            update = t_ref[at, :] + (
                w_ref[here, :] * product[:, :128]
                + a_ref[at, :] * product[:, 128:]
                + before * k_ref[at, :]
            )
            if sweep < SWEEPS - 1:
                put(b, update)
                start(b, update)
            else:
                finish(b, rows_of(b) + update)


class Finish:
    def __init__(self, write):
        self.last = {}
        self.write = write

    def keep(self, b, values):
        self.last[b] = values[:, 0:1]

    def __call__(self, b, values):
        self.write(b, values)


def network_kernel(
    count, state, cells, rows, weak, capture, mass, binding, charge,
    rows_out, deposit,
    table, both, rest, x_ref, t_ref, k_ref, a_ref, w_ref, c_ref, iterate, gain_both, gain_rest,
):
    load_matrices(weak, capture, both, rest)
    rho, eps, lam = (state[f].reshape(256, 128) for f in range(3))
    inverse = 1.0 / rho
    weak_high, weak_low = split(0.62 + 0.04 * rho + 0.05 * (lam * inverse))
    capture_high, capture_low = split(0.3 * jax.nn.sigmoid(eps * inverse))
    table[...] = jnp.concatenate([weak_high, weak_low, capture_high, capture_low], axis=1)
    gains = jnp.concatenate([column(binding[...]), column(charge[...])], axis=1)
    high, low = split(gains)
    gain_both[...] = jnp.concatenate([high, high], axis=0)
    gain_rest[...] = low
    rows_out[...] = jnp.zeros(rows_out.shape, F32)
    deposit[...] = jnp.zeros(deposit.shape, F32)
    lane = lanes(BLOCK)
    sublane = lax.broadcasted_iota(jnp.int32, (256, 128), 0)
    ones = jnp.ones((256, 128), BF16)

    def chunk(k, carry):
        base = k * CHUNK

        def place(b):
            return pl.ds(pl.multiple_of(base + b * BLOCK, BLOCK), BLOCK)

        def inside(b):
            return pl.ds(b * BLOCK, BLOCK)

        for b in range(CHUNK // BLOCK):
            cell = column(cells[pl.ds(k * (CHUNK // BLOCK) + b, 1), :])
            row_id = lax.shift_right_logical(cell, 7)
            hot = jnp.concatenate([row_id == lane, row_id == lane + 128], axis=1)
            picked = matmul(jnp.where(hot, 1.0, 0.0).astype(BF16), table[...])
            here = jnp.bitwise_and(cell, 127) == lane
            here = jnp.concatenate([here, here, here, here], axis=1)
            picked = jnp.where(here, picked, 0.0).astype(BF16)
            w_ref[inside(b), :] = matmul(picked[:, :256], ones)
            c_ref[inside(b), :] = matmul(picked[:, 256:], ones)

        def write_first(b, values):
            iterate[inside(b), :] = values

        def write_last(b, values):
            slot = base + b * BLOCK + lax.broadcasted_iota(jnp.int32, (BLOCK, 128), 0)
            occupied = slot < count[0, 0]
            rows_out[place(b), :] = jnp.where(occupied, values, 0.0)
            change = jnp.where(occupied, values - rows[place(b), :], 0.0)
            high, low = split(change)
            x_ref[inside(b), :] = jnp.concatenate([high, low], axis=1)

        finish = Finish(write_first)
        newton(
            0, finish.keep, lambda b, current, target: target, lambda b: rows[place(b), :],
            both, rest, w_ref, c_ref, x_ref, t_ref, k_ref, a_ref, finish,
        )
        finish = Finish(write_last)
        newton(
            0, finish.keep, lambda b, current, target: target - (current - rows[place(b), :]),
            lambda b: iterate[inside(b), :],
            both, rest, w_ref, c_ref, x_ref, t_ref, k_ref, a_ref, finish,
        )
        hots, values = [], []
        for b in range(CHUNK // BLOCK):
            number = pl.ds(k * (CHUNK // BLOCK) + b, 1)
            cell = cells[number, :]
            hot = lax.shift_right_logical(cell, 7) == sublane
            hots.append(jnp.where(hot, 1.0, 0.0).astype(BF16))
            x = x_ref[inside(b), :]
            gain = matmul(x, gain_both[...]) + matmul(x[:, :128], gain_rest[...])
            weight = jnp.where(
                jnp.bitwise_and(column(cell), 127) == lane, column(mass[number, :]), 0.0
            )
            gain = gain * jnp.concatenate([weight, weight], axis=1)
            high, low = split(gain)
            values.append(jnp.concatenate([high, low], axis=1))
        sums = matmul(jnp.concatenate(hots, axis=1), jnp.concatenate(values, axis=0))
        deposit[0] += sums[:, :128] + sums[:, 256:384]
        deposit[1] += sums[:, 128:256] + sums[:, 384:]
        return carry

    lax.fori_loop(0, (count[0, 0] + CHUNK - 1) // CHUNK, chunk, 0)


VMEM = pl.BlockSpec(memory_space=pltpu.VMEM)
SMEM = pl.BlockSpec(memory_space=pltpu.SMEM)
HBM = pl.BlockSpec(memory_space=pltpu.HBM)


def call(kernel, name, outs, args, scratch=(), flops=0, first=(), out=VMEM):
    args = [
        pltpu.with_memory_space_constraint(a, pltpu.HBM) if s is HBM else a
        for a, s in zip(args, list(first) + [None] * len(args))
    ]
    moved = sum(a.size * 4 for a in args) + sum(4 * math.prod(o) for o in outs)
    return pl.pallas_call(
        kernel,
        name=name,
        out_shape=[jax.ShapeDtypeStruct(o, F32) for o in outs],
        in_specs=list(first) + [VMEM] * (len(args) - len(first)),
        out_specs=[out] * len(outs),
        scratch_shapes=list(scratch),
        compiler_params=pltpu.CompilerParams(vmem_limit_bytes=24 * 2**20),
        cost_estimate=pl.CostEstimate(flops=flops, bytes_accessed=moved, transcendentals=0),
    )(*args)


def swap_halves(packed):
    halves = lax.axis_size("grp")
    return lax.ppermute(packed, "grp", [(i, (i + 1) % halves) for i in range(halves)])


def send(message, step, kinds):
    count = lax.axis_size("brick")
    pairs = [(i, (i + step) % count) for i in range(count) if i % 2 in kinds]
    return lax.ppermute(message, "brick", pairs)


def swap_even_pairs(message):
    count = lax.axis_size("brick")
    return lax.ppermute(message, "brick", [(i, i ^ 1) for i in range(count)])


def on_device(
    density,
    energy_field,
    lepton_field,
    velocity,
    abundance,
    tracer_mass,
    tracer_cell,
    tracer_count,
    weak_rates,
    capture_rates,
    binding,
    charge_ratio,
):
    fields = (density, energy_field, lepton_field)
    whole, tile = (3, 4, 64, 128), (64, 128)
    pads = pltpu.VMEM((12, 80, 128), F32)
    planes = pltpu.VMEM((4, 64, 128), F32)
    messages = [(416, 128), (512, 128)]
    state, speeds, partial, low_first, low_second, folded, packed = call(
        edges_kernel, "edges", [whole] * 3 + messages + [(32, 128), tile], (*fields, velocity),
        [pads, pltpu.SemaphoreType.DMA((4,))], 0, [HBM] * 4,
    )
    (pair,) = call(
        pair_kernel, "pair", [(928, 128)], (state, speeds, partial, folded, low_first)
    )
    low_first = send(low_first, 1, (1,))
    low_second = send(low_second, 1, (1,))
    from_other = swap_halves(packed)
    high_first, high_second = call(
        backward_kernel, "backward", messages, (state, speeds, partial, folded, pair, from_other)
    )
    pair = swap_even_pairs(pair)
    high_first = send(high_first, -1, (0,))
    high_second = send(high_second, -1, (0,))

    rows = pltpu.VMEM((CHUNK, 128), F32)
    matrices = [pltpu.VMEM((256, 256), BF16), pltpu.VMEM((128, 256), BF16)]
    finished, deposit = call(
        network_kernel, "network", [(1024, 128), (2, 256, 128)],
        (
            tracer_count, state, tracer_cell.reshape(8, 128), abundance.reshape(1024, 128),
            weak_rates, capture_rates, tracer_mass.reshape(8, 128),
            binding.reshape(1, 128), charge_ratio.reshape(1, 128),
        ),
        [pltpu.VMEM((256, 512), BF16), *matrices, pltpu.VMEM((CHUNK, 256), BF16)]
        + [rows] * 6 + matrices,
        6 * 2 * 1024 * 128 * 256 * 18, [SMEM],
    )
    mid, sent = call(
        midpoint_kernel, "midpoint", [whole, (128, 128)],
        (state, speeds, partial, low_first, high_first, pair, packed, from_other, deposit), [planes],
    )
    from_other = swap_halves(sent)
    (advanced,) = call(
        advance_kernel, "advance", [whole], (state, speeds, mid, deposit), [pads]
    )
    outs = call(
        finish_kernel, "finish", [(4, 64, 128)] * 3,
        (state, speeds, advanced, low_second, high_second, pair, sent, from_other),
        [pltpu.VMEM(whole, F32), pltpu.SemaphoreType.DMA((3,))], 0, (), pl.BlockSpec(memory_space=pl.ANY),
    )
    return (*outs, finished[None, None])


def solution(mesh):
    return jax.shard_map(
        on_device,
        mesh=mesh,
        in_specs=(
            P("brick", None, "grp"),
            P("brick", None, "grp"),
            P("brick", None, "grp"),
            P(None, "brick", None, "grp"),
            P("grp", "brick", None, None),
            P("grp", "brick", None),
            P("grp", "brick", None),
            P("grp", "brick"),
            P(),
            P(),
            P(),
            P(),
        ),
        out_specs=(
            P("brick", None, "grp"),
            P("brick", None, "grp"),
            P("brick", None, "grp"),
            P("grp", "brick", None, None),
        ),
        check_vma=False,
    )
```

```python
import math

import jax
import jax.numpy as jnp
from jax import lax
from jax.experimental import pallas as pl
from jax.experimental.pallas import tpu as pltpu
from jax.sharding import PartitionSpec as P

SWEEPS = 8
CHUNK = 512
BLOCK = 128
COURANT = 0.8
HALF = 0.5 * COURANT / 12.0
FULL = COURANT / 12.0
F32 = jnp.float32
BF16 = jnp.bfloat16


def split(values):
    high = values.astype(BF16)
    return high, (values - high.astype(F32)).astype(BF16)


def matmul(a, b):
    return lax.dot_general(a, b, (((1,), (0,)), ((), ())), preferred_element_type=F32)


def lanes(rows=64):
    return lax.broadcasted_iota(jnp.int32, (rows, 128), 1)


def groups():
    return lax.shift_right_logical(lanes(), 2)


def spreading():
    row = lax.broadcasted_iota(jnp.int32, (128, 128), 0)
    source = jnp.bitwise_and(126 + jnp.bitwise_and(lanes(128), 3), 127)
    return jnp.where(row == source, 1.0, 0.0)


def circulant():
    row = lax.broadcasted_iota(jnp.int32, (128, 128), 0)
    offset = jnp.bitwise_and(row - lanes(128), 127)
    near = jnp.where(offset == 1, 8.0, jnp.where(offset == 127, -8.0, 0.0))
    return jnp.where(offset == 2, -1.0, jnp.where(offset == 126, 1.0, near))


def twice(matrix):
    matrix = matrix.astype(BF16)
    return jnp.concatenate([matrix, matrix], axis=0)


def parts(values):
    high, low = split(values)
    return jnp.concatenate([high, low], axis=1)


def unpack_z(packed, first, lane):
    moved = pltpu.roll(packed, (126 - first) % 128, 1)
    return jnp.where(jnp.logical_or(lane < 2, lane >= 126), moved, 0.0)


def edge_correction(other, own, lane):
    lack = other - own
    place = jnp.bitwise_and(lane, 3)
    far = jnp.where(place < 2, -pltpu.roll(lack, 126, 1), pltpu.roll(lack, 2, 1))
    near = jnp.where(place == 1, pltpu.roll(lack, 127, 1), 0.0)
    near = near - jnp.where(place == 2, pltpu.roll(lack, 1, 1), 0.0)
    return far + 8.0 * near


def along_y(tile, pad):
    pad[pl.ds(8, 64), :] = tile
    pad[pl.ds(0, 8), :] = tile[56:]
    pad[pl.ds(72, 8), :] = tile[:8]
    return 8.0 * (pad[pl.ds(9, 64), :] - pad[pl.ds(7, 64), :]) - (
        pad[pl.ds(10, 64), :] - pad[pl.ds(6, 64), :]
    )


def z_products(get, velocity, f, weights):
    speed_z = [parts(velocity[2, i] * get(i)) for i in range(4)]
    return matmul(jnp.concatenate(speed_z, axis=0), weights)


def xy_differences(get, velocity, pads, f):
    for i in range(4):
        plane = [velocity[0, j] * get(j) for j in range(4) if 0 < abs(j - i) < 3]
        if i == 0:
            total = 8.0 * plane[0] - plane[1]
        elif i == 1:
            total = 8.0 * (plane[1] - plane[0]) - plane[2]
        elif i == 2:
            total = 8.0 * (plane[2] - plane[1]) + plane[0]
        else:
            total = plane[0] - 8.0 * plane[1]
        yield i, total + along_y(velocity[1, i] * get(i), pads.at[4 * f + i])


SIDES = ((0, 1, -1.0), (3, 2, 1.0))


def rows_of_tile(number):
    return pl.ds(64 * number, 64)


def fold(folded, edge, place, group):
    folded = jnp.where(group == place, edge[:32], folded)
    return jnp.where(group == place + 16, edge[32:], folded)


def write_late(state, velocity, partial, planes, late):
    for k, plane in enumerate(planes):
        for f in range(3):
            late[rows_of_tile(2 * f + k), :] = velocity[0, plane] * (
                state[f, plane] - HALF * partial[f, plane]
            )


def edges_kernel(
    density, energy, lepton, speeds, state, velocity, slopes, low_first, folded, packed, sems
):
    wait_speeds = pltpu.make_async_copy(speeds, velocity, sems.at[3])
    wait_speeds.start()
    copies = [
        pltpu.make_async_copy(ref, state.at[f], sems.at[f])
        for f, ref in enumerate((density, energy, lepton))
    ]
    for copy in copies:
        copy.start()
    weights = twice(jnp.concatenate([circulant(), spreading()], axis=1))
    group = groups()
    pack = jnp.zeros((64, 128), F32)
    up = down = jnp.zeros((32, 128), F32)
    wait_speeds.wait()
    for f in range(3):
        copies[f].wait()
        product = z_products(lambda i: state[f, i], velocity, f, weights)
        for i in range(4):
            slopes[f, i] = product[64 * i : 64 * i + 64, :128]
            edge = product[64 * i : 64 * i + 64, 128:]
            pack = jnp.where(group == 4 * f + i, edge, pack)
            if i < 2:
                down = fold(down, edge, 4 * f + 3 - i, group[:32])
            else:
                up = fold(up, edge, 4 * f + 3 - i, group[:32])
                low_first[rows_of_tile(2 * f + 3 - i), :] = velocity[0, i] * state[f, i]
    packed[...] = pack
    folded[...] = down
    low_first[pl.ds(384, 32), :] = up
    for k in range(2):
        low_first[pl.ds(416 + 64 * k, 64), :] = velocity[0, 3 - k]


def messages_kernel(
    state, velocity, slopes, folded, packed,
    partial, low_second, high_first, high_second, copied,
    pads,
):
    for f in range(3):
        for i, total in xy_differences(lambda i: state[f, i], velocity, pads, f):
            partial[f, i] = total + slopes[f, i]
            if i < 2:
                high_first[rows_of_tile(2 * f + i), :] = velocity[0, i] * state[f, i]
    write_late(state, velocity, partial, (3, 2), low_second)
    write_late(state, velocity, partial, (0, 1), high_second)
    high_first[pl.ds(384, 32), :] = folded[...]
    for k in range(2):
        high_second[rows_of_tile(6 + k), :] = velocity[0, k]
    copied[pl.ds(0, 64), :] = packed[...]
    copied[pl.ds(64, 464), :] = jnp.zeros((464, 128), F32)


def midpoint_kernel(
    state, velocity, partial, low, high, packed, from_other, deposit, mid, exchanged, total
):
    lane = lanes()
    correction = edge_correction(from_other[pl.ds(0, 64), :], packed[...], lane)
    group = groups()
    weights = twice(spreading())
    pack = jnp.zeros((64, 128), F32)
    for f in range(3):
        for i in range(4):
            total[i] = partial[f, i] + unpack_z(correction, 4 * (4 * f + i), lane)
        for (near, far, sign), side in zip(SIDES, (low, high)):
            close = side[rows_of_tile(2 * f), :]
            total[near] += sign * (8.0 * close - side[rows_of_tile(2 * f + 1), :])
            total[far] += -sign * close
        speed_z = []
        for i in range(4):
            value = state[f, i] - HALF * total[i]
            mid[f, i] = value
            speed_z.append(parts(velocity[2, i] * value))
        edge = matmul(jnp.concatenate(speed_z, axis=0), weights)
        for i in range(4):
            pack = jnp.where(group == 4 * f + i, edge[64 * i : 64 * i + 64], pack)
    exchanged[pl.ds(0, 64), :] = pack
    edge = pl.ds(384, 32)
    upper = jnp.bitwise_and(group[:32], 3) >= 2
    folded = jnp.where(upper, high[edge, :], low[edge, :])
    exchanged[pl.ds(64, 32), :] = folded
    exchanged[pl.ds(96, 32), :] = pltpu.roll(folded, 64, 1)


def advance_kernel(state, velocity, mid, deposit, advanced, pads):
    weights = twice(circulant())
    for f in range(3):
        slopes = z_products(lambda i: mid[f, i], velocity, f, weights)
        for i, total in xy_differences(lambda i: mid[f, i], velocity, pads, f):
            value = state[f, i] - FULL * (total + slopes[64 * i : 64 * i + 64])
            if f > 0:
                value = value + deposit[f - 1, pl.ds(64 * i, 64), :]
            advanced[f, i] = value


def finish_kernel(
    state, velocity, advanced, low_first, low, high, sent, from_other,
    density_out, energy_out, lepton_out, result, sems,
):
    lane = lanes()
    plane = jnp.bitwise_and(groups(), 3)
    weights = twice(spreading())
    edge_speed = jnp.zeros((64, 128), F32)
    speeds = (
        [low_first[pl.ds(416 + 64 * k, 64), :] for k in range(2)],
        [high[rows_of_tile(6 + k), :] for k in range(2)],
    )
    for (near, far, _), pair in zip(SIDES, speeds):
        for number, values in zip((near, far), pair):
            edge = matmul(parts(values), weights)
            edge_speed = jnp.where(plane == number, edge, edge_speed)
    own, side = pl.ds(0, 64), pl.ds(64, 64)
    correction = edge_correction(from_other[own, :], sent[own, :], lane)
    moved = edge_correction(from_other[side, :], sent[side, :], lane)
    moved = HALF * (edge_speed * moved)
    before, after = pltpu.roll(moved, 4, 1), pltpu.roll(moved, 124, 1)
    below = jnp.where(plane == 0, 8.0 * moved - after, -before)
    above = jnp.where(plane == 2, after, before - 8.0 * moved)
    correction = FULL * (correction + jnp.where(plane < 2, below, above))
    copies = []
    for f, out in enumerate((density_out, energy_out, lepton_out)):
        for (near, far, sign), side, (speed, speed_far) in zip(SIDES, (low, high), speeds):
            here = velocity[0, near] * state[f, near]
            behind = velocity[0, far] * state[f, far]
            step = sign * HALF
            close, remote = (side[rows_of_tile(2 * f + k), :] for k in range(2))
            close = close + step * (speed * (8.0 * here - behind))
            remote = remote - step * (speed_far * here)
            for i, part in ((near, remote - 8.0 * close), (far, close)):
                packed = unpack_z(correction, 4 * (4 * f + i), lane)
                result[f, i] = advanced[f, i] + (FULL * sign) * part - packed
        copies.append(pltpu.make_async_copy(result.at[f], out, sems.at[f]))
        copies[f].start()
    for copy in copies:
        copy.wait()


def column(row):
    return jnp.transpose(jnp.broadcast_to(row, (128, 128)))


def load_matrices(weak, capture, both, rest):
    matrix = jnp.concatenate([weak[...], capture[...]], axis=1)
    high, low = split(matrix)
    both[...] = jnp.concatenate([high, high], axis=0)
    rest[...] = low


def newton(base, start, get_target, rows_of, both, rest, w_ref, c_ref, x_ref, t_ref, k_ref, a_ref, finish):
    blocks = CHUNK // BLOCK

    def products(b):
        x = x_ref[pl.ds(b * BLOCK, BLOCK), :]
        return matmul(x, both[...]) + matmul(x[:, :128], rest[...])

    def put(b, values):
        high, low = split(values)
        x_ref[pl.ds(b * BLOCK, BLOCK), :] = jnp.concatenate([high, low], axis=1)

    for b in range(blocks):
        put(b, rows_of(b))
    for b in range(blocks):
        at = pl.ds(b * BLOCK, BLOCK)
        here = pl.ds(base + b * BLOCK, BLOCK)
        product = products(b)
        rows = rows_of(b)
        rate_weak, rate_capture = w_ref[here, :], c_ref[here, :]
        alpha = rate_capture * rows[:, 0:1]
        target = rate_weak * product[:, :128] + alpha * product[:, 128:]
        target = get_target(b, rows, target)
        a_ref[at, :] = alpha
        k_ref[at, :] = rate_capture * product[:, 128:]
        t_ref[at, :] = target
        put(b, target)
        start(b, target)
    for sweep in range(SWEEPS):
        for b in range(blocks):
            at = pl.ds(b * BLOCK, BLOCK)
            here = pl.ds(base + b * BLOCK, BLOCK)
            product = products(b)
            before = finish.last[b]
            update = t_ref[at, :] + (
                w_ref[here, :] * product[:, :128]
                + a_ref[at, :] * product[:, 128:]
                + before * k_ref[at, :]
            )
            if sweep < SWEEPS - 1:
                put(b, update)
                start(b, update)
            else:
                finish(b, rows_of(b) + update)


class Finish:
    def __init__(self, write):
        self.last = {}
        self.write = write

    def keep(self, b, values):
        self.last[b] = values[:, 0:1]

    def __call__(self, b, values):
        self.write(b, values)


def network_kernel(
    count, state, cells, rows, weak, capture, mass, binding, charge,
    rows_out, deposit,
    table, both, rest, x_ref, t_ref, k_ref, a_ref, w_ref, c_ref, iterate, gain_both, gain_rest,
):
    load_matrices(weak, capture, both, rest)
    rho, eps, lam = (state[f].reshape(256, 128) for f in range(3))
    inverse = 1.0 / rho
    weak_high, weak_low = split(0.62 + 0.04 * rho + 0.05 * (lam * inverse))
    capture_high, capture_low = split(0.3 * jax.nn.sigmoid(eps * inverse))
    table[...] = jnp.concatenate([weak_high, weak_low, capture_high, capture_low], axis=1)
    gains = jnp.concatenate([column(binding[...]), column(charge[...])], axis=1)
    high, low = split(gains)
    gain_both[...] = jnp.concatenate([high, high], axis=0)
    gain_rest[...] = low
    rows_out[...] = jnp.zeros(rows_out.shape, F32)
    deposit[...] = jnp.zeros(deposit.shape, F32)
    lane = lanes(BLOCK)
    sublane = lax.broadcasted_iota(jnp.int32, (256, 128), 0)
    ones = jnp.ones((256, 128), BF16)

    def chunk(k, carry):
        base = k * CHUNK

        def place(b):
            return pl.ds(pl.multiple_of(base + b * BLOCK, BLOCK), BLOCK)

        def inside(b):
            return pl.ds(b * BLOCK, BLOCK)

        for b in range(CHUNK // BLOCK):
            cell = column(cells[pl.ds(k * (CHUNK // BLOCK) + b, 1), :])
            row_id = lax.shift_right_logical(cell, 7)
            hot = jnp.concatenate([row_id == lane, row_id == lane + 128], axis=1)
            picked = matmul(jnp.where(hot, 1.0, 0.0).astype(BF16), table[...])
            here = jnp.bitwise_and(cell, 127) == lane
            here = jnp.concatenate([here, here, here, here], axis=1)
            picked = jnp.where(here, picked, 0.0).astype(BF16)
            w_ref[inside(b), :] = matmul(picked[:, :256], ones)
            c_ref[inside(b), :] = matmul(picked[:, 256:], ones)

        def write_first(b, values):
            iterate[inside(b), :] = values

        def write_last(b, values):
            slot = base + b * BLOCK + lax.broadcasted_iota(jnp.int32, (BLOCK, 128), 0)
            occupied = slot < count[0, 0]
            rows_out[place(b), :] = jnp.where(occupied, values, 0.0)
            change = jnp.where(occupied, values - rows[place(b), :], 0.0)
            high, low = split(change)
            x_ref[inside(b), :] = jnp.concatenate([high, low], axis=1)

        finish = Finish(write_first)
        newton(
            0, finish.keep, lambda b, current, target: target, lambda b: rows[place(b), :],
            both, rest, w_ref, c_ref, x_ref, t_ref, k_ref, a_ref, finish,
        )
        finish = Finish(write_last)
        newton(
            0, finish.keep, lambda b, current, target: target - (current - rows[place(b), :]),
            lambda b: iterate[inside(b), :],
            both, rest, w_ref, c_ref, x_ref, t_ref, k_ref, a_ref, finish,
        )
        hots, values = [], []
        for b in range(CHUNK // BLOCK):
            number = pl.ds(k * (CHUNK // BLOCK) + b, 1)
            cell = cells[number, :]
            hot = lax.shift_right_logical(cell, 7) == sublane
            hots.append(jnp.where(hot, 1.0, 0.0).astype(BF16))
            x = x_ref[inside(b), :]
            gain = matmul(x, gain_both[...]) + matmul(x[:, :128], gain_rest[...])
            weight = jnp.where(
                jnp.bitwise_and(column(cell), 127) == lane, column(mass[number, :]), 0.0
            )
            gain = gain * jnp.concatenate([weight, weight], axis=1)
            high, low = split(gain)
            values.append(jnp.concatenate([high, low], axis=1))
        sums = matmul(jnp.concatenate(hots, axis=1), jnp.concatenate(values, axis=0))
        deposit[0] += sums[:, :128] + sums[:, 256:384]
        deposit[1] += sums[:, 128:256] + sums[:, 384:]
        return carry

    lax.fori_loop(0, (count[0, 0] + CHUNK - 1) // CHUNK, chunk, 0)


VMEM = pl.BlockSpec(memory_space=pltpu.VMEM)
SMEM = pl.BlockSpec(memory_space=pltpu.SMEM)
HBM = pl.BlockSpec(memory_space=pltpu.HBM)


def call(kernel, name, outs, args, scratch=(), flops=0, first=(), out=VMEM):
    args = [
        pltpu.with_memory_space_constraint(a, pltpu.HBM) if s is HBM else a
        for a, s in zip(args, list(first) + [None] * len(args))
    ]
    moved = sum(a.size * 4 for a in args) + sum(4 * math.prod(o) for o in outs)
    return pl.pallas_call(
        kernel,
        name=name,
        out_shape=[jax.ShapeDtypeStruct(o, F32) for o in outs],
        in_specs=list(first) + [VMEM] * (len(args) - len(first)),
        out_specs=[out] * len(outs),
        scratch_shapes=list(scratch),
        compiler_params=pltpu.CompilerParams(vmem_limit_bytes=24 * 2**20),
        cost_estimate=pl.CostEstimate(flops=flops, bytes_accessed=moved, transcendentals=0),
    )(*args)


def swap_halves(packed):
    halves = lax.axis_size("grp")
    return lax.ppermute(packed, "grp", [(i, (i + 1) % halves) for i in range(halves)])


def send(message, step):
    count = lax.axis_size("brick")
    return lax.ppermute(message, "brick", [(i, (i + step) % count) for i in range(count)])


def on_device(
    density,
    energy_field,
    lepton_field,
    velocity,
    abundance,
    tracer_mass,
    tracer_cell,
    tracer_count,
    weak_rates,
    capture_rates,
    binding,
    charge_ratio,
):
    fields = (density, energy_field, lepton_field)
    whole, tile = (3, 4, 64, 128), (64, 128)
    pads = pltpu.VMEM((12, 80, 128), F32)
    planes = pltpu.VMEM((4, 64, 128), F32)
    state, speeds, slopes, low_first, folded, packed = call(
        edges_kernel, "edges", [whole] * 3 + [(544, 128), (32, 128), tile], (*fields, velocity),
        [pltpu.SemaphoreType.DMA((4,))], 0, [HBM] * 4,
    )
    low_first = send(low_first, 1)
    partial, low_second, high_first, high_second, copied = call(
        messages_kernel, "messages", [whole, (384, 128), (416, 128), (512, 128), (528, 128)],
        (state, speeds, slopes, folded, packed), [pads],
    )
    low_second = send(low_second, 1)
    high_first = send(high_first, -1)
    high_second = send(high_second, -1)
    from_other = swap_halves(copied)

    rows = pltpu.VMEM((CHUNK, 128), F32)
    matrices = [pltpu.VMEM((256, 256), BF16), pltpu.VMEM((128, 256), BF16)]
    finished, deposit = call(
        network_kernel, "network", [(1024, 128), (2, 256, 128)],
        (
            tracer_count, state, tracer_cell.reshape(8, 128), abundance.reshape(1024, 128),
            weak_rates, capture_rates, tracer_mass.reshape(8, 128),
            binding.reshape(1, 128), charge_ratio.reshape(1, 128),
        ),
        [pltpu.VMEM((256, 512), BF16), *matrices, pltpu.VMEM((CHUNK, 256), BF16)]
        + [rows] * 6 + matrices,
        6 * 2 * 1024 * 128 * 256 * 18, [SMEM],
    )
    mid, sent = call(
        midpoint_kernel, "midpoint", [whole, (128, 128)],
        (state, speeds, partial, low_first, high_first, packed, from_other, deposit), [planes],
    )
    from_other = swap_halves(sent)
    (advanced,) = call(
        advance_kernel, "advance", [whole], (state, speeds, mid, deposit), [pads]
    )
    outs = call(
        finish_kernel, "finish", [(4, 64, 128)] * 3,
        (state, speeds, advanced, low_first, low_second, high_second, sent, from_other),
        [pltpu.VMEM(whole, F32), pltpu.SemaphoreType.DMA((3,))], 0, (), pl.BlockSpec(memory_space=pl.ANY),
    )
    return (*outs, finished[None, None])


def solution(mesh):
    return jax.shard_map(
        on_device,
        mesh=mesh,
        in_specs=(
            P("brick", None, "grp"),
            P("brick", None, "grp"),
            P("brick", None, "grp"),
            P(None, "brick", None, "grp"),
            P("grp", "brick", None, None),
            P("grp", "brick", None),
            P("grp", "brick", None),
            P("grp", "brick"),
            P(),
            P(),
            P(),
            P(),
        ),
        out_specs=(
            P("brick", None, "grp"),
            P("brick", None, "grp"),
            P("brick", None, "grp"),
            P("grp", "brick", None, None),
        ),
        check_vma=False,
    )
```

```python
import math

import jax
import jax.numpy as jnp
from jax import lax
from jax.experimental import pallas as pl
from jax.experimental.pallas import tpu as pltpu
from jax.sharding import PartitionSpec as P

SWEEPS = 8
CHUNK = 512
BLOCK = 128
COURANT = 0.8
HALF = 0.5 * COURANT / 12.0
FULL = COURANT / 12.0
F32 = jnp.float32
BF16 = jnp.bfloat16


def split(values):
    high = values.astype(BF16)
    return high, (values - high.astype(F32)).astype(BF16)


def matmul(a, b):
    return lax.dot_general(a, b, (((1,), (0,)), ((), ())), preferred_element_type=F32)


def lanes(rows=64):
    return lax.broadcasted_iota(jnp.int32, (rows, 128), 1)


def groups():
    return lax.shift_right_logical(lanes(), 2)


def spreading():
    row = lax.broadcasted_iota(jnp.int32, (128, 128), 0)
    source = jnp.bitwise_and(126 + jnp.bitwise_and(lanes(128), 3), 127)
    return jnp.where(row == source, 1.0, 0.0)


def circulant():
    row = lax.broadcasted_iota(jnp.int32, (128, 128), 0)
    offset = jnp.bitwise_and(row - lanes(128), 127)
    near = jnp.where(offset == 1, 8.0, jnp.where(offset == 127, -8.0, 0.0))
    return jnp.where(offset == 2, -1.0, jnp.where(offset == 126, 1.0, near))


def twice(matrix):
    matrix = matrix.astype(BF16)
    return jnp.concatenate([matrix, matrix], axis=0)


def parts(values):
    high, low = split(values)
    return jnp.concatenate([high, low], axis=1)


def unpack_z(packed, first, lane):
    moved = pltpu.roll(packed, (126 - first) % 128, 1)
    return jnp.where(jnp.logical_or(lane < 2, lane >= 126), moved, 0.0)


def edge_correction(other, own, lane):
    lack = other - own
    place = jnp.bitwise_and(lane, 3)
    far = jnp.where(place < 2, -pltpu.roll(lack, 126, 1), pltpu.roll(lack, 2, 1))
    near = jnp.where(place == 1, pltpu.roll(lack, 127, 1), 0.0)
    near = near - jnp.where(place == 2, pltpu.roll(lack, 1, 1), 0.0)
    return far + 8.0 * near


def along_y(tile, pad):
    pad[pl.ds(8, 64), :] = tile
    pad[pl.ds(0, 8), :] = tile[56:]
    pad[pl.ds(72, 8), :] = tile[:8]
    return 8.0 * (pad[pl.ds(9, 64), :] - pad[pl.ds(7, 64), :]) - (
        pad[pl.ds(10, 64), :] - pad[pl.ds(6, 64), :]
    )


def z_products(get, velocity, f, weights):
    speed_z = [parts(velocity[2, i] * get(i)) for i in range(4)]
    return matmul(jnp.concatenate(speed_z, axis=0), weights)


def xy_differences(get, velocity, pads, f):
    for i in range(4):
        plane = [velocity[0, j] * get(j) for j in range(4) if 0 < abs(j - i) < 3]
        if i == 0:
            total = 8.0 * plane[0] - plane[1]
        elif i == 1:
            total = 8.0 * (plane[1] - plane[0]) - plane[2]
        elif i == 2:
            total = 8.0 * (plane[2] - plane[1]) + plane[0]
        else:
            total = plane[0] - 8.0 * plane[1]
        yield i, total + along_y(velocity[1, i] * get(i), pads.at[4 * f + i])


SIDES = ((0, 1, -1.0), (3, 2, 1.0))


def rows_of_tile(number):
    return pl.ds(64 * number, 64)


def fold(folded, edge, place, group):
    folded = jnp.where(group == place, edge[:32], folded)
    return jnp.where(group == place + 16, edge[32:], folded)


def write_late(state, velocity, partial, planes, late):
    for k, plane in enumerate(planes):
        for f in range(3):
            late[rows_of_tile(2 * f + k), :] = velocity[0, plane] * (
                state[f, plane] - HALF * partial[f, plane]
            )


def edges_kernel(
    density, energy, lepton, speeds, cells_in, mass_in, binding_in, charge_in,
    state, velocity, slopes, low_first, folded, packed, cells, mass, binding, charge,
    sems,
):
    wait_speeds = pltpu.make_async_copy(speeds, velocity, sems.at[3])
    wait_speeds.start()
    copies = [
        pltpu.make_async_copy(ref, state.at[f], sems.at[f])
        for f, ref in enumerate((density, energy, lepton))
    ]
    small = [
        pltpu.make_async_copy(source, target, sems.at[4 + n])
        for n, (source, target) in enumerate(
            (
                (cells_in, cells), (mass_in, mass), (binding_in, binding), (charge_in, charge),
            )
        )
    ]
    for copy in copies + small:
        copy.start()
    weights = twice(jnp.concatenate([circulant(), spreading()], axis=1))
    group = groups()
    pack = jnp.zeros((64, 128), F32)
    up = down = jnp.zeros((32, 128), F32)
    wait_speeds.wait()
    for f in range(3):
        copies[f].wait()
        product = z_products(lambda i: state[f, i], velocity, f, weights)
        for i in range(4):
            slopes[f, i] = product[64 * i : 64 * i + 64, :128]
            edge = product[64 * i : 64 * i + 64, 128:]
            pack = jnp.where(group == 4 * f + i, edge, pack)
            if i < 2:
                down = fold(down, edge, 4 * f + 3 - i, group[:32])
            else:
                up = fold(up, edge, 4 * f + 3 - i, group[:32])
                low_first[rows_of_tile(2 * f + 3 - i), :] = velocity[0, i] * state[f, i]
    packed[...] = pack
    folded[...] = down
    low_first[pl.ds(384, 32), :] = up
    for k in range(2):
        low_first[pl.ds(416 + 64 * k, 64), :] = velocity[0, 3 - k]
    for copy in small:
        copy.wait()


def messages_kernel(
    state, velocity, slopes, folded, packed,
    partial, low_second, high_first, high_second, copied,
    pads,
):
    for f in range(3):
        for i, total in xy_differences(lambda i: state[f, i], velocity, pads, f):
            partial[f, i] = total + slopes[f, i]
            if i < 2:
                high_first[rows_of_tile(2 * f + i), :] = velocity[0, i] * state[f, i]
    write_late(state, velocity, partial, (3, 2), low_second)
    write_late(state, velocity, partial, (0, 1), high_second)
    high_first[pl.ds(384, 32), :] = folded[...]
    for k in range(2):
        high_second[rows_of_tile(6 + k), :] = velocity[0, k]
    copied[pl.ds(0, 64), :] = packed[...]
    copied[pl.ds(64, 464), :] = jnp.zeros((464, 128), F32)


def midpoint_kernel(
    state, velocity, partial, low, high, packed, from_other, deposit, mid, exchanged, total
):
    lane = lanes()
    correction = edge_correction(from_other[pl.ds(0, 64), :], packed[...], lane)
    group = groups()
    weights = twice(spreading())
    pack = jnp.zeros((64, 128), F32)
    for f in range(3):
        for i in range(4):
            total[i] = partial[f, i] + unpack_z(correction, 4 * (4 * f + i), lane)
        for (near, far, sign), side in zip(SIDES, (low, high)):
            close = side[rows_of_tile(2 * f), :]
            total[near] += sign * (8.0 * close - side[rows_of_tile(2 * f + 1), :])
            total[far] += -sign * close
        speed_z = []
        for i in range(4):
            value = state[f, i] - HALF * total[i]
            mid[f, i] = value
            speed_z.append(parts(velocity[2, i] * value))
        edge = matmul(jnp.concatenate(speed_z, axis=0), weights)
        for i in range(4):
            pack = jnp.where(group == 4 * f + i, edge[64 * i : 64 * i + 64], pack)
    exchanged[pl.ds(0, 64), :] = pack
    edge = pl.ds(384, 32)
    upper = jnp.bitwise_and(group[:32], 3) >= 2
    folded = jnp.where(upper, high[edge, :], low[edge, :])
    exchanged[pl.ds(64, 32), :] = folded
    exchanged[pl.ds(96, 32), :] = pltpu.roll(folded, 64, 1)


def advance_kernel(state, velocity, mid, deposit, advanced, pads):
    weights = twice(circulant())
    for f in range(3):
        slopes = z_products(lambda i: mid[f, i], velocity, f, weights)
        for i, total in xy_differences(lambda i: mid[f, i], velocity, pads, f):
            value = state[f, i] - FULL * (total + slopes[64 * i : 64 * i + 64])
            if f > 0:
                value = value + deposit[f - 1, pl.ds(64 * i, 64), :]
            advanced[f, i] = value


def finish_kernel(
    state, velocity, advanced, low_first, low, high, sent, from_other,
    density_out, energy_out, lepton_out, result, sems,
):
    lane = lanes()
    plane = jnp.bitwise_and(groups(), 3)
    weights = twice(spreading())
    edge_speed = jnp.zeros((64, 128), F32)
    speeds = (
        [low_first[pl.ds(416 + 64 * k, 64), :] for k in range(2)],
        [high[rows_of_tile(6 + k), :] for k in range(2)],
    )
    for (near, far, _), pair in zip(SIDES, speeds):
        for number, values in zip((near, far), pair):
            edge = matmul(parts(values), weights)
            edge_speed = jnp.where(plane == number, edge, edge_speed)
    own, side = pl.ds(0, 64), pl.ds(64, 64)
    correction = edge_correction(from_other[own, :], sent[own, :], lane)
    moved = edge_correction(from_other[side, :], sent[side, :], lane)
    moved = HALF * (edge_speed * moved)
    before, after = pltpu.roll(moved, 4, 1), pltpu.roll(moved, 124, 1)
    below = jnp.where(plane == 0, 8.0 * moved - after, -before)
    above = jnp.where(plane == 2, after, before - 8.0 * moved)
    correction = FULL * (correction + jnp.where(plane < 2, below, above))
    copies = []
    for f, out in enumerate((density_out, energy_out, lepton_out)):
        for (near, far, sign), side, (speed, speed_far) in zip(SIDES, (low, high), speeds):
            here = velocity[0, near] * state[f, near]
            behind = velocity[0, far] * state[f, far]
            step = sign * HALF
            close, remote = (side[rows_of_tile(2 * f + k), :] for k in range(2))
            close = close + step * (speed * (8.0 * here - behind))
            remote = remote - step * (speed_far * here)
            for i, part in ((near, remote - 8.0 * close), (far, close)):
                packed = unpack_z(correction, 4 * (4 * f + i), lane)
                result[f, i] = advanced[f, i] + (FULL * sign) * part - packed
        copies.append(pltpu.make_async_copy(result.at[f], out, sems.at[f]))
        copies[f].start()
    for copy in copies:
        copy.wait()


def column(row):
    return jnp.transpose(jnp.broadcast_to(row, (128, 128)))


def load_matrices(weak, capture, both, rest):
    matrix = jnp.concatenate([weak[...], capture[...]], axis=1)
    high, low = split(matrix)
    both[...] = jnp.concatenate([high, high], axis=0)
    rest[...] = low


def newton(base, start, get_target, rows_of, both, rest, w_ref, c_ref, x_ref, t_ref, k_ref, a_ref, finish):
    blocks = CHUNK // BLOCK

    def products(b):
        x = x_ref[pl.ds(b * BLOCK, BLOCK), :]
        return matmul(x, both[...]) + matmul(x[:, :128], rest[...])

    def put(b, values):
        high, low = split(values)
        x_ref[pl.ds(b * BLOCK, BLOCK), :] = jnp.concatenate([high, low], axis=1)

    for b in range(blocks):
        put(b, rows_of(b))
    for b in range(blocks):
        at = pl.ds(b * BLOCK, BLOCK)
        here = pl.ds(base + b * BLOCK, BLOCK)
        product = products(b)
        rows = rows_of(b)
        rate_weak, rate_capture = w_ref[here, :], c_ref[here, :]
        alpha = rate_capture * rows[:, 0:1]
        target = rate_weak * product[:, :128] + alpha * product[:, 128:]
        target = get_target(b, rows, target)
        a_ref[at, :] = alpha
        k_ref[at, :] = rate_capture * product[:, 128:]
        t_ref[at, :] = target
        put(b, target)
        start(b, target)
    for sweep in range(SWEEPS):
        for b in range(blocks):
            at = pl.ds(b * BLOCK, BLOCK)
            here = pl.ds(base + b * BLOCK, BLOCK)
            product = products(b)
            before = finish.last[b]
            update = t_ref[at, :] + (
                w_ref[here, :] * product[:, :128]
                + a_ref[at, :] * product[:, 128:]
                + before * k_ref[at, :]
            )
            if sweep < SWEEPS - 1:
                put(b, update)
                start(b, update)
            else:
                finish(b, rows_of(b) + update)


class Finish:
    def __init__(self, write):
        self.last = {}
        self.write = write

    def keep(self, b, values):
        self.last[b] = values[:, 0:1]

    def __call__(self, b, values):
        self.write(b, values)


def network_kernel(
    count, state, cells, rows, weak, capture, mass, binding, charge,
    rows_out, deposit,
    table, both, rest, x_ref, t_ref, k_ref, a_ref, w_ref, c_ref, iterate, gain_both, gain_rest,
):
    occupied_slots = count[0, 0]
    load_matrices(weak, capture, both, rest)
    rho, eps, lam = (state[f].reshape(256, 128) for f in range(3))
    inverse = 1.0 / rho
    weak_high, weak_low = split(0.62 + 0.04 * rho + 0.05 * (lam * inverse))
    capture_high, capture_low = split(0.3 * jax.nn.sigmoid(eps * inverse))
    table[...] = jnp.concatenate([weak_high, weak_low, capture_high, capture_low], axis=1)
    gains = jnp.concatenate([column(binding[...]), column(charge[...])], axis=1)
    high, low = split(gains)
    gain_both[...] = jnp.concatenate([high, high], axis=0)
    gain_rest[...] = low
    rows_out[...] = jnp.zeros(rows_out.shape, F32)
    deposit[...] = jnp.zeros(deposit.shape, F32)
    lane = lanes(BLOCK)
    sublane = lax.broadcasted_iota(jnp.int32, (256, 128), 0)
    ones = jnp.ones((256, 128), BF16)

    def chunk(k, carry):
        base = k * CHUNK

        def place(b):
            return pl.ds(pl.multiple_of(base + b * BLOCK, BLOCK), BLOCK)

        def inside(b):
            return pl.ds(b * BLOCK, BLOCK)

        for b in range(CHUNK // BLOCK):
            cell = column(cells[pl.ds(k * (CHUNK // BLOCK) + b, 1), :])
            row_id = lax.shift_right_logical(cell, 7)
            hot = jnp.concatenate([row_id == lane, row_id == lane + 128], axis=1)
            picked = matmul(jnp.where(hot, 1.0, 0.0).astype(BF16), table[...])
            here = jnp.bitwise_and(cell, 127) == lane
            here = jnp.concatenate([here, here, here, here], axis=1)
            picked = jnp.where(here, picked, 0.0).astype(BF16)
            w_ref[inside(b), :] = matmul(picked[:, :256], ones)
            c_ref[inside(b), :] = matmul(picked[:, 256:], ones)

        def write_first(b, values):
            iterate[inside(b), :] = values

        def write_last(b, values):
            slot = base + b * BLOCK + lax.broadcasted_iota(jnp.int32, (BLOCK, 128), 0)
            occupied = slot < occupied_slots
            rows_out[place(b), :] = jnp.where(occupied, values, 0.0)
            change = jnp.where(occupied, values - rows[place(b), :], 0.0)
            high, low = split(change)
            x_ref[inside(b), :] = jnp.concatenate([high, low], axis=1)

        finish = Finish(write_first)
        newton(
            0, finish.keep, lambda b, current, target: target, lambda b: rows[place(b), :],
            both, rest, w_ref, c_ref, x_ref, t_ref, k_ref, a_ref, finish,
        )
        finish = Finish(write_last)
        newton(
            0, finish.keep, lambda b, current, target: target - (current - rows[place(b), :]),
            lambda b: iterate[inside(b), :],
            both, rest, w_ref, c_ref, x_ref, t_ref, k_ref, a_ref, finish,
        )
        hots, values = [], []
        for b in range(CHUNK // BLOCK):
            number = pl.ds(k * (CHUNK // BLOCK) + b, 1)
            cell = cells[number, :]
            hot = lax.shift_right_logical(cell, 7) == sublane
            hots.append(jnp.where(hot, 1.0, 0.0).astype(BF16))
            x = x_ref[inside(b), :]
            gain = matmul(x, gain_both[...]) + matmul(x[:, :128], gain_rest[...])
            weight = jnp.where(
                jnp.bitwise_and(column(cell), 127) == lane, column(mass[number, :]), 0.0
            )
            gain = gain * jnp.concatenate([weight, weight], axis=1)
            high, low = split(gain)
            values.append(jnp.concatenate([high, low], axis=1))
        sums = matmul(jnp.concatenate(hots, axis=1), jnp.concatenate(values, axis=0))
        deposit[0] += sums[:, :128] + sums[:, 256:384]
        deposit[1] += sums[:, 128:256] + sums[:, 384:]
        return carry

    lax.fori_loop(0, (occupied_slots + CHUNK - 1) // CHUNK, chunk, 0)


VMEM = pl.BlockSpec(memory_space=pltpu.VMEM)
HBM = pl.BlockSpec(memory_space=pltpu.HBM)
SMEM = pl.BlockSpec(memory_space=pltpu.SMEM)


def call(kernel, name, outs, args, scratch=(), flops=0, first=(), out=VMEM, integers=()):
    args = [
        pltpu.with_memory_space_constraint(a, pltpu.HBM) if s is HBM else a
        for a, s in zip(args, list(first) + [None] * len(args))
    ]
    moved = sum(a.size * 4 for a in args) + sum(4 * math.prod(o) for o in outs)
    return pl.pallas_call(
        kernel,
        name=name,
        out_shape=[
            jax.ShapeDtypeStruct(o, jnp.int32 if n in integers else F32) for n, o in enumerate(outs)
        ],
        in_specs=list(first) + [VMEM] * (len(args) - len(first)),
        out_specs=[out] * len(outs),
        scratch_shapes=list(scratch),
        compiler_params=pltpu.CompilerParams(vmem_limit_bytes=24 * 2**20),
        cost_estimate=pl.CostEstimate(flops=flops, bytes_accessed=moved, transcendentals=0),
    )(*args)


def swap_halves(packed):
    halves = lax.axis_size("grp")
    return lax.ppermute(packed, "grp", [(i, (i + 1) % halves) for i in range(halves)])


def send(message, step):
    count = lax.axis_size("brick")
    return lax.ppermute(message, "brick", [(i, (i + step) % count) for i in range(count)])


def on_device(
    density,
    energy_field,
    lepton_field,
    velocity,
    abundance,
    tracer_mass,
    tracer_cell,
    tracer_count,
    weak_rates,
    capture_rates,
    binding,
    charge_ratio,
):
    fields = (density, energy_field, lepton_field)
    whole, tile = (3, 4, 64, 128), (64, 128)
    pads = pltpu.VMEM((12, 80, 128), F32)
    planes = pltpu.VMEM((4, 64, 128), F32)
    small, row = (8, 128), (1, 128)
    state, speeds, slopes, low_first, folded, packed, cells, mass, *tables = call(
        edges_kernel, "edges",
        [whole] * 3 + [(544, 128), (32, 128), tile, small, small, row, row],
        (
            *fields, velocity, tracer_cell.reshape(small), tracer_mass.reshape(small),
            binding.reshape(row), charge_ratio.reshape(row),
        ),
        [pltpu.SemaphoreType.DMA((8,))], 0, [HBM] * 8, VMEM, (6,),
    )
    low_first = send(low_first, 1)
    partial, low_second, high_first, high_second, copied = call(
        messages_kernel, "messages", [whole, (384, 128), (416, 128), (512, 128), (528, 128)],
        (state, speeds, slopes, folded, packed), [pads],
    )
    low_second = send(low_second, 1)
    high_first = send(high_first, -1)
    high_second = send(high_second, -1)
    from_other = swap_halves(copied)

    rows = pltpu.VMEM((CHUNK, 128), F32)
    matrices = [pltpu.VMEM((256, 256), BF16), pltpu.VMEM((128, 256), BF16)]
    finished, deposit = call(
        network_kernel, "network", [(1024, 128), (2, 256, 128)],
        (
            tracer_count, state, cells, abundance.reshape(1024, 128),
            weak_rates, capture_rates, mass, *tables,
        ),
        [pltpu.VMEM((256, 512), BF16), *matrices, pltpu.VMEM((CHUNK, 256), BF16)]
        + [rows] * 6 + matrices,
        6 * 2 * 1024 * 128 * 256 * 18, [SMEM],
    )
    mid, sent = call(
        midpoint_kernel, "midpoint", [whole, (128, 128)],
        (state, speeds, partial, low_first, high_first, packed, from_other, deposit), [planes],
    )
    from_other = swap_halves(sent)
    (advanced,) = call(
        advance_kernel, "advance", [whole], (state, speeds, mid, deposit), [pads]
    )
    outs = call(
        finish_kernel, "finish", [(4, 64, 128)] * 3,
        (state, speeds, advanced, low_first, low_second, high_second, sent, from_other),
        [pltpu.VMEM(whole, F32), pltpu.SemaphoreType.DMA((3,))], 0, (), pl.BlockSpec(memory_space=pl.ANY),
    )
    return (*outs, finished[None, None])


def solution(mesh):
    return jax.shard_map(
        on_device,
        mesh=mesh,
        in_specs=(
            P("brick", None, "grp"),
            P("brick", None, "grp"),
            P("brick", None, "grp"),
            P(None, "brick", None, "grp"),
            P("grp", "brick", None, None),
            P("grp", "brick", None),
            P("grp", "brick", None),
            P("grp", "brick"),
            P(),
            P(),
            P(),
            P(),
        ),
        out_specs=(
            P("brick", None, "grp"),
            P("brick", None, "grp"),
            P("brick", None, "grp"),
            P("grp", "brick", None, None),
        ),
        check_vma=False,
    )
```

```python
import math

import jax
import jax.numpy as jnp
from jax import lax
from jax.experimental import pallas as pl
from jax.experimental.pallas import tpu as pltpu
from jax.sharding import PartitionSpec as P

SWEEPS = 8
CHUNK = 512
BLOCK = 128
COURANT = 0.8
HALF = 0.5 * COURANT / 12.0
FULL = COURANT / 12.0
F32 = jnp.float32
BF16 = jnp.bfloat16


def split(values):
    high = values.astype(BF16)
    return high, (values - high.astype(F32)).astype(BF16)


def matmul(a, b):
    return lax.dot_general(a, b, (((1,), (0,)), ((), ())), preferred_element_type=F32)


def lanes(rows=64):
    return lax.broadcasted_iota(jnp.int32, (rows, 128), 1)


def groups():
    return lax.shift_right_logical(lanes(), 2)


def spreading():
    row = lax.broadcasted_iota(jnp.int32, (128, 128), 0)
    source = jnp.bitwise_and(126 + jnp.bitwise_and(lanes(128), 3), 127)
    return jnp.where(row == source, 1.0, 0.0)


def circulant():
    row = lax.broadcasted_iota(jnp.int32, (128, 128), 0)
    offset = jnp.bitwise_and(row - lanes(128), 127)
    near = jnp.where(offset == 1, 8.0, jnp.where(offset == 127, -8.0, 0.0))
    return jnp.where(offset == 2, -1.0, jnp.where(offset == 126, 1.0, near))


def twice(matrix):
    matrix = matrix.astype(BF16)
    return jnp.concatenate([matrix, matrix], axis=0)


def parts(values):
    high, low = split(values)
    return jnp.concatenate([high, low], axis=1)


def unpack_z(packed, first, lane):
    moved = pltpu.roll(packed, (126 - first) % 128, 1)
    return jnp.where(jnp.logical_or(lane < 2, lane >= 126), moved, 0.0)


def edge_correction(other, own, lane):
    lack = other - own
    place = jnp.bitwise_and(lane, 3)
    far = jnp.where(place < 2, -pltpu.roll(lack, 126, 1), pltpu.roll(lack, 2, 1))
    near = jnp.where(place == 1, pltpu.roll(lack, 127, 1), 0.0)
    near = near - jnp.where(place == 2, pltpu.roll(lack, 1, 1), 0.0)
    return far + 8.0 * near


def along_y(tile, pad):
    pad[pl.ds(8, 64), :] = tile
    pad[pl.ds(0, 8), :] = tile[56:]
    pad[pl.ds(72, 8), :] = tile[:8]
    return 8.0 * (pad[pl.ds(9, 64), :] - pad[pl.ds(7, 64), :]) - (
        pad[pl.ds(10, 64), :] - pad[pl.ds(6, 64), :]
    )


def z_products(get, velocity, f, weights):
    speed_z = [parts(velocity[2, i] * get(i)) for i in range(4)]
    return matmul(jnp.concatenate(speed_z, axis=0), weights)


def xy_differences(get, velocity, pads, f):
    for i in range(4):
        plane = [velocity[0, j] * get(j) for j in range(4) if 0 < abs(j - i) < 3]
        if i == 0:
            total = 8.0 * plane[0] - plane[1]
        elif i == 1:
            total = 8.0 * (plane[1] - plane[0]) - plane[2]
        elif i == 2:
            total = 8.0 * (plane[2] - plane[1]) + plane[0]
        else:
            total = plane[0] - 8.0 * plane[1]
        yield i, total + along_y(velocity[1, i] * get(i), pads.at[4 * f + i])


SIDES = ((0, 1, -1.0), (3, 2, 1.0))


def rows_of_tile(number):
    return pl.ds(64 * number, 64)


def fold(folded, edge, place, group):
    folded = jnp.where(group == place, edge[:32], folded)
    return jnp.where(group == place + 16, edge[32:], folded)


def write_late(state, velocity, partial, planes, late):
    for k, plane in enumerate(planes):
        for f in range(3):
            late[rows_of_tile(2 * f + k), :] = velocity[0, plane] * (
                state[f, plane] - HALF * partial[f, plane]
            )


def edges_kernel(
    density, energy, lepton, speeds, cells_in, mass_in, binding_in, charge_in,
    state, velocity, slopes, low_first, folded, packed, cells, mass, binding, charge,
    sems,
):
    wait_speeds = pltpu.make_async_copy(speeds, velocity, sems.at[3])
    wait_speeds.start()
    copies = [
        pltpu.make_async_copy(ref, state.at[f], sems.at[f])
        for f, ref in enumerate((density, energy, lepton))
    ]
    small = [
        pltpu.make_async_copy(source, target, sems.at[4 + n])
        for n, (source, target) in enumerate(
            (
                (cells_in, cells), (mass_in, mass), (binding_in, binding), (charge_in, charge),
            )
        )
    ]
    for copy in copies + small:
        copy.start()
    weights = twice(jnp.concatenate([circulant(), spreading()], axis=1))
    group = groups()
    pack = jnp.zeros((64, 128), F32)
    up = down = jnp.zeros((32, 128), F32)
    wait_speeds.wait()
    for f in range(3):
        copies[f].wait()
        product = z_products(lambda i: state[f, i], velocity, f, weights)
        for i in range(4):
            slopes[f, i] = product[64 * i : 64 * i + 64, :128]
            edge = product[64 * i : 64 * i + 64, 128:]
            pack = jnp.where(group == 4 * f + i, edge, pack)
            if i < 2:
                down = fold(down, edge, 4 * f + 3 - i, group[:32])
            else:
                up = fold(up, edge, 4 * f + 3 - i, group[:32])
                low_first[rows_of_tile(2 * f + 3 - i), :] = velocity[0, i] * state[f, i]
    packed[...] = pack
    folded[...] = down
    low_first[pl.ds(384, 32), :] = up
    for k in range(2):
        low_first[pl.ds(416 + 64 * k, 64), :] = velocity[0, 3 - k]
    for copy in small:
        copy.wait()


def messages_kernel(
    state, velocity, slopes, folded, packed,
    partial, low_second, high_first, high_second, copied,
    pads,
):
    for f in range(3):
        for i, total in xy_differences(lambda i: state[f, i], velocity, pads, f):
            partial[f, i] = total + slopes[f, i]
            if i < 2:
                high_first[rows_of_tile(2 * f + i), :] = velocity[0, i] * state[f, i]
    write_late(state, velocity, partial, (3, 2), low_second)
    write_late(state, velocity, partial, (0, 1), high_second)
    high_first[pl.ds(384, 32), :] = folded[...]
    for k in range(2):
        high_second[rows_of_tile(6 + k), :] = velocity[0, k]
    copied[...] = packed[...]


def midpoint_kernel(
    state, velocity, partial, low, high, packed, from_other, deposit, mid, exchanged, total
):
    lane = lanes()
    correction = edge_correction(from_other[...], packed[...], lane)
    group = groups()
    weights = twice(spreading())
    pack = jnp.zeros((64, 128), F32)
    for f in range(3):
        for i in range(4):
            total[i] = partial[f, i] + unpack_z(correction, 4 * (4 * f + i), lane)
        for (near, far, sign), side in zip(SIDES, (low, high)):
            close = side[rows_of_tile(2 * f), :]
            total[near] += sign * (8.0 * close - side[rows_of_tile(2 * f + 1), :])
            total[far] += -sign * close
        speed_z = []
        for i in range(4):
            value = state[f, i] - HALF * total[i]
            mid[f, i] = value
            speed_z.append(parts(velocity[2, i] * value))
        edge = matmul(jnp.concatenate(speed_z, axis=0), weights)
        for i in range(4):
            pack = jnp.where(group == 4 * f + i, edge[64 * i : 64 * i + 64], pack)
    exchanged[pl.ds(0, 64), :] = pack
    edge = pl.ds(384, 32)
    upper = jnp.bitwise_and(group[:32], 3) >= 2
    folded = jnp.where(upper, high[edge, :], low[edge, :])
    exchanged[pl.ds(64, 32), :] = folded
    exchanged[pl.ds(96, 32), :] = pltpu.roll(folded, 64, 1)


def advance_kernel(state, velocity, mid, deposit, advanced, pads):
    weights = twice(circulant())
    for f in range(3):
        slopes = z_products(lambda i: mid[f, i], velocity, f, weights)
        for i, total in xy_differences(lambda i: mid[f, i], velocity, pads, f):
            value = state[f, i] - FULL * (total + slopes[64 * i : 64 * i + 64])
            if f > 0:
                value = value + deposit[f - 1, pl.ds(64 * i, 64), :]
            advanced[f, i] = value


def finish_kernel(
    state, velocity, advanced, low_first, low, high, sent, from_other,
    density_out, energy_out, lepton_out, result, sems,
):
    lane = lanes()
    plane = jnp.bitwise_and(groups(), 3)
    weights = twice(spreading())
    edge_speed = jnp.zeros((64, 128), F32)
    speeds = (
        [low_first[pl.ds(416 + 64 * k, 64), :] for k in range(2)],
        [high[rows_of_tile(6 + k), :] for k in range(2)],
    )
    for (near, far, _), pair in zip(SIDES, speeds):
        for number, values in zip((near, far), pair):
            edge = matmul(parts(values), weights)
            edge_speed = jnp.where(plane == number, edge, edge_speed)
    own, side = pl.ds(0, 64), pl.ds(64, 64)
    correction = edge_correction(from_other[own, :], sent[own, :], lane)
    moved = edge_correction(from_other[side, :], sent[side, :], lane)
    moved = HALF * (edge_speed * moved)
    before, after = pltpu.roll(moved, 4, 1), pltpu.roll(moved, 124, 1)
    below = jnp.where(plane == 0, 8.0 * moved - after, -before)
    above = jnp.where(plane == 2, after, before - 8.0 * moved)
    correction = FULL * (correction + jnp.where(plane < 2, below, above))
    copies = []
    for f, out in enumerate((density_out, energy_out, lepton_out)):
        for (near, far, sign), side, (speed, speed_far) in zip(SIDES, (low, high), speeds):
            here = velocity[0, near] * state[f, near]
            behind = velocity[0, far] * state[f, far]
            step = sign * HALF
            close, remote = (side[rows_of_tile(2 * f + k), :] for k in range(2))
            close = close + step * (speed * (8.0 * here - behind))
            remote = remote - step * (speed_far * here)
            for i, part in ((near, remote - 8.0 * close), (far, close)):
                packed = unpack_z(correction, 4 * (4 * f + i), lane)
                result[f, i] = advanced[f, i] + (FULL * sign) * part - packed
        copies.append(pltpu.make_async_copy(result.at[f], out, sems.at[f]))
        copies[f].start()
    for copy in copies:
        copy.wait()


def column(row):
    return jnp.transpose(jnp.broadcast_to(row, (128, 128)))


def load_matrices(weak, capture, both, rest):
    matrix = jnp.concatenate([weak[...], capture[...]], axis=1)
    high, low = split(matrix)
    both[...] = jnp.concatenate([high, high], axis=0)
    rest[...] = low


def newton(base, start, get_target, rows_of, both, rest, w_ref, c_ref, x_ref, t_ref, k_ref, a_ref, finish):
    blocks = CHUNK // BLOCK

    def products(b):
        x = x_ref[pl.ds(b * BLOCK, BLOCK), :]
        return matmul(x, both[...]) + matmul(x[:, :128], rest[...])

    def put(b, values):
        high, low = split(values)
        x_ref[pl.ds(b * BLOCK, BLOCK), :] = jnp.concatenate([high, low], axis=1)

    for b in range(blocks):
        put(b, rows_of(b))
    for b in range(blocks):
        at = pl.ds(b * BLOCK, BLOCK)
        here = pl.ds(base + b * BLOCK, BLOCK)
        product = products(b)
        rows = rows_of(b)
        rate_weak, rate_capture = w_ref[here, :], c_ref[here, :]
        alpha = rate_capture * rows[:, 0:1]
        target = rate_weak * product[:, :128] + alpha * product[:, 128:]
        target = get_target(b, rows, target)
        a_ref[at, :] = alpha
        k_ref[at, :] = rate_capture * product[:, 128:]
        t_ref[at, :] = target
        put(b, target)
        start(b, target)
    ahead = {b: products(b) for b in range(2)}
    for sweep in range(SWEEPS):
        for b in range(blocks):
            at = pl.ds(b * BLOCK, BLOCK)
            here = pl.ds(base + b * BLOCK, BLOCK)
            product = ahead.pop(b)
            if b + 2 < blocks or sweep < SWEEPS - 1:
                ahead[(b + 2) % blocks] = products((b + 2) % blocks)
            before = finish.last[b]
            update = t_ref[at, :] + (
                w_ref[here, :] * product[:, :128]
                + a_ref[at, :] * product[:, 128:]
                + before * k_ref[at, :]
            )
            if sweep < SWEEPS - 1:
                put(b, update)
                start(b, update)
            else:
                finish(b, rows_of(b) + update)


class Finish:
    def __init__(self, write):
        self.last = {}
        self.write = write

    def keep(self, b, values):
        self.last[b] = values[:, 0:1]

    def __call__(self, b, values):
        self.write(b, values)


def network_kernel(
    count, state, cells, rows, weak, capture, mass, binding, charge,
    rows_out, deposit,
    table, both, rest, x_ref, t_ref, k_ref, a_ref, w_ref, c_ref, iterate, gain_both, gain_rest,
):
    occupied_slots = count[0, 0]
    load_matrices(weak, capture, both, rest)
    rho, eps, lam = (state[f].reshape(256, 128) for f in range(3))
    inverse = 1.0 / rho
    weak_high, weak_low = split(0.62 + 0.04 * rho + 0.05 * (lam * inverse))
    capture_high, capture_low = split(0.3 * jax.nn.sigmoid(eps * inverse))
    table[...] = jnp.concatenate([weak_high, weak_low, capture_high, capture_low], axis=1)
    gains = jnp.concatenate([column(binding[...]), column(charge[...])], axis=1)
    high, low = split(gains)
    gain_both[...] = jnp.concatenate([high, high], axis=0)
    gain_rest[...] = low
    rows_out[...] = jnp.zeros(rows_out.shape, F32)
    deposit[...] = jnp.zeros(deposit.shape, F32)
    lane = lanes(BLOCK)
    sublane = lax.broadcasted_iota(jnp.int32, (256, 128), 0)
    ones = jnp.ones((256, 128), BF16)

    def chunk(k, carry):
        base = k * CHUNK

        def place(b):
            return pl.ds(pl.multiple_of(base + b * BLOCK, BLOCK), BLOCK)

        def inside(b):
            return pl.ds(b * BLOCK, BLOCK)

        for b in range(CHUNK // BLOCK):
            cell = column(cells[pl.ds(k * (CHUNK // BLOCK) + b, 1), :])
            row_id = lax.shift_right_logical(cell, 7)
            hot = jnp.concatenate([row_id == lane, row_id == lane + 128], axis=1)
            picked = matmul(jnp.where(hot, 1.0, 0.0).astype(BF16), table[...])
            here = jnp.bitwise_and(cell, 127) == lane
            here = jnp.concatenate([here, here, here, here], axis=1)
            picked = jnp.where(here, picked, 0.0).astype(BF16)
            w_ref[inside(b), :] = matmul(picked[:, :256], ones)
            c_ref[inside(b), :] = matmul(picked[:, 256:], ones)

        def write_first(b, values):
            iterate[inside(b), :] = values

        def write_last(b, values):
            slot = base + b * BLOCK + lax.broadcasted_iota(jnp.int32, (BLOCK, 128), 0)
            occupied = slot < occupied_slots
            rows_out[place(b), :] = jnp.where(occupied, values, 0.0)
            change = jnp.where(occupied, values - rows[place(b), :], 0.0)
            high, low = split(change)
            x_ref[inside(b), :] = jnp.concatenate([high, low], axis=1)

        finish = Finish(write_first)
        newton(
            0, finish.keep, lambda b, current, target: target, lambda b: rows[place(b), :],
            both, rest, w_ref, c_ref, x_ref, t_ref, k_ref, a_ref, finish,
        )
        finish = Finish(write_last)
        newton(
            0, finish.keep, lambda b, current, target: target - (current - rows[place(b), :]),
            lambda b: iterate[inside(b), :],
            both, rest, w_ref, c_ref, x_ref, t_ref, k_ref, a_ref, finish,
        )
        hots, values = [], []
        for b in range(CHUNK // BLOCK):
            number = pl.ds(k * (CHUNK // BLOCK) + b, 1)
            cell = cells[number, :]
            hot = lax.shift_right_logical(cell, 7) == sublane
            hots.append(jnp.where(hot, 1.0, 0.0).astype(BF16))
            x = x_ref[inside(b), :]
            gain = matmul(x, gain_both[...]) + matmul(x[:, :128], gain_rest[...])
            weight = jnp.where(
                jnp.bitwise_and(column(cell), 127) == lane, column(mass[number, :]), 0.0
            )
            gain = gain * jnp.concatenate([weight, weight], axis=1)
            high, low = split(gain)
            values.append(jnp.concatenate([high, low], axis=1))
        sums = matmul(jnp.concatenate(hots, axis=1), jnp.concatenate(values, axis=0))
        deposit[0] += sums[:, :128] + sums[:, 256:384]
        deposit[1] += sums[:, 128:256] + sums[:, 384:]
        return carry

    lax.fori_loop(0, (occupied_slots + CHUNK - 1) // CHUNK, chunk, 0)


VMEM = pl.BlockSpec(memory_space=pltpu.VMEM)
HBM = pl.BlockSpec(memory_space=pltpu.HBM)
SMEM = pl.BlockSpec(memory_space=pltpu.SMEM)


def call(kernel, name, outs, args, scratch=(), flops=0, first=(), out=VMEM, integers=()):
    args = [
        pltpu.with_memory_space_constraint(a, pltpu.HBM) if s is HBM else a
        for a, s in zip(args, list(first) + [None] * len(args))
    ]
    moved = sum(a.size * 4 for a in args) + sum(4 * math.prod(o) for o in outs)
    return pl.pallas_call(
        kernel,
        name=name,
        out_shape=[
            jax.ShapeDtypeStruct(o, jnp.int32 if n in integers else F32) for n, o in enumerate(outs)
        ],
        in_specs=list(first) + [VMEM] * (len(args) - len(first)),
        out_specs=[out] * len(outs),
        scratch_shapes=list(scratch),
        compiler_params=pltpu.CompilerParams(vmem_limit_bytes=24 * 2**20),
        cost_estimate=pl.CostEstimate(flops=flops, bytes_accessed=moved, transcendentals=0),
    )(*args)


def swap_halves(packed):
    halves = lax.axis_size("grp")
    return lax.ppermute(packed, "grp", [(i, (i + 1) % halves) for i in range(halves)])


def send(message, step):
    count = lax.axis_size("brick")
    return lax.ppermute(message, "brick", [(i, (i + step) % count) for i in range(count)])


def on_device(
    density,
    energy_field,
    lepton_field,
    velocity,
    abundance,
    tracer_mass,
    tracer_cell,
    tracer_count,
    weak_rates,
    capture_rates,
    binding,
    charge_ratio,
):
    fields = (density, energy_field, lepton_field)
    whole, tile = (3, 4, 64, 128), (64, 128)
    pads = pltpu.VMEM((12, 80, 128), F32)
    planes = pltpu.VMEM((4, 64, 128), F32)
    small, row = (8, 128), (1, 128)
    state, speeds, slopes, low_first, folded, packed, cells, mass, *tables = call(
        edges_kernel, "edges",
        [whole] * 3 + [(544, 128), (32, 128), tile, small, small, row, row],
        (
            *fields, velocity, tracer_cell.reshape(small), tracer_mass.reshape(small),
            binding.reshape(row), charge_ratio.reshape(row),
        ),
        [pltpu.SemaphoreType.DMA((8,))], 0, [HBM] * 8, VMEM, (6,),
    )
    low_first = send(low_first, 1)
    partial, low_second, high_first, high_second, copied = call(
        messages_kernel, "messages", [whole, (384, 128), (416, 128), (512, 128), tile],
        (state, speeds, slopes, folded, packed), [pads],
    )
    low_second = send(low_second, 1)
    high_first = send(high_first, -1)
    high_second = send(high_second, -1)
    from_other = swap_halves(copied)

    rows = pltpu.VMEM((CHUNK, 128), F32)
    matrices = [pltpu.VMEM((256, 256), BF16), pltpu.VMEM((128, 256), BF16)]
    finished, deposit = call(
        network_kernel, "network", [(1024, 128), (2, 256, 128)],
        (
            tracer_count, state, cells, abundance.reshape(1024, 128),
            weak_rates, capture_rates, mass, *tables,
        ),
        [pltpu.VMEM((256, 512), BF16), *matrices, pltpu.VMEM((CHUNK, 256), BF16)]
        + [rows] * 6 + matrices,
        6 * 2 * 1024 * 128 * 256 * 18, [SMEM],
    )
    mid, sent = call(
        midpoint_kernel, "midpoint", [whole, (128, 128)],
        (state, speeds, partial, low_first, high_first, packed, from_other, deposit), [planes],
    )
    from_other = swap_halves(sent)
    (advanced,) = call(
        advance_kernel, "advance", [whole], (state, speeds, mid, deposit), [pads]
    )
    outs = call(
        finish_kernel, "finish", [(4, 64, 128)] * 3,
        (state, speeds, advanced, low_first, low_second, high_second, sent, from_other),
        [pltpu.VMEM(whole, F32), pltpu.SemaphoreType.DMA((3,))], 0, (), pl.BlockSpec(memory_space=pl.ANY),
    )
    return (*outs, finished[None, None])


def solution(mesh):
    return jax.shard_map(
        on_device,
        mesh=mesh,
        in_specs=(
            P("brick", None, "grp"),
            P("brick", None, "grp"),
            P("brick", None, "grp"),
            P(None, "brick", None, "grp"),
            P("grp", "brick", None, None),
            P("grp", "brick", None),
            P("grp", "brick", None),
            P("grp", "brick"),
            P(),
            P(),
            P(),
            P(),
        ),
        out_specs=(
            P("brick", None, "grp"),
            P("brick", None, "grp"),
            P("brick", None, "grp"),
            P("grp", "brick", None, None),
        ),
        check_vma=False,
    )
```
